32 devices in a mesh: ctx: 16 (over z, y, x), fsdp: 2 (over core).
Axes of the slice: x: 2, y: 2, z: 4, core: 2. Of those that a mesh axis runs over, the one named last changes fastest.
Arguments:
- out_grad: bfloat16 [4096, 16384], P('fsdp', 'ctx'), may hold values from -6 to 6
- gate_values: bfloat16 [4096, 16384], P('fsdp', 'ctx'), may hold values from -6 to 6
- kv_product: bfloat16 [4096, 16384], P('fsdp', 'ctx'), may hold values from -6 to 6
- w_out: bfloat16 [4096, 4096], P('ctx', 'fsdp'), may hold values from -0.09375 to 0.09375
- filters: bfloat16 [2, 16, 128, 128], P('fsdp', 'ctx'), may hold values from -0.5 to 0.5
Outputs:
- gate_grad: float32 [4096, 16384], P('fsdp', 'ctx')
- kv_grad: bfloat16 [4096, 16384], P('fsdp', 'ctx')
- filter_grad: float32 [2, 16, 128, 128], P('fsdp', 'ctx')
- w_grad: float32 [4096, 4096], P('ctx', 'fsdp')
The draws below stay inside these ranges and needn't reach their ends.
All inputs are finite; a program needn't handle non-finite values.
Results may differ from the reference program's by a relative error of at most 0.0049.
Values may be sent and summed in bfloat16 or wider, within the bound.
No kernel may reach another device: no remote copies, remote signals or barrier semaphores. Data moves between devices by JAX's collectives and lax.ppermute only.
A program may use at most 192 MiB of HBM per device.

```python
import math
import jax
import jax.numpy as jnp
from jax import lax

D = 4096
TAPS = 128
TOKENS = 16384
CPD = 128
N_CTX = 16
N_FSDP = 2


def with_spikes(array, stream_key, source, target, parts, factor):
    owner, partner = [(jnp.arange(array.shape[dim]) // (array.shape[dim] // parts)).reshape([-1 if axis == dim else 1 for axis in range(array.ndim)]) for dim in (source, target)]
    chosen = jax.random.permutation(stream_key, parts)[partner]
    strong = (owner == chosen) | (owner == (partner + parts // 2) % parts)
    return jnp.where(strong, factor * array, array)


def level_of(key, shape, cuts, least, high):
    def one(axis_at, blocks):
        draws = jax.random.uniform(jax.random.fold_in(jax.random.fold_in(key, 6), axis_at), (blocks,), jnp.float32, least / len(cuts), high / len(cuts))
        return jnp.repeat(jnp.exp(draws), shape[axis_at] // blocks).reshape((-1,) + (1,) * (len(shape) - axis_at - 1))

    gain = one(*cuts[0])
    for cut in cuts[1:]:
        gain = gain * one(*cut)
    return gain


def gaussian(rng, shape, scale, bound, split=(), held_as=jnp.bfloat16):
    drawn = scale * jax.random.normal(rng, shape, jnp.float32)
    if split:
        drawn = drawn * level_of(rng, shape, split, -0.22, 0.18)
    return jnp.clip(drawn, -bound, bound).astype(held_as)


def gaussian_with(rng, shape, deviation, most, cuts, heavy, held_as=jnp.bfloat16):
    array = deviation * jax.random.normal(rng, shape, jnp.float32)
    if cuts:
        array = array * level_of(rng, shape, cuts, -0.22, 0.18)
    return jnp.clip(with_spikes(array, jax.random.fold_in(rng, 3), *heavy), -most, most).astype(held_as)


def setup_inputs(seed: int = 0) -> dict:
    key_of = jax.random.split(jax.random.key(seed), 6)
    out_grad = gaussian_with(key_of[0], (D, TOKENS), 1.0, 6.0, ((0, 2), (1, 16)), (1, 0, 16, 2.0))
    gate_values = gaussian(key_of[1], (D, TOKENS), 1.0, 6.0, ((0, 2), (1, 16)))
    kv_product = gaussian(key_of[2], (D, TOKENS), 1.0, 6.0, ((0, 2), (1, 16)))
    w_out = gaussian(key_of[3], (D, D), D ** -0.5, 0.09375, ((0, 16), (1, 2)))
    filters = gaussian(key_of[4], (N_FSDP, N_CTX, CPD, TAPS), TAPS ** -0.5, 0.5, ((0, 2), (1, 16)))
    return {"out_grad": out_grad, "gate_values": gate_values, "kv_product": kv_product, "w_out": w_out, "filters": filters}


exact_mode = lax.Precision.HIGHEST

def toeplitz_pair(filters):
    tap_count = filters.shape[1]
    offset = jnp.arange(tap_count)[None, :] - jnp.arange(tap_count)[:, None]
    lower_take = jnp.take(filters, jnp.where(offset >= 0, offset, 0), axis=1)
    near_band = jnp.where(offset >= 0, lower_take, 0.0)
    upper_take = jnp.take(filters, jnp.where(offset < 0, offset + tap_count, 0), axis=1)
    far_band = jnp.where(offset < 0, upper_take, 0.0)
    return (near_band, far_band)

def causal_mix(filters, signal):
    channels, seq_len = signal.shape
    tap_count = filters.shape[1]
    near_band, far_band = toeplitz_pair(filters)
    current = signal.reshape(channels, seq_len // tap_count, tap_count)
    previous = jnp.concatenate([jnp.zeros((channels, 1, tap_count), signal.dtype), current[:, :-1]], axis=1)
    result = jnp.einsum('cbs,csr->cbr', current, near_band, precision=exact_mode)
    result = result + jnp.einsum('cbs,csr->cbr', previous, far_band, precision=exact_mode)
    return result.reshape(channels, seq_len)

def channel_block(block_args):
    filters, signal, cotangent = block_args
    mixed, pullback = jax.vjp(causal_mix, filters, signal)
    filter_part, signal_grad = pullback(cotangent)
    return (mixed, signal_grad, filter_part)

def reference(out_grad, gate_values, kv_product, w_out, filters):
    mix_grad = jnp.dot(w_out.T, out_grad, preferred_element_type=jnp.float32)
    conv_grad = (mix_grad * gate_values.astype(jnp.float32)).astype(jnp.bfloat16)
    groups = D // 128
    flat_filters = filters.astype(jnp.float32).reshape(groups, 128, TAPS)
    signal = kv_product.astype(jnp.float32).reshape(groups, 128, TOKENS)
    cotangent = conv_grad.astype(jnp.float32).reshape(groups, 128, TOKENS)
    mixed, signal_grad, filter_part = lax.map(channel_block, (flat_filters, signal, cotangent))
    mixed = mixed.reshape(D, TOKENS).astype(jnp.bfloat16)
    kv_grad = signal_grad.reshape(D, TOKENS).astype(jnp.bfloat16)
    norm_scale = 1.0 / math.sqrt(TOKENS)
    filter_grad = filter_part.reshape(filters.shape) * norm_scale
    mixed_wide = mixed.astype(jnp.float32)
    gate_grad = mix_grad * mixed_wide
    gated_rows = (gate_values.astype(jnp.float32) * mixed_wide).astype(jnp.bfloat16)
    w_grad = jnp.dot(out_grad, gated_rows.T, preferred_element_type=jnp.float32) * norm_scale
    return (gate_grad, kv_grad, filter_grad, w_grad)
```

```python
import functools
import math

import jax
import jax.numpy as jnp
from jax import lax
from jax.experimental import pallas as pl
from jax.experimental.pallas import tpu as pltpu
from jax.sharding import PartitionSpec as P

F32 = jnp.float32
BF16 = jnp.bfloat16
GROUP = 128
UNROLL = 8


def band_masks(taps):
    row = lax.broadcasted_iota(jnp.int32, (taps, taps), 0)
    lane = lax.broadcasted_iota(jnp.int32, (taps, taps), 1)
    return row, lane


def circulant(taps_row, taps):
    wide = jnp.broadcast_to(taps_row, (taps, taps))
    return pltpu.roll(wide, 0, 1, stride=1, stride_axis=0)


def mix_kernel(filt_ref, kv_ref, prior_ref, gate_ref, mixed_ref, gated_ref, cur, prev, out, filt):
    group, seq_len = kv_ref.shape
    taps = filt_ref.shape[1]
    blocks = seq_len // taps
    filt[...] = filt_ref[...].astype(F32)
    prev[:, 0, :] = prior_ref[...].astype(F32)
    for b in range(blocks):
        piece = kv_ref[:, b * taps : (b + 1) * taps].astype(F32)
        cur[:, b, :] = piece
        if b + 1 < blocks:
            prev[:, b + 1, :] = piece
    row, lane = band_masks(taps)
    near_mask = jnp.where(lane >= row, 1.0, 0.0).astype(BF16)

    def step(i, _):
        for u in range(UNROLL):
            c = i * UNROLL + u
            band = circulant(filt[pl.ds(c, 1), :], taps).astype(BF16)
            near = band * near_mask
            pair = jnp.concatenate([near, band - near], axis=0)
            data = jnp.concatenate([cur[c], prev[c]], axis=1).astype(BF16)
            out[c] = jnp.dot(data, pair, preferred_element_type=F32)
        return 0

    lax.fori_loop(0, group // UNROLL, step, 0)
    for b in range(blocks):
        span = slice(b * taps, (b + 1) * taps)
        mixed = out[:, b, :].astype(BF16)
        mixed_ref[:, span] = mixed
        gated_ref[:, span] = (gate_ref[:, span].astype(F32) * mixed.astype(F32)).astype(BF16)


def run_mix(filters, kv, prior, gate):
    chan, seq_len = kv.shape
    taps = filters.shape[1]
    blocks = seq_len // taps
    rows = lambda width: pl.BlockSpec((GROUP, width), lambda g: (g, 0))
    return pl.pallas_call(
        mix_kernel,
        grid=(chan // GROUP,),
        in_specs=[rows(taps), rows(seq_len), rows(taps), rows(seq_len)],
        out_specs=[rows(seq_len), rows(seq_len)],
        out_shape=[jax.ShapeDtypeStruct((chan, seq_len), BF16)] * 2,
        scratch_shapes=[pltpu.VMEM((GROUP, blocks, taps), F32)] * 3 + [pltpu.VMEM((GROUP, taps), F32)],
        compiler_params=pltpu.CompilerParams(vmem_limit_bytes=32 * 1024 * 1024),
        name="mix_kernel",
    )(filters, kv, prior, gate)


def grad_kernel(
    back_ref, grad_ref, after_ref, kv_ref, kv_grad_ref, filt_ref, cur, later, sig, out, back, total
):
    group, seq_len = kv_ref.shape
    taps = back_ref.shape[1]
    blocks = seq_len // taps
    back[...] = back_ref[...].astype(F32)
    later[:, blocks - 1, :] = after_ref[...].astype(F32)
    row, lane = band_masks(taps)
    flip = jnp.where(row + lane == taps - 1, 1.0, 0.0).astype(BF16)
    for b in range(blocks):
        span = slice(b * taps, (b + 1) * taps)
        piece = grad_ref[:, span].astype(F32)
        cur[:, b, :] = piece
        if b > 0:
            later[:, b - 1, :] = piece
        sig[:, b, :] = jnp.dot(kv_ref[:, span], flip, preferred_element_type=F32)
    near_mask = jnp.where(row >= lane, 1.0, 0.0).astype(BF16)
    upper = lane + row >= taps - 1

    def step(i, _):
        for u in range(UNROLL):
            c = i * UNROLL + u
            band = circulant(back[pl.ds(c, 1), :], taps).astype(BF16)
            near = band * near_mask
            pair = jnp.concatenate([near, band - near], axis=0)
            data = jnp.concatenate([cur[c], later[c]], axis=1).astype(BF16)
            out[c] = jnp.dot(data, pair, preferred_element_type=F32)
            outer = lax.dot_general(
                sig[c].astype(BF16), data, (((0,), (0,)), ((), ())), preferred_element_type=F32
            )
            joint = jnp.where(upper, outer[:, :taps], outer[:, taps:])
            skew = pltpu.roll(joint, 1, 1, stride=1, stride_axis=0)
            total[pl.ds(c, 1), :] = jnp.sum(skew, axis=0, keepdims=True)
        return 0

    lax.fori_loop(0, group // UNROLL, step, 0)
    for b in range(blocks):
        kv_grad_ref[:, b * taps : (b + 1) * taps] = out[:, b, :].astype(BF16)
    filt_ref[...] = total[...]


def run_grad(back, grad, after, kv):
    chan, seq_len = kv.shape
    taps = back.shape[1]
    blocks = seq_len // taps
    rows = lambda width: pl.BlockSpec((GROUP, width), lambda g: (g, 0))
    return pl.pallas_call(
        grad_kernel,
        grid=(chan // GROUP,),
        in_specs=[rows(taps), rows(seq_len), rows(taps), rows(seq_len)],
        out_specs=[rows(seq_len), rows(taps)],
        out_shape=[
            jax.ShapeDtypeStruct((chan, seq_len), BF16),
            jax.ShapeDtypeStruct((chan, taps), F32),
        ],
        scratch_shapes=[pltpu.VMEM((GROUP, blocks, taps), F32)] * 4
        + [pltpu.VMEM((GROUP, taps), F32)] * 2,
        compiler_params=pltpu.CompilerParams(vmem_limit_bytes=32 * 1024 * 1024),
        name="grad_kernel",
    )(back, grad, after, kv)


def on_device(out_grad, gate_values, kv_product, w_out, filters):
    ctx_count = lax.axis_size("ctx")
    chan_count = filters.shape[2]
    taps = filters.shape[3]
    seq_len = out_grad.shape[1]
    norm_scale = 1.0 / math.sqrt(ctx_count * seq_len)
    to_right = [(i, i + 1) for i in range(ctx_count - 1)]
    to_left = [(i + 1, i) for i in range(ctx_count - 1)]

    prior = lax.ppermute(kv_product[:, seq_len - taps :], "ctx", to_right)
    all_filters = lax.all_gather(filters.reshape(chan_count, taps), "ctx", axis=0, tiled=True)
    grad_full = lax.all_gather(out_grad, "fsdp", axis=0, tiled=True)
    w_full = lax.all_gather(w_out, "ctx", axis=0, tiled=True)

    mixed, gated = run_mix(all_filters, kv_product, prior, gate_values)
    w_part = lax.dot_general(
        grad_full, gated, (((1,), (1,)), ((), ())), preferred_element_type=F32
    )
    w_grad = lax.psum_scatter(w_part, "ctx", scatter_dimension=0, tiled=True) * norm_scale

    mix_grad = lax.dot_general(
        w_full, grad_full, (((0,), (0,)), ((), ())), preferred_element_type=F32
    )
    conv_grad = (mix_grad * gate_values.astype(F32)).astype(BF16)
    gate_grad = mix_grad * mixed.astype(F32)
    after = lax.ppermute(conv_grad[:, :taps], "ctx", to_left)
    back = jnp.roll(all_filters[:, ::-1], 1, axis=1)
    kv_grad, filt_part = run_grad(back, conv_grad, after, kv_product)
    filter_grad = lax.psum_scatter(filt_part, "ctx", scatter_dimension=0, tiled=True) * norm_scale
    return (gate_grad, kv_grad, filter_grad.reshape(filters.shape), w_grad)


def solution(mesh):
    in_specs = (
        P("fsdp", "ctx"),
        P("fsdp", "ctx"),
        P("fsdp", "ctx"),
        P("ctx", "fsdp"),
        P("fsdp", "ctx", None, None),
    )
    out_specs = (P("fsdp", "ctx"), P("fsdp", "ctx"), P("fsdp", "ctx", None, None), P("ctx", "fsdp"))
    return jax.shard_map(
        on_device, mesh=mesh, in_specs=in_specs, out_specs=out_specs, check_vma=False
    )
```

```python
import math

import jax
import jax.numpy as jnp
import ml_dtypes
import numpy as np
from jax import lax
from jax.experimental import pallas as pl
from jax.experimental.pallas import tpu as pltpu
from jax.sharding import PartitionSpec as P

F32 = jnp.float32
BF16 = jnp.bfloat16
MIB = 1024 * 1024


def split_pair(matrix):
    high = matrix.astype(ml_dtypes.bfloat16)
    low = (matrix - high.astype(np.float64)).astype(ml_dtypes.bfloat16)
    return high, low


def dft_matrices(taps):
    points = 2 * taps
    place = np.arange(taps)
    angle = 2.0 * np.pi * ((place[:, None] * place[None, :]) % points) / points
    turn = (-1.0) ** place
    forward = np.concatenate([np.cos(angle), -np.sin(angle)], axis=1)
    forward[:, taps] = turn
    weight = np.full((taps, 1), 2.0 / points)
    weight[0] = 1.0 / points
    backward = np.concatenate([weight * np.cos(angle), -weight * np.sin(angle)], axis=0)
    backward[taps, :] = turn / points
    forward = np.concatenate(split_pair(forward), axis=0)
    backward = np.concatenate(split_pair(backward), axis=1)
    return forward, backward


def spectrum(block, forward):
    taps = block.shape[1]
    both = jnp.dot(jnp.concatenate([block, block], axis=1), forward, preferred_element_type=F32)
    return both[:, :taps], both[:, taps:]


def inverse(real, imag, backward):
    taps = real.shape[1]
    whole = jnp.concatenate([real, imag], axis=1)
    high = whole.astype(BF16)
    low = (whole - high.astype(F32)).astype(BF16)
    both = jnp.dot(high, backward, preferred_element_type=F32)
    rest = jnp.dot(low, backward[:, :taps], preferred_element_type=F32)
    return both[:, :taps] + both[:, taps:] + rest


def lane_facts(taps):
    lane = lax.broadcasted_iota(jnp.int32, (1, taps), 1)
    sign = jnp.where(lane % 2 == 0, 1.0, -1.0)
    return lane == 0, sign


def filter_spectrum(filt, forward, first):
    real, imag = spectrum(filt, forward)
    return real, jnp.where(first, imag, real), jnp.where(first, 0.0, imag)


def mix_kernel(filt_ref, kv_ref, prior_ref, gate_ref, forward_ref, backward_ref, mixed_ref, gated_ref):
    taps = filt_ref.shape[1]
    blocks = kv_ref.shape[1] // taps
    forward, backward = forward_ref[...], backward_ref[...]
    first, sign = lane_facts(taps)
    sign_imag = jnp.where(first, 1.0, sign)
    h_real, h_last, h_imag = filter_spectrum(filt_ref[...], forward, first)
    prev_real, prev_imag = spectrum(prior_ref[...], forward)
    for b in range(blocks):
        span = slice(b * taps, (b + 1) * taps)
        real, imag = spectrum(kv_ref[:, span], forward)
        win_real = real + sign * prev_real
        win_imag = imag + sign_imag * prev_imag
        mixed = inverse(
            h_real * win_real - h_imag * win_imag, h_last * win_imag + h_imag * win_real, backward
        ).astype(BF16)
        mixed_ref[:, span] = mixed
        gated_ref[:, span] = (gate_ref[:, span].astype(F32) * mixed.astype(F32)).astype(BF16)
        prev_real, prev_imag = real, imag


def run_mix(filters, kv, prior, gate, forward, backward):
    chan, seq_len = kv.shape
    taps = filters.shape[1]
    group = min(256, chan)
    rows = lambda width: pl.BlockSpec((group, width), lambda g: (g, 0))
    whole = lambda array: pl.BlockSpec(array.shape, lambda g: (0, 0))
    return pl.pallas_call(
        mix_kernel,
        grid=(chan // group,),
        in_specs=[rows(taps), rows(seq_len), rows(taps), rows(seq_len), whole(forward), whole(backward)],
        out_specs=[rows(seq_len), rows(seq_len)],
        out_shape=[jax.ShapeDtypeStruct((chan, seq_len), BF16)] * 2,
        compiler_params=pltpu.CompilerParams(vmem_limit_bytes=32 * MIB),
        name="mix_kernel",
    )(filters, kv, prior, gate, forward, backward)


def grad_kernel(
    filt_ref, grad_ref, after_ref, kv_ref, forward_ref, backward_ref, kv_grad_ref, filt_grad_ref
):
    taps = filt_ref.shape[1]
    blocks = kv_ref.shape[1] // taps
    forward, backward = forward_ref[...], backward_ref[...]
    first, sign = lane_facts(taps)
    sign_imag = jnp.where(first, 1.0, sign)
    h_real, h_last, h_imag = filter_spectrum(filt_ref[...], forward, first)
    total_real = total_imag = None
    next_real, next_imag = spectrum(after_ref[...], forward)
    for b in reversed(range(blocks)):
        span = slice(b * taps, (b + 1) * taps)
        real, imag = spectrum(grad_ref[:, span], forward)
        win_real = real + sign * next_real
        win_imag = imag + sign_imag * next_imag
        kv_grad_ref[:, span] = inverse(
            h_real * win_real + h_imag * win_imag, h_last * win_imag - h_imag * win_real, backward
        ).astype(BF16)
        x_real, x_last, x_imag = filter_spectrum(kv_ref[:, span], forward, first)
        part_real = x_real * win_real + x_imag * win_imag
        part_imag = x_last * win_imag - x_imag * win_real
        total_real = part_real if total_real is None else total_real + part_real
        total_imag = part_imag if total_imag is None else total_imag + part_imag
        next_real, next_imag = real, imag
    filt_grad_ref[...] = inverse(total_real, total_imag, backward)


def run_grad(filters, grad, after, kv, forward, backward):
    chan, seq_len = kv.shape
    taps = filters.shape[1]
    group = min(256, chan)
    rows = lambda width: pl.BlockSpec((group, width), lambda g: (g, 0))
    whole = lambda array: pl.BlockSpec(array.shape, lambda g: (0, 0))
    return pl.pallas_call(
        grad_kernel,
        grid=(chan // group,),
        in_specs=[rows(taps), rows(seq_len), rows(taps), rows(seq_len), whole(forward), whole(backward)],
        out_specs=[rows(seq_len), rows(taps)],
        out_shape=[
            jax.ShapeDtypeStruct((chan, seq_len), BF16),
            jax.ShapeDtypeStruct((chan, taps), F32),
        ],
        compiler_params=pltpu.CompilerParams(vmem_limit_bytes=32 * MIB),
        name="grad_kernel",
    )(filters, grad, after, kv, forward, backward)


def weight_kernel(place_ref, g00, g01, g10, g11, left_ref, right_ref, send_a, keep_a, send_b, keep_b):
    rows = g00.shape[0]
    stack = jnp.concatenate([g01[...], g11[...], g00[...], g10[...]], axis=0)
    contract = (((1,), (1,)), ((), ()))
    left = lax.dot_general(stack, left_ref[...], contract, preferred_element_type=F32).astype(BF16)
    send_a[0] = left[:rows]
    send_a[1] = left[rows : 2 * rows]
    keep_a[0] = left[2 * rows : 3 * rows]
    keep_a[1] = left[3 * rows :]
    right = lax.dot_general(stack, right_ref[...], contract, preferred_element_type=F32).astype(BF16)
    send_b[0] = right[3 * rows :]
    send_b[1] = right[rows : 2 * rows]
    keep_b[0] = right[2 * rows : 3 * rows]
    keep_b[1] = right[:rows]


def run_weight(place, grad_full, gated, rows):
    chan, seq_len = gated.shape
    width = chan // 4
    grad_spec = lambda k: pl.BlockSpec((rows, seq_len), lambda n, place: (place[k], 0))
    gated_spec = lambda first: pl.BlockSpec((width, seq_len), lambda n, place: (n + first, 0))
    out_spec = pl.BlockSpec((2, rows, width), lambda n, place: (0, 0, n))
    return pl.pallas_call(
        weight_kernel,
        grid_spec=pltpu.PrefetchScalarGridSpec(
            num_scalar_prefetch=1,
            grid=(2,),
            in_specs=[grad_spec(k) for k in range(4)] + [gated_spec(0), gated_spec(2)],
            out_specs=[out_spec] * 4,
        ),
        out_shape=[jax.ShapeDtypeStruct((2, rows, chan // 2), BF16)] * 4,
        compiler_params=pltpu.CompilerParams(vmem_limit_bytes=48 * MIB),
        name="weight_kernel",
    )(place, grad_full, grad_full, grad_full, grad_full, gated, gated)


class Layout:
    def __init__(self):
        self.count = lax.axis_size("ctx")
        self.depth = self.count // 4
        index = lax.axis_index("ctx")
        self.z, self.y, self.x = index // 4, (index // 2) % 2, index % 2

    def swap_x(self, array):
        return lax.ppermute(array, "ctx", [(i, i ^ 1) for i in range(self.count)])

    def swap_y(self, array):
        return lax.ppermute(array, "ctx", [(i, i ^ 2) for i in range(self.count)])

    def shift_z(self, array, by):
        return lax.ppermute(array, "ctx", [(i, (i + 4 * by) % self.count) for i in range(self.count)])


def pick(bit, array, axis):
    halves = [lax.index_in_dim(array, k, axis, keepdims=False) for k in range(2)]
    return jnp.where(bit == 0, halves[0], halves[1])


def gather_filters(at, own):
    def ordered(bit, mine, other):
        return jnp.stack([jnp.where(bit == 0, mine, other), jnp.where(bit == 0, other, mine)])

    pair = ordered(at.x, own, at.swap_x(own))
    plane = ordered(at.y, pair, at.swap_y(pair))
    slots = [at.shift_z(plane, by) for by in range(at.depth - 1, 0, -1)] + [plane]
    ring = jnp.stack(slots + slots)
    whole = lax.dynamic_slice_in_dim(ring, at.depth - 1 - at.z, at.depth, axis=0)
    return whole.reshape((at.count * own.shape[0],) + own.shape[1:])


def reduce_filters(at, part, chan_count):
    taps = part.shape[1]
    part = part.reshape(at.depth, 2, 2, chan_count, taps)
    part = pick(at.x, part, 2) + at.swap_x(pick(1 - at.x, part, 2))
    part = pick(at.y, part, 1) + at.swap_y(pick(1 - at.y, part, 1))
    at_z = lambda by: lax.dynamic_index_in_dim(part, (at.z + by) % at.depth, 0, keepdims=False)
    total = at_z(0)
    for by in range(1, at.depth):
        total = total + at.shift_z(at_z(by), by)
    return total


def reduce_weight(at, grad_full, gated, rows):
    total = None
    received = []
    for by in sorted(range(at.depth), key=lambda d: -min(d, at.depth - d)):
        base = 4 * ((at.z + by) % at.depth)
        place = jnp.stack(
            [base + 2 * (at.y ^ dy) + (at.x ^ dx) for dy in range(2) for dx in range(2)]
        ).astype(jnp.int32)
        send_a, keep_a, send_b, keep_b = run_weight(place, grad_full, gated, rows)
        got_a, got_b = at.swap_x(send_a), at.swap_y(send_b)
        next_a = (keep_a[1].astype(F32) + got_a[1].astype(F32)).astype(BF16)
        next_b = (keep_b[1].astype(F32) + got_b[1].astype(F32)).astype(BF16)
        last_a, last_b = at.swap_y(next_a), at.swap_x(next_b)
        sum_a = keep_a[0].astype(F32) + got_a[0].astype(F32) + last_a.astype(F32)
        sum_b = keep_b[0].astype(F32) + got_b[0].astype(F32) + last_b.astype(F32)
        joint = jnp.concatenate([sum_a, sum_b], axis=1)
        if by == 0:
            total = joint
        else:
            received.append(at.shift_z(joint.astype(BF16), by))
    for piece in received:
        total = total + piece.astype(F32)
    return total


def on_device(out_grad, gate_values, kv_product, w_out, filters):
    at = Layout()
    chan_count = filters.shape[2]
    taps = filters.shape[3]
    seq_len = out_grad.shape[1]
    norm_scale = 1.0 / math.sqrt(at.count * seq_len)
    to_right = [(i, i + 1) for i in range(at.count - 1)]
    to_left = [(i + 1, i) for i in range(at.count - 1)]
    forward, backward = (jnp.asarray(m) for m in dft_matrices(taps))

    prior = lax.ppermute(kv_product[:, seq_len - taps :], "ctx", to_right)
    all_filters = gather_filters(at, filters.reshape(chan_count, taps))
    grad_full = lax.all_gather(out_grad, "fsdp", axis=0, tiled=True)
    w_full = lax.all_gather(w_out, "ctx", axis=0, tiled=True)

    mixed, gated = run_mix(all_filters, kv_product, prior, gate_values, forward, backward)
    w_grad = reduce_weight(at, grad_full, gated, w_out.shape[0]) * norm_scale

    mix_grad = lax.dot_general(
        w_full, grad_full, (((0,), (0,)), ((), ())), preferred_element_type=F32
    )
    conv_grad = (mix_grad * gate_values.astype(F32)).astype(BF16)
    gate_grad = mix_grad * mixed.astype(F32)
    after = lax.ppermute(conv_grad[:, :taps], "ctx", to_left)
    kv_grad, filt_part = run_grad(all_filters, conv_grad, after, kv_product, forward, backward)
    filter_grad = reduce_filters(at, filt_part, chan_count) * norm_scale
    return (gate_grad, kv_grad, filter_grad.reshape(filters.shape), w_grad)


def solution(mesh):
    in_specs = (
        P("fsdp", "ctx"),
        P("fsdp", "ctx"),
        P("fsdp", "ctx"),
        P("ctx", "fsdp"),
        P("fsdp", "ctx", None, None),
    )
    out_specs = (P("fsdp", "ctx"), P("fsdp", "ctx"), P("fsdp", "ctx", None, None), P("ctx", "fsdp"))
    return jax.shard_map(
        on_device, mesh=mesh, in_specs=in_specs, out_specs=out_specs, check_vma=False
    )
```

```python
import math

import jax
import jax.numpy as jnp
import ml_dtypes
import numpy as np
from jax import lax
from jax.experimental import pallas as pl
from jax.experimental.pallas import tpu as pltpu
from jax.sharding import PartitionSpec as P

F32 = jnp.float32
BF16 = jnp.bfloat16
MIB = 1024 * 1024


def split_pair(matrix):
    high = matrix.astype(ml_dtypes.bfloat16)
    low = (matrix - high.astype(np.float64)).astype(ml_dtypes.bfloat16)
    return high, low


def dft_matrices(taps):
    points = 2 * taps
    place = np.arange(taps)
    angle = 2.0 * np.pi * ((place[:, None] * place[None, :]) % points) / points
    turn = (-1.0) ** place
    forward = np.concatenate([np.cos(angle), -np.sin(angle)], axis=1)
    forward[:, taps] = turn
    weight = np.full((taps, 1), 2.0 / points)
    weight[0] = 1.0 / points
    backward = np.concatenate([weight * np.cos(angle), -weight * np.sin(angle)], axis=0)
    backward[taps, :] = turn / points
    forward = np.concatenate(split_pair(forward), axis=0)
    backward = np.concatenate(split_pair(backward), axis=1)
    return forward, backward


def spectrum(block, forward):
    taps = block.shape[1]
    both = jnp.dot(jnp.concatenate([block, block], axis=1), forward, preferred_element_type=F32)
    return both[:, :taps], both[:, taps:]


def inverse(real, imag, backward):
    taps = real.shape[1]
    whole = jnp.concatenate([real, imag], axis=1)
    high = whole.astype(BF16)
    low = (whole - high.astype(F32)).astype(BF16)
    both = jnp.dot(high, backward, preferred_element_type=F32)
    rest = jnp.dot(low, backward[:, :taps], preferred_element_type=F32)
    return both[:, :taps] + both[:, taps:] + rest


def lane_facts(taps):
    lane = lax.broadcasted_iota(jnp.int32, (1, taps), 1)
    sign = jnp.where(lane % 2 == 0, 1.0, -1.0)
    return lane == 0, sign


def filter_spectrum(filt, forward, first):
    real, imag = spectrum(filt, forward)
    return real, jnp.where(first, imag, real), jnp.where(first, 0.0, imag)


def mix_kernel(filt_ref, kv_ref, prior_ref, gate_ref, forward_ref, backward_ref, mixed_ref, gated_ref):
    taps = filt_ref.shape[1]
    blocks = kv_ref.shape[1] // taps
    forward, backward = forward_ref[...], backward_ref[...]
    first, sign = lane_facts(taps)
    sign_imag = jnp.where(first, 1.0, sign)
    h_real, h_last, h_imag = filter_spectrum(filt_ref[...], forward, first)
    prev_real, prev_imag = spectrum(prior_ref[...], forward)
    for b in range(blocks):
        span = slice(b * taps, (b + 1) * taps)
        real, imag = spectrum(kv_ref[:, span], forward)
        win_real = real + sign * prev_real
        win_imag = imag + sign_imag * prev_imag
        mixed = inverse(
            h_real * win_real - h_imag * win_imag, h_last * win_imag + h_imag * win_real, backward
        ).astype(BF16)
        mixed_ref[:, span] = mixed
        gated_ref[:, span] = (gate_ref[:, span].astype(F32) * mixed.astype(F32)).astype(BF16)
        prev_real, prev_imag = real, imag


def run_mix(filters, kv, prior, gate, forward, backward):
    chan, seq_len = kv.shape
    taps = filters.shape[1]
    group = min(256, chan)
    rows = lambda width: pl.BlockSpec((group, width), lambda g: (g, 0))
    whole = lambda array: pl.BlockSpec(array.shape, lambda g: (0, 0))
    return pl.pallas_call(
        mix_kernel,
        grid=(chan // group,),
        in_specs=[rows(taps), rows(seq_len), rows(taps), rows(seq_len), whole(forward), whole(backward)],
        out_specs=[rows(seq_len), rows(seq_len)],
        out_shape=[jax.ShapeDtypeStruct((chan, seq_len), BF16)] * 2,
        compiler_params=pltpu.CompilerParams(vmem_limit_bytes=32 * MIB),
        name="mix_kernel",
    )(filters, kv, prior, gate, forward, backward)


def grad_kernel(
    filt_ref, grad_ref, after_ref, kv_ref, forward_ref, backward_ref, kv_grad_ref, filt_grad_ref
):
    taps = filt_ref.shape[1]
    blocks = kv_ref.shape[1] // taps
    forward, backward = forward_ref[...], backward_ref[...]
    first, sign = lane_facts(taps)
    sign_imag = jnp.where(first, 1.0, sign)
    h_real, h_last, h_imag = filter_spectrum(filt_ref[...], forward, first)
    total_real = total_imag = None
    next_real, next_imag = spectrum(after_ref[...], forward)
    for b in reversed(range(blocks)):
        span = slice(b * taps, (b + 1) * taps)
        real, imag = spectrum(grad_ref[:, span], forward)
        win_real = real + sign * next_real
        win_imag = imag + sign_imag * next_imag
        kv_grad_ref[:, span] = inverse(
            h_real * win_real + h_imag * win_imag, h_last * win_imag - h_imag * win_real, backward
        ).astype(BF16)
        x_real, x_last, x_imag = filter_spectrum(kv_ref[:, span], forward, first)
        part_real = x_real * win_real + x_imag * win_imag
        part_imag = x_last * win_imag - x_imag * win_real
        total_real = part_real if total_real is None else total_real + part_real
        total_imag = part_imag if total_imag is None else total_imag + part_imag
        next_real, next_imag = real, imag
    filt_grad_ref[...] = inverse(total_real, total_imag, backward)


def run_grad(filters, grad, after, kv, forward, backward):
    chan, seq_len = kv.shape
    taps = filters.shape[1]
    group = min(256, chan)
    rows = lambda width: pl.BlockSpec((group, width), lambda g: (g, 0))
    whole = lambda array: pl.BlockSpec(array.shape, lambda g: (0, 0))
    return pl.pallas_call(
        grad_kernel,
        grid=(chan // group,),
        in_specs=[rows(taps), rows(seq_len), rows(taps), rows(seq_len), whole(forward), whole(backward)],
        out_specs=[rows(seq_len), rows(taps)],
        out_shape=[
            jax.ShapeDtypeStruct((chan, seq_len), BF16),
            jax.ShapeDtypeStruct((chan, taps), F32),
        ],
        compiler_params=pltpu.CompilerParams(vmem_limit_bytes=32 * MIB),
        name="grad_kernel",
    )(filters, grad, after, kv, forward, backward)


def weight_kernel(place_ref, g00, g01, g10, g11, left_ref, right_ref, send_a, keep_a, send_b, keep_b):
    rows = g00.shape[0]
    stack = jnp.concatenate([g01[...], g11[...], g00[...], g10[...]], axis=0)
    contract = (((1,), (1,)), ((), ()))
    left = lax.dot_general(stack, left_ref[...], contract, preferred_element_type=F32).astype(BF16)
    send_a[0] = left[:rows]
    send_a[1] = left[rows : 2 * rows]
    keep_a[0] = left[2 * rows : 3 * rows]
    keep_a[1] = left[3 * rows :]
    right = lax.dot_general(stack, right_ref[...], contract, preferred_element_type=F32).astype(BF16)
    send_b[0] = right[3 * rows :]
    send_b[1] = right[rows : 2 * rows]
    keep_b[0] = right[2 * rows : 3 * rows]
    keep_b[1] = right[:rows]


def run_weight(place, grad_full, gated, rows):
    chan, seq_len = gated.shape
    width = chan // 4
    grad_spec = lambda k: pl.BlockSpec((rows, seq_len), lambda n, place: (place[k], 0))
    gated_spec = lambda first: pl.BlockSpec((width, seq_len), lambda n, place: (n + first, 0))
    out_spec = pl.BlockSpec((2, rows, width), lambda n, place: (0, 0, n))
    return pl.pallas_call(
        weight_kernel,
        grid_spec=pltpu.PrefetchScalarGridSpec(
            num_scalar_prefetch=1,
            grid=(2,),
            in_specs=[grad_spec(k) for k in range(4)] + [gated_spec(0), gated_spec(2)],
            out_specs=[out_spec] * 4,
        ),
        out_shape=[jax.ShapeDtypeStruct((2, rows, chan // 2), BF16)] * 4,
        compiler_params=pltpu.CompilerParams(vmem_limit_bytes=48 * MIB),
        name="weight_kernel",
    )(place, grad_full, grad_full, grad_full, grad_full, gated, gated)


def product_kernel(slots, place_ref, grad_hbm, *refs):
    pieces, (mixed_ref, gate_ref, gate_grad_ref, conv_grad_ref, grad, sems) = refs[: 5 * slots], refs[5 * slots :]
    step = pl.program_id(0)
    rows = pieces[0].shape[1]

    @pl.when(step == 0)
    def _():
        copies = [
            pltpu.make_async_copy(
                grad_hbm.at[pl.ds(pl.multiple_of(place_ref[k] * rows, rows), rows)],
                grad.at[pl.ds(k * rows, rows)],
                sems.at[k],
            )
            for k in range(4 * slots)
        ]
        for copy in copies:
            copy.start()
        for copy in copies:
            copy.wait()

    upper = step < pl.num_programs(0) // 2
    wide = []
    for k in range(slots):
        own, by_x, by_y, diag_a, diag_b = pieces[5 * k : 5 * k + 5]
        wide += [own[...], by_x[...], by_y[...], jnp.where(upper, diag_a[...], diag_b[...])]
    total = jnp.dot(jnp.concatenate(wide, axis=1), grad[...], preferred_element_type=F32)
    gate_grad_ref[...] = total * mixed_ref[...].astype(F32)
    conv_grad_ref[...] = (total * gate_ref[...].astype(F32)).astype(BF16)


def run_product(place, grad_full, pieces, mixed, gate):
    chan, seq_len = mixed.shape
    depth = grad_full.shape[0]
    rows = pieces[0].shape[1]
    slots = len(pieces) // 5
    group = min(512, chan // 2)
    half = chan // 2 // group
    full = lambda width: pl.BlockSpec((group, width), lambda m, place: (m, 0))
    low = pl.BlockSpec((group, rows), lambda m, place: (jnp.minimum(m, half - 1), 0))
    high = pl.BlockSpec((group, rows), lambda m, place: (jnp.maximum(m - half, 0), 0))
    return pl.pallas_call(
        lambda *refs: product_kernel(slots, *refs),
        grid_spec=pltpu.PrefetchScalarGridSpec(
            num_scalar_prefetch=1,
            grid=(chan // group,),
            in_specs=[pl.BlockSpec(memory_space=pl.ANY)]
            + [full(rows), full(rows), full(rows), low, high] * slots
            + [full(seq_len), full(seq_len)],
            out_specs=[full(seq_len), full(seq_len)],
            scratch_shapes=[pltpu.VMEM((depth, seq_len), BF16), pltpu.SemaphoreType.DMA((4 * slots,))],
        ),
        out_shape=[
            jax.ShapeDtypeStruct((chan, seq_len), F32),
            jax.ShapeDtypeStruct((chan, seq_len), BF16),
        ],
        compiler_params=pltpu.CompilerParams(vmem_limit_bytes=50 * MIB),
        name="product_kernel",
    )(place, grad_full, *pieces, mixed, gate)


class Layout:
    def __init__(self):
        self.count = lax.axis_size("ctx")
        self.depth = self.count // 4
        index = lax.axis_index("ctx")
        self.z, self.y, self.x = index // 4, (index // 2) % 2, index % 2

    def swap_x(self, array):
        return lax.ppermute(array, "ctx", [(i, i ^ 1) for i in range(self.count)])

    def swap_y(self, array):
        return lax.ppermute(array, "ctx", [(i, i ^ 2) for i in range(self.count)])

    def shift_z(self, array, by):
        return lax.ppermute(array, "ctx", [(i, (i + 4 * by) % self.count) for i in range(self.count)])


def pick(bit, array, axis):
    halves = [lax.index_in_dim(array, k, axis, keepdims=False) for k in range(2)]
    return jnp.where(bit == 0, halves[0], halves[1])


def gather_filters(at, own):
    def ordered(bit, mine, other):
        return jnp.stack([jnp.where(bit == 0, mine, other), jnp.where(bit == 0, other, mine)])

    pair = ordered(at.x, own, at.swap_x(own))
    plane = ordered(at.y, pair, at.swap_y(pair))
    slots = [at.shift_z(plane, by) for by in range(at.depth - 1, 0, -1)] + [plane]
    ring = jnp.stack(slots + slots)
    whole = lax.dynamic_slice_in_dim(ring, at.depth - 1 - at.z, at.depth, axis=0)
    return whole.reshape((at.count * own.shape[0],) + own.shape[1:])


def reduce_filters(at, part, chan_count):
    taps = part.shape[1]
    part = part.reshape(at.depth, 2, 2, chan_count, taps)
    part = pick(at.x, part, 2) + at.swap_x(pick(1 - at.x, part, 2))
    part = pick(at.y, part, 1) + at.swap_y(pick(1 - at.y, part, 1))
    at_z = lambda by: lax.dynamic_index_in_dim(part, (at.z + by) % at.depth, 0, keepdims=False)
    total = at_z(0)
    for by in range(1, at.depth):
        total = total + at.shift_z(at_z(by), by)
    return total


def gather_weight(at, own):
    half = own.shape[0] // 2
    pieces, place = [], []
    before = None
    for by in sorted(range(at.depth), key=lambda d: min(d, at.depth - d)):
        if by == 0:
            slot = own
        else:
            source = own if before is None else lax.optimization_barrier((own, before))[0]
            slot = before = at.shift_z(source, by)
        from_x, from_y = at.swap_x(slot), at.swap_y(slot)
        pieces += [slot, from_x, from_y, at.swap_x(from_y[:half]), at.swap_y(from_x[half:])]
        base = 4 * ((at.z - by) % at.depth)
        place += [base + 2 * (at.y ^ dy) + (at.x ^ dx) for dy in range(2) for dx in range(2)]
    return pieces, jnp.stack(place).astype(jnp.int32)


def reduce_weight(at, grad_full, gated, rows):
    total = None
    received = []
    for by in sorted(range(at.depth), key=lambda d: -min(d, at.depth - d)):
        base = 4 * ((at.z + by) % at.depth)
        place = jnp.stack(
            [base + 2 * (at.y ^ dy) + (at.x ^ dx) for dy in range(2) for dx in range(2)]
        ).astype(jnp.int32)
        send_a, keep_a, send_b, keep_b = run_weight(place, grad_full, gated, rows)
        got_a, got_b = at.swap_x(send_a), at.swap_y(send_b)
        next_a = (keep_a[1].astype(F32) + got_a[1].astype(F32)).astype(BF16)
        next_b = (keep_b[1].astype(F32) + got_b[1].astype(F32)).astype(BF16)
        last_a, last_b = at.swap_y(next_a), at.swap_x(next_b)
        sum_a = keep_a[0].astype(F32) + got_a[0].astype(F32) + last_a.astype(F32)
        sum_b = keep_b[0].astype(F32) + got_b[0].astype(F32) + last_b.astype(F32)
        joint = jnp.concatenate([sum_a, sum_b], axis=1)
        if by == 0:
            total = joint
        else:
            received.append(at.shift_z(joint.astype(BF16), by))
    for piece in received:
        total = total + piece.astype(F32)
    return total


def on_device(out_grad, gate_values, kv_product, w_out, filters):
    at = Layout()
    chan_count = filters.shape[2]
    taps = filters.shape[3]
    seq_len = out_grad.shape[1]
    norm_scale = 1.0 / math.sqrt(at.count * seq_len)
    to_right = [(i, i + 1) for i in range(at.count - 1)]
    to_left = [(i + 1, i) for i in range(at.count - 1)]
    forward, backward = (jnp.asarray(m) for m in dft_matrices(taps))

    prior = lax.ppermute(kv_product[:, seq_len - taps :], "ctx", to_right)
    all_filters = gather_filters(at, filters.reshape(chan_count, taps))
    grad_full = lax.all_gather(out_grad, "fsdp", axis=0, tiled=True)
    pieces, place = gather_weight(at, w_out.T)

    mixed, gated = run_mix(all_filters, kv_product, prior, gate_values, forward, backward)
    w_grad = reduce_weight(at, grad_full, gated, w_out.shape[0]) * norm_scale

    gate_grad, conv_grad = run_product(place, grad_full, pieces, mixed, gate_values)
    after = lax.ppermute(conv_grad[:, :taps], "ctx", to_left)
    kv_grad, filt_part = run_grad(all_filters, conv_grad, after, kv_product, forward, backward)
    filter_grad = reduce_filters(at, filt_part, chan_count) * norm_scale
    return (gate_grad, kv_grad, filter_grad.reshape(filters.shape), w_grad)


def solution(mesh):
    in_specs = (
        P("fsdp", "ctx"),
        P("fsdp", "ctx"),
        P("fsdp", "ctx"),
        P("ctx", "fsdp"),
        P("fsdp", "ctx", None, None),
    )
    out_specs = (P("fsdp", "ctx"), P("fsdp", "ctx"), P("fsdp", "ctx", None, None), P("ctx", "fsdp"))
    return jax.shard_map(
        on_device, mesh=mesh, in_specs=in_specs, out_specs=out_specs, check_vma=False
    )
```

```python
import math

import jax
import jax.numpy as jnp
import ml_dtypes
import numpy as np
from jax import lax
from jax.experimental import pallas as pl
from jax.experimental.pallas import tpu as pltpu
from jax.sharding import PartitionSpec as P

F32 = jnp.float32
BF16 = jnp.bfloat16
MIB = 1024 * 1024


def split_pair(matrix):
    high = matrix.astype(ml_dtypes.bfloat16)
    low = (matrix - high.astype(np.float64)).astype(ml_dtypes.bfloat16)
    return high, low


def dft_matrices(taps):
    points = 2 * taps
    place = np.arange(taps)
    angle = 2.0 * np.pi * ((place[:, None] * place[None, :]) % points) / points
    turn = (-1.0) ** place
    forward = np.concatenate([np.cos(angle), -np.sin(angle)], axis=1)
    forward[:, taps] = turn
    weight = np.full((taps, 1), 2.0 / points)
    weight[0] = 1.0 / points
    backward = np.concatenate([weight * np.cos(angle), -weight * np.sin(angle)], axis=0)
    backward[taps, :] = turn / points
    forward = np.concatenate(split_pair(forward), axis=0)
    backward = np.concatenate(split_pair(backward), axis=1)
    return forward, backward


def spectrum(block, forward):
    taps = block.shape[1]
    both = jnp.dot(jnp.concatenate([block, block], axis=1), forward, preferred_element_type=F32)
    return both[:, :taps], both[:, taps:]


def inverse(real, imag, backward):
    taps = real.shape[1]
    whole = jnp.concatenate([real, imag], axis=1)
    high = whole.astype(BF16)
    low = (whole - high.astype(F32)).astype(BF16)
    both = jnp.dot(high, backward, preferred_element_type=F32)
    rest = jnp.dot(low, backward[:, :taps], preferred_element_type=F32)
    return both[:, :taps] + both[:, taps:] + rest


def lane_facts(taps):
    lane = lax.broadcasted_iota(jnp.int32, (1, taps), 1)
    sign = jnp.where(lane % 2 == 0, 1.0, -1.0)
    return lane == 0, sign


def filter_spectrum(filt, forward, first):
    real, imag = spectrum(filt, forward)
    return real, jnp.where(first, imag, real), jnp.where(first, 0.0, imag)


def mix_kernel(filt_ref, kv_ref, prior_ref, gate_ref, forward_ref, backward_ref, mixed_ref, gated_ref):
    taps = filt_ref.shape[1]
    blocks = kv_ref.shape[1] // taps
    forward, backward = forward_ref[...], backward_ref[...]
    first, sign = lane_facts(taps)
    sign_imag = jnp.where(first, 1.0, sign)
    h_real, h_last, h_imag = filter_spectrum(filt_ref[...], forward, first)
    prev_real, prev_imag = spectrum(prior_ref[...], forward)
    for b in range(blocks):
        span = slice(b * taps, (b + 1) * taps)
        real, imag = spectrum(kv_ref[:, span], forward)
        win_real = real + sign * prev_real
        win_imag = imag + sign_imag * prev_imag
        mixed = inverse(
            h_real * win_real - h_imag * win_imag, h_last * win_imag + h_imag * win_real, backward
        ).astype(BF16)
        mixed_ref[:, span] = mixed
        gated_ref[:, span] = (gate_ref[:, span].astype(F32) * mixed.astype(F32)).astype(BF16)
        prev_real, prev_imag = real, imag


def run_mix(filters, kv, prior, gate, forward, backward):
    chan, seq_len = kv.shape
    taps = filters.shape[1]
    group = min(256, chan)
    rows = lambda width: pl.BlockSpec((group, width), lambda g: (g, 0))
    whole = lambda array: pl.BlockSpec(array.shape, lambda g: (0, 0))
    return pl.pallas_call(
        mix_kernel,
        grid=(chan // group,),
        in_specs=[rows(taps), rows(seq_len), rows(taps), rows(seq_len), whole(forward), whole(backward)],
        out_specs=[rows(seq_len), rows(seq_len)],
        out_shape=[jax.ShapeDtypeStruct((chan, seq_len), BF16)] * 2,
        compiler_params=pltpu.CompilerParams(vmem_limit_bytes=32 * MIB),
        name="mix_kernel",
    )(filters, kv, prior, gate, forward, backward)


def weight_kernel(place_ref, g00, g01, g10, g11, left_ref, right_ref, send_a, keep_a, send_b, keep_b):
    rows = g00.shape[0]
    stack = jnp.concatenate([g01[...], g11[...], g00[...], g10[...]], axis=0)
    contract = (((1,), (1,)), ((), ()))
    left = lax.dot_general(stack, left_ref[...], contract, preferred_element_type=F32).astype(BF16)
    send_a[0] = left[:rows]
    send_a[1] = left[rows : 2 * rows]
    keep_a[0] = left[2 * rows : 3 * rows]
    keep_a[1] = left[3 * rows :]
    right = lax.dot_general(stack, right_ref[...], contract, preferred_element_type=F32).astype(BF16)
    send_b[0] = right[3 * rows :]
    send_b[1] = right[rows : 2 * rows]
    keep_b[0] = right[2 * rows : 3 * rows]
    keep_b[1] = right[:rows]


def run_weight(place, grad_full, gated, rows):
    chan, seq_len = gated.shape
    width = chan // 4
    grad_spec = lambda k: pl.BlockSpec((rows, seq_len), lambda n, place: (place[k], 0))
    gated_spec = lambda first: pl.BlockSpec((width, seq_len), lambda n, place: (n + first, 0))
    out_spec = pl.BlockSpec((2, rows, width), lambda n, place: (0, 0, n))
    return pl.pallas_call(
        weight_kernel,
        grid_spec=pltpu.PrefetchScalarGridSpec(
            num_scalar_prefetch=1,
            grid=(2,),
            in_specs=[grad_spec(k) for k in range(4)] + [gated_spec(0), gated_spec(2)],
            out_specs=[out_spec] * 4,
        ),
        out_shape=[jax.ShapeDtypeStruct((2, rows, chan // 2), BF16)] * 4,
        compiler_params=pltpu.CompilerParams(vmem_limit_bytes=48 * MIB),
        name="weight_kernel",
    )(place, grad_full, grad_full, grad_full, grad_full, gated, gated)


def product_kernel(count, place_ref, grad_hbm, *refs):
    pieces = refs[:count]
    mixed_ref, gate_ref, kv_ref, prior_ref, filt_ref, forward_ref, backward_ref = refs[count : count + 7]
    gate_grad_ref, kv_grad_ref, last_ref, head_ref, filt_grad_ref, conv, grad, sems = refs[-8:]
    step = pl.program_id(0)
    rows = pieces[0].shape[1]

    @pl.when(step == 0)
    def _():
        copies = [
            pltpu.make_async_copy(
                grad_hbm.at[pl.ds(pl.multiple_of(place_ref[k] * rows, rows), rows)],
                grad.at[pl.ds(k * rows, rows)],
                sems.at[k],
            )
            for k in range(count)
        ]
        for copy in copies:
            copy.start()
        for copy in copies:
            copy.wait()

    wide = [piece[...] for piece in pieces]
    total = jnp.dot(jnp.concatenate(wide, axis=1), grad[...], preferred_element_type=F32)
    gate_grad_ref[...] = total * mixed_ref[...].astype(F32)
    conv[...] = (total * gate_ref[...].astype(F32)).astype(BF16)

    group, taps = filt_ref.shape
    blocks = kv_ref.shape[1] // taps
    forward, backward = forward_ref[...], backward_ref[...]
    first, sign = lane_facts(taps)
    sign_imag = jnp.where(first, 1.0, sign)
    part = min(256, group)
    for at in range(0, group, part):
        chans = slice(at, at + part)
        h_real, h_last, h_imag = filter_spectrum(filt_ref[chans, :], forward, first)

        def pull_back(win_real, win_imag):
            return inverse(
                h_real * win_real + h_imag * win_imag, h_last * win_imag - h_imag * win_real, backward
            )

        past_real, past_imag = spectrum(prior_ref[chans, :], forward)
        g_real = g_imag = sum_real = sum_imag = 0.0
        for b in range(blocks):
            span = slice(b * taps, (b + 1) * taps)
            now_real, now_imag = spectrum(conv[chans, span], forward)
            back = pull_back(g_real + sign * now_real, g_imag + sign_imag * now_imag).astype(BF16)
            if b == 0:
                head_ref[chans, :] = back
            else:
                kv_grad_ref[chans, (b - 1) * taps : b * taps] = back
            x_real, x_imag = spectrum(kv_ref[chans, span], forward)
            win_real = x_real + sign * past_real
            win_imag = x_imag + sign_imag * past_imag
            win_last, win_skew = jnp.where(first, win_imag, win_real), jnp.where(first, 0.0, win_imag)
            sum_real = sum_real + now_real * win_real + now_imag * win_skew
            sum_imag = sum_imag + now_imag * win_last - now_real * win_skew
            g_real, g_imag = now_real, now_imag
            past_real, past_imag = x_real, x_imag
        last = pull_back(g_real, g_imag)
        last_ref[chans, :] = last
        kv_grad_ref[chans, (blocks - 1) * taps :] = last.astype(BF16)
        filt_grad_ref[chans, :] = inverse(sum_real, sum_imag, backward)


def run_product(part, place, grad_full, pieces, mixed, gate, kv, prior, filters, forward, backward, written):
    chan, seq_len = mixed.shape
    taps = filters.shape[1]
    depth = grad_full.shape[0]
    rows = pieces[0].shape[1]
    count = len(pieces)
    group = min(512, chan // 2)
    steps = chan // 2 // group
    offset = part * steps
    full = lambda width: pl.BlockSpec((group, width), lambda m, place: (m + offset, 0))
    local = pl.BlockSpec((group, rows), lambda m, place: (m, 0))
    whole = lambda array: pl.BlockSpec(array.shape, lambda m, place: (0, 0))
    anywhere = pl.BlockSpec(memory_space=pl.ANY)
    return pl.pallas_call(
        lambda *refs: product_kernel(count, *refs),
        grid_spec=pltpu.PrefetchScalarGridSpec(
            num_scalar_prefetch=1,
            grid=(steps,),
            in_specs=[anywhere]
            + [local if piece.shape[0] < chan else full(rows) for piece in pieces]
            + [full(seq_len), full(seq_len), full(seq_len), full(taps), full(taps)]
            + [whole(forward), whole(backward)]
            + [anywhere] * len(written),
            out_specs=[full(seq_len), full(seq_len), full(taps), full(taps), full(taps)],
            scratch_shapes=[
                pltpu.VMEM((group, seq_len), BF16),
                pltpu.VMEM((depth, seq_len), BF16),
                pltpu.SemaphoreType.DMA((count,)),
            ],
        ),
        out_shape=[
            jax.ShapeDtypeStruct((chan, seq_len), F32),
            jax.ShapeDtypeStruct((chan, seq_len), BF16),
            jax.ShapeDtypeStruct((chan, taps), F32),
            jax.ShapeDtypeStruct((chan, taps), BF16),
            jax.ShapeDtypeStruct((chan, taps), F32),
        ],
        input_output_aliases={9 + count + k: k for k in range(len(written))},
        compiler_params=pltpu.CompilerParams(vmem_limit_bytes=50 * MIB),
        name="product_kernel",
    )(place, grad_full, *pieces, mixed, gate, kv, prior, filters, forward, backward, *written)


def after(array, *earlier):
    return lax.optimization_barrier((array,) + earlier)[0] if earlier else array


class Layout:
    def __init__(self):
        self.count = lax.axis_size("ctx")
        self.depth = self.count // 4
        index = lax.axis_index("ctx")
        self.z, self.y, self.x = index // 4, (index // 2) % 2, index % 2
        self.pairs_x = [(i, i ^ 1) for i in range(self.count)]
        self.pairs_y = [(i, i ^ 2) for i in range(self.count)]

    def pairs_z(self, by):
        return [(i, (i + 4 * by) % self.count) for i in range(self.count)]

    def places(self, by):
        base = 4 * ((self.z + by) % self.depth)
        return [base + 2 * (self.y ^ dy) + (self.x ^ dx) for dy in range(2) for dx in range(2)]


class Stages:
    def __init__(self, at):
        self.at = at
        self.arrived = [(), ()]
        self.now = []
        self.ready = ()

    def advance(self):
        self.arrived.append(tuple(self.now))
        self.now, self.ready = [], ()

    def hold(self, array):
        return after(array, *self.arrived[-2])

    def computed(self, *arrays):
        self.ready += arrays

    def send(self, array, pairs, *earlier):
        got = lax.ppermute(after(array, *self.arrived[-2], *self.ready, *earlier), "ctx", pairs)
        self.now.append(got)
        return got

    def swap_x(self, array, *earlier):
        return self.send(array, self.at.pairs_x, *earlier)

    def swap_y(self, array, *earlier):
        return self.send(array, self.at.pairs_y, *earlier)


def pick(bit, array, axis):
    halves = [lax.index_in_dim(array, k, axis, keepdims=False) for k in range(2)]
    return jnp.where(bit == 0, halves[0], halves[1])


def gather_filters(at, own):
    def ordered(bit, mine, other):
        return jnp.stack([jnp.where(bit == 0, mine, other), jnp.where(bit == 0, other, mine)])

    from_x = lax.ppermute(own, "ctx", at.pairs_x)
    pair = ordered(at.x, own, from_x)
    from_y = lax.ppermute(pair, "ctx", at.pairs_y)
    plane = ordered(at.y, pair, from_y)
    slots = [lax.ppermute(plane, "ctx", at.pairs_z(by)) for by in range(at.depth - 1, 0, -1)]
    ring = jnp.stack((slots + [plane]) * 2)
    whole = lax.dynamic_slice_in_dim(ring, at.depth - 1 - at.z, at.depth, axis=0)
    whole = whole.reshape((at.count * own.shape[0],) + own.shape[1:])
    return whole, from_x, from_y, slots


def reduce_filters(at, part, chan_count):
    taps = part.shape[1]
    part = part.reshape(at.depth, 2, 2, chan_count, taps)
    part = pick(at.x, part, 2) + lax.ppermute(pick(1 - at.x, part, 2), "ctx", at.pairs_x)
    part = pick(at.y, part, 1) + lax.ppermute(pick(1 - at.y, part, 1), "ctx", at.pairs_y)
    at_z = lambda by: lax.dynamic_index_in_dim(part, (at.z + by) % at.depth, 0, keepdims=False)
    total = at_z(0)
    for by in range(1, at.depth):
        total = total + lax.ppermute(at_z(by), "ctx", at.pairs_z(by))
    return total


def on_device(out_grad, gate_values, kv_product, w_out, filters):
    at = Layout()
    stages = Stages(at)
    chan_count = filters.shape[2]
    taps = filters.shape[3]
    seq_len = out_grad.shape[1]
    rows, chan = w_out.shape
    half = chan // 2
    norm_scale = 1.0 / math.sqrt(at.count * seq_len)
    to_right = [(i, i + 1) for i in range(at.count - 1)]
    to_left = [(i + 1, i) for i in range(at.count - 1)]
    forward, backward = (jnp.asarray(m) for m in dft_matrices(taps))

    prior = lax.ppermute(kv_product[:, seq_len - taps :], "ctx", to_right)
    all_filters, first_x, first_y, first_z = gather_filters(at, filters.reshape(chan_count, taps))
    grad_full = lax.all_gather(out_grad, "fsdp", axis=0, tiled=True)

    near = sorted(range(at.depth), key=lambda d: min(d, at.depth - d))
    far = near[::-1]
    own = w_out.T
    shards = [own]
    for by in near[1:]:
        before = first_z if len(shards) == 1 else shards[-1:]
        shards.append(lax.ppermute(after(own, *before), "ctx", at.pairs_z(by)))
    from_x, from_y, diag_a, diag_b = {}, {}, {}, {}
    kept, summed = {}, {}

    def gather_first(k, *earlier):
        from_x[k] = stages.swap_x(shards[k], *earlier)
        from_y[k] = stages.swap_y(shards[k], *earlier)

    def gather_second(k):
        diag_a[k] = stages.swap_x(from_y[k][:half])
        diag_b[k] = stages.swap_y(from_x[k][half:])

    def weight_part(k):
        place = jnp.stack(at.places(far[k])).astype(jnp.int32)
        kept[k] = run_weight(place, grad_full, stages.hold(gated), rows)
        stages.computed(kept[k][0])

    def reduce_first(k):
        send_a, keep_a, send_b, keep_b = kept[k]
        kept[k] = (keep_a, stages.swap_x(send_a), keep_b, stages.swap_y(send_b))

    def reduce_second(k):
        keep_a, got_a, keep_b, got_b = kept[k]
        next_a = (keep_a[1].astype(F32) + got_a[1].astype(F32)).astype(BF16)
        next_b = (keep_b[1].astype(F32) + got_b[1].astype(F32)).astype(BF16)
        kept[k] = (keep_a, got_a, stages.swap_y(next_a), keep_b, got_b, stages.swap_x(next_b))

    def reduce_third(k):
        keep_a, got_a, last_a, keep_b, got_b, last_b = kept.pop(k)
        sum_a = keep_a[0].astype(F32) + got_a[0].astype(F32) + last_a.astype(F32)
        sum_b = keep_b[0].astype(F32) + got_b[0].astype(F32) + last_b.astype(F32)
        joint = jnp.concatenate([sum_a, sum_b], axis=1)
        by = far[k]
        summed[k] = joint if by == 0 else lax.ppermute(joint.astype(BF16), "ctx", at.pairs_z(by))

    mixed = gated = place = products = None

    def mix():
        nonlocal mixed, gated
        mixed, gated = run_mix(all_filters, stages.hold(kv_product), prior, gate_values, forward, backward)
        stages.computed(mixed)

    def product(part):
        nonlocal products
        diag = (diag_a, diag_b)[part]
        pieces = [p for k in range(at.depth) for p in (shards[k], from_x[k], from_y[k], diag[k])]
        places = jnp.stack([c for by in near for c in at.places(-by)]).astype(jnp.int32)
        products = run_product(
            part, places, grad_full, pieces, stages.hold(mixed), gate_values, kv_product, prior,
            all_filters, forward, backward, products or (),
        )
        stages.computed(products[3])

    depth = at.depth
    plan = {}
    for k in range(depth):
        plan.setdefault(k, []).append((gather_first, k))
        plan.setdefault(k + 2, []).append((gather_second, k))
        plan.setdefault(k + depth, []).append((reduce_first, k))
        plan.setdefault(k + depth + 2, []).append((reduce_second, k))
    for stage in range(2 * depth + 4):
        if stage == 2:
            mix()
        for k in range(depth):
            if stage == max(3, k + depth - 1):
                weight_part(k)
            if stage == k + depth + 4:
                reduce_third(k)
        if stage in (depth + 3, depth + 4):
            product(stage - depth - 3)
        for action, k in plan.get(stage, []):
            if action is gather_first and k == 0:
                gather_first(0, first_x, first_y)
            else:
                action(k)
        stages.advance()

    total = summed[depth - 1]
    for k in range(depth - 1):
        total = total + summed[k].astype(F32)
    w_grad = total * norm_scale

    gate_grad, kv_grad, last, head, filt_part = products
    tail = lax.ppermute(head, "ctx", to_left)
    kv_grad = lax.dynamic_update_slice(
        kv_grad, (last + tail.astype(F32)).astype(BF16), (0, seq_len - taps)
    )
    filter_grad = reduce_filters(at, filt_part, chan_count) * norm_scale
    return (gate_grad, kv_grad, filter_grad.reshape(filters.shape), w_grad)


def solution(mesh):
    in_specs = (
        P("fsdp", "ctx"),
        P("fsdp", "ctx"),
        P("fsdp", "ctx"),
        P("ctx", "fsdp"),
        P("fsdp", "ctx", None, None),
    )
    out_specs = (P("fsdp", "ctx"), P("fsdp", "ctx"), P("fsdp", "ctx", None, None), P("ctx", "fsdp"))
    return jax.shard_map(
        on_device, mesh=mesh, in_specs=in_specs, out_specs=out_specs, check_vma=False
    )
```

```python
import math

import jax
import jax.numpy as jnp
import ml_dtypes
import numpy as np
from jax import lax
from jax.experimental import pallas as pl
from jax.experimental.pallas import tpu as pltpu
from jax.sharding import PartitionSpec as P

F32 = jnp.float32
BF16 = jnp.bfloat16
MIB = 1024 * 1024
PARTS = 2


def split_pair(matrix):
    high = matrix.astype(ml_dtypes.bfloat16)
    low = (matrix - high.astype(np.float64)).astype(ml_dtypes.bfloat16)
    return high, low


def dft_matrices(taps):
    points = 2 * taps
    place = np.arange(taps)
    angle = 2.0 * np.pi * ((place[:, None] * place[None, :]) % points) / points
    turn = (-1.0) ** place
    forward = np.concatenate([np.cos(angle), -np.sin(angle)], axis=1)
    forward[:, taps] = turn
    weight = np.full((taps, 1), 2.0 / points)
    weight[0] = 1.0 / points
    backward = np.concatenate([weight * np.cos(angle), -weight * np.sin(angle)], axis=0)
    backward[taps, :] = turn / points
    forward = np.concatenate(split_pair(forward), axis=0)
    backward = np.concatenate(split_pair(backward), axis=1)
    return forward, backward


def spectrum(block, forward):
    taps = block.shape[1]
    both = jnp.dot(jnp.concatenate([block, block], axis=1), forward, preferred_element_type=F32)
    return both[:, :taps], both[:, taps:]


def inverse(real, imag, backward):
    taps = real.shape[1]
    whole = jnp.concatenate([real, imag], axis=1)
    high = whole.astype(BF16)
    low = (whole - high.astype(F32)).astype(BF16)
    both = jnp.dot(high, backward, preferred_element_type=F32)
    rest = jnp.dot(low, backward[:, :taps], preferred_element_type=F32)
    return both[:, :taps] + both[:, taps:] + rest


def lane_facts(taps):
    lane = lax.broadcasted_iota(jnp.int32, (1, taps), 1)
    sign = jnp.where(lane % 2 == 0, 1.0, -1.0)
    return lane == 0, sign


def filter_spectrum(filt, forward, first):
    real, imag = spectrum(filt, forward)
    return real, jnp.where(first, imag, real), jnp.where(first, 0.0, imag)


def mix_kernel(filt_ref, kv_ref, prior_ref, gate_ref, forward_ref, backward_ref, mixed_ref, gated_ref):
    taps = filt_ref.shape[1]
    blocks = kv_ref.shape[1] // taps
    forward, backward = forward_ref[...], backward_ref[...]
    first, sign = lane_facts(taps)
    sign_imag = jnp.where(first, 1.0, sign)
    h_real, h_last, h_imag = filter_spectrum(filt_ref[...], forward, first)
    prev_real, prev_imag = spectrum(prior_ref[...], forward)
    for b in range(blocks):
        span = slice(b * taps, (b + 1) * taps)
        real, imag = spectrum(kv_ref[:, span], forward)
        win_real = real + sign * prev_real
        win_imag = imag + sign_imag * prev_imag
        mixed = inverse(
            h_real * win_real - h_imag * win_imag, h_last * win_imag + h_imag * win_real, backward
        ).astype(BF16)
        mixed_ref[:, span] = mixed
        gated_ref[:, span] = (gate_ref[:, span].astype(F32) * mixed.astype(F32)).astype(BF16)
        prev_real, prev_imag = real, imag


def run_mix(filters, kv, prior, gate, forward, backward):
    chan, seq_len = kv.shape
    taps = filters.shape[1]
    group = min(256, chan)
    rows = lambda width: pl.BlockSpec((group, width), lambda g: (g, 0))
    whole = lambda array: pl.BlockSpec(array.shape, lambda g: (0, 0))
    return pl.pallas_call(
        mix_kernel,
        grid=(chan // group,),
        in_specs=[rows(taps), rows(seq_len), rows(taps), rows(seq_len), whole(forward), whole(backward)],
        out_specs=[rows(seq_len), rows(seq_len)],
        out_shape=[jax.ShapeDtypeStruct((chan, seq_len), BF16)] * 2,
        compiler_params=pltpu.CompilerParams(vmem_limit_bytes=32 * MIB),
        cost_estimate=pl.CostEstimate(
            flops=14 * chan * seq_len * 2 * taps, bytes_accessed=8 * chan * seq_len, transcendentals=0
        ),
        name="mix_kernel",
    )(filters, kv, prior, gate, forward, backward)


def weight_kernel(place_ref, g00, g01, g10, g11, left_ref, right_ref, send_a, keep_a, send_b, keep_b):
    rows = g00.shape[0]
    stack = jnp.concatenate([g01[...], g11[...], g00[...], g10[...]], axis=0)
    contract = (((1,), (1,)), ((), ()))
    left = lax.dot_general(stack, left_ref[...], contract, preferred_element_type=F32).astype(BF16)
    send_a[0] = left[:rows]
    send_a[1] = left[rows : 2 * rows]
    keep_a[0] = left[2 * rows : 3 * rows]
    keep_a[1] = left[3 * rows :]
    right = lax.dot_general(stack, right_ref[...], contract, preferred_element_type=F32).astype(BF16)
    send_b[0] = right[3 * rows :]
    send_b[1] = right[rows : 2 * rows]
    keep_b[0] = right[2 * rows : 3 * rows]
    keep_b[1] = right[:rows]


def run_weight(place, grad_full, gated, rows):
    chan, seq_len = gated.shape
    width = chan // 4
    grad_spec = lambda k: pl.BlockSpec((rows, seq_len), lambda n, place: (place[k], 0))
    gated_spec = lambda first: pl.BlockSpec((width, seq_len), lambda n, place: (n + first, 0))
    out_spec = pl.BlockSpec((2, rows, width), lambda n, place: (0, 0, n))
    return pl.pallas_call(
        weight_kernel,
        grid_spec=pltpu.PrefetchScalarGridSpec(
            num_scalar_prefetch=1,
            grid=(2,),
            in_specs=[grad_spec(k) for k in range(4)] + [gated_spec(0), gated_spec(2)],
            out_specs=[out_spec] * 4,
        ),
        out_shape=[jax.ShapeDtypeStruct((2, rows, chan // 2), BF16)] * 4,
        compiler_params=pltpu.CompilerParams(vmem_limit_bytes=48 * MIB),
        cost_estimate=pl.CostEstimate(
            flops=8 * rows * chan * seq_len,
            bytes_accessed=2 * (4 * rows * (seq_len + chan) + chan * seq_len),
            transcendentals=0,
        ),
        name="weight_kernel",
    )(place, grad_full, grad_full, grad_full, grad_full, gated, gated)


def product_kernel(count, place_ref, grad_hbm, *refs):
    pieces = refs[:count]
    mixed_ref, gate_ref, kv_ref, prior_ref, filt_ref, forward_ref, backward_ref = refs[count : count + 7]
    gate_grad_ref, kv_grad_ref, last_ref, head_ref, filt_grad_ref, conv, grad, sems = refs[-8:]
    step = pl.program_id(0)
    rows = pieces[0].shape[1]

    @pl.when(step == 0)
    def _():
        copies = [
            pltpu.make_async_copy(
                grad_hbm.at[pl.ds(pl.multiple_of(place_ref[k] * rows, rows), rows)],
                grad.at[pl.ds(k * rows, rows)],
                sems.at[k],
            )
            for k in range(count)
        ]
        for copy in copies:
            copy.start()
        for copy in copies:
            copy.wait()

    wide = [piece[...] for piece in pieces]
    total = jnp.dot(jnp.concatenate(wide, axis=1), grad[...], preferred_element_type=F32)
    gate_grad_ref[...] = total * mixed_ref[...].astype(F32)
    conv[...] = (total * gate_ref[...].astype(F32)).astype(BF16)

    group, taps = filt_ref.shape
    blocks = kv_ref.shape[1] // taps
    forward, backward = forward_ref[...], backward_ref[...]
    first, sign = lane_facts(taps)
    sign_imag = jnp.where(first, 1.0, sign)
    part = min(256, group)
    for at in range(0, group, part):
        chans = slice(at, at + part)
        h_real, h_last, h_imag = filter_spectrum(filt_ref[chans, :], forward, first)

        def pull_back(win_real, win_imag):
            return inverse(
                h_real * win_real + h_imag * win_imag, h_last * win_imag - h_imag * win_real, backward
            )

        past_real, past_imag = spectrum(prior_ref[chans, :], forward)
        g_real = g_imag = sum_real = sum_imag = 0.0
        for b in range(blocks):
            span = slice(b * taps, (b + 1) * taps)
            now_real, now_imag = spectrum(conv[chans, span], forward)
            back = pull_back(g_real + sign * now_real, g_imag + sign_imag * now_imag).astype(BF16)
            if b == 0:
                head_ref[chans, :] = back
            else:
                kv_grad_ref[chans, (b - 1) * taps : b * taps] = back
            x_real, x_imag = spectrum(kv_ref[chans, span], forward)
            win_real = x_real + sign * past_real
            win_imag = x_imag + sign_imag * past_imag
            win_last, win_skew = jnp.where(first, win_imag, win_real), jnp.where(first, 0.0, win_imag)
            sum_real = sum_real + now_real * win_real + now_imag * win_skew
            sum_imag = sum_imag + now_imag * win_last - now_real * win_skew
            g_real, g_imag = now_real, now_imag
            past_real, past_imag = x_real, x_imag
        last = pull_back(g_real, g_imag)
        last_ref[chans, :] = last
        kv_grad_ref[chans, (blocks - 1) * taps :] = last.astype(BF16)
        filt_grad_ref[chans, :] = inverse(sum_real, sum_imag, backward)


def run_product(part, place, grad_full, pieces, mixed, gate, kv, prior, filters, forward, backward, written):
    chan, seq_len = mixed.shape
    taps = filters.shape[1]
    depth = grad_full.shape[0]
    rows = pieces[0].shape[1]
    count = len(pieces)
    group = min(512, chan // PARTS)
    steps = chan // PARTS // group
    offset = part * steps
    local_offset = offset % (chan // 2 // group)
    full = lambda width: pl.BlockSpec((group, width), lambda m, place: (m + offset, 0))
    local = pl.BlockSpec((group, rows), lambda m, place: (m + local_offset, 0))
    whole = lambda array: pl.BlockSpec(array.shape, lambda m, place: (0, 0))
    anywhere = pl.BlockSpec(memory_space=pl.ANY)
    return pl.pallas_call(
        lambda *refs: product_kernel(count, *refs),
        grid_spec=pltpu.PrefetchScalarGridSpec(
            num_scalar_prefetch=1,
            grid=(steps,),
            in_specs=[anywhere]
            + [local if piece.shape[0] < chan else full(rows) for piece in pieces]
            + [full(seq_len), full(seq_len), full(seq_len), full(taps), full(taps)]
            + [whole(forward), whole(backward)]
            + [anywhere] * len(written),
            out_specs=[full(seq_len), full(seq_len), full(taps), full(taps), full(taps)],
            scratch_shapes=[
                pltpu.VMEM((group, seq_len), BF16),
                pltpu.VMEM((depth, seq_len), BF16),
                pltpu.SemaphoreType.DMA((count,)),
            ],
        ),
        out_shape=[
            jax.ShapeDtypeStruct((chan, seq_len), F32),
            jax.ShapeDtypeStruct((chan, seq_len), BF16),
            jax.ShapeDtypeStruct((chan, taps), F32),
            jax.ShapeDtypeStruct((chan, taps), BF16),
            jax.ShapeDtypeStruct((chan, taps), F32),
        ],
        input_output_aliases={9 + count + k: k for k in range(len(written))},
        compiler_params=pltpu.CompilerParams(vmem_limit_bytes=50 * MIB),
        cost_estimate=pl.CostEstimate(
            flops=group * steps * seq_len * (2 * depth + 32 * taps),
            bytes_accessed=2 * depth * (seq_len + group * steps) + 12 * group * steps * seq_len,
            transcendentals=0,
        ),
        name="product_kernel",
    )(place, grad_full, *pieces, mixed, gate, kv, prior, filters, forward, backward, *written)


def after(array, *earlier):
    return lax.optimization_barrier((array,) + earlier)[0] if earlier else array


class Layout:
    def __init__(self):
        self.count = lax.axis_size("ctx")
        self.depth = self.count // 4
        index = lax.axis_index("ctx")
        self.z, self.y, self.x = index // 4, (index // 2) % 2, index % 2
        self.pairs_x = [(i, i ^ 1) for i in range(self.count)]
        self.pairs_y = [(i, i ^ 2) for i in range(self.count)]

    def pairs_z(self, by):
        return [(i, (i + 4 * by) % self.count) for i in range(self.count)]

    def places(self, by):
        base = 4 * ((self.z + by) % self.depth)
        return [base + 2 * (self.y ^ dy) + (self.x ^ dx) for dy in range(2) for dx in range(2)]


class Stages:
    def __init__(self, at):
        self.at = at
        self.arrived = [()] * 3
        self.now = []
        self.ready = self.next_ready = ()

    def advance(self):
        self.arrived.append(tuple(self.now))
        self.now, self.ready, self.next_ready = [], self.next_ready, ()

    def hold(self, array):
        return after(array, *self.arrived[-2])

    def finished(self, *arrays):
        self.next_ready += arrays

    def send(self, array, pairs, *earlier):
        got = lax.ppermute(after(array, *self.arrived[-2], *self.ready, *earlier), "ctx", pairs)
        self.now.append(got)
        return got

    def swap_x(self, array, *earlier):
        return self.send(array, self.at.pairs_x, *earlier)

    def swap_y(self, array, *earlier):
        return self.send(array, self.at.pairs_y, *earlier)


def pick(bit, array, axis):
    halves = [lax.index_in_dim(array, k, axis, keepdims=False) for k in range(2)]
    return jnp.where(bit == 0, halves[0], halves[1])


def gather_filters(at, own):
    def ordered(bit, mine, other):
        return jnp.stack([jnp.where(bit == 0, mine, other), jnp.where(bit == 0, other, mine)], axis=1)

    slots = [lax.ppermute(own, "ctx", at.pairs_z(by)) for by in range(at.depth - 1, 0, -1)]
    ring = jnp.stack((slots + [own]) * 2)
    column = lax.dynamic_slice_in_dim(ring, at.depth - 1 - at.z, at.depth, axis=0)
    from_x = lax.ppermute(column, "ctx", at.pairs_x)
    pair = ordered(at.x, column, from_x)
    from_y = lax.ppermute(pair, "ctx", at.pairs_y)
    whole = ordered(at.y, pair, from_y).reshape((at.count * own.shape[0],) + own.shape[1:])
    return whole, from_x, from_y


def reduce_filters(at, part, chan_count):
    taps = part.shape[1]
    part = part.reshape(at.depth, 2, 2, chan_count, taps)
    part = pick(at.x, part, 2) + lax.ppermute(pick(1 - at.x, part, 2), "ctx", at.pairs_x)
    part = pick(at.y, part, 1) + lax.ppermute(pick(1 - at.y, part, 1), "ctx", at.pairs_y)
    at_z = lambda by: lax.dynamic_index_in_dim(part, (at.z + by) % at.depth, 0, keepdims=False)
    total = at_z(0)
    for by in range(1, at.depth):
        total = total + lax.ppermute(at_z(by), "ctx", at.pairs_z(by))
    return total


def on_device(out_grad, gate_values, kv_product, w_out, filters):
    at = Layout()
    stages = Stages(at)
    chan_count = filters.shape[2]
    taps = filters.shape[3]
    seq_len = out_grad.shape[1]
    rows, chan = w_out.shape
    half = chan // 2
    norm_scale = 1.0 / math.sqrt(at.count * seq_len)
    to_right = [(i, i + 1) for i in range(at.count - 1)]
    to_left = [(i + 1, i) for i in range(at.count - 1)]
    forward, backward = (jnp.asarray(m) for m in dft_matrices(taps))

    prior = lax.ppermute(kv_product[:, seq_len - taps :], "ctx", to_right)
    all_filters, first_x, first_y = gather_filters(at, filters.reshape(chan_count, taps))
    grad_full = lax.all_gather(out_grad, "fsdp", axis=0, tiled=True)

    near = sorted(range(at.depth), key=lambda d: min(d, at.depth - d))
    far = near[::-1]
    own = w_out.T
    shards = [own]
    for by in near[1:]:
        shards.append(lax.ppermute(after(own, *shards[1:][-1:]), "ctx", at.pairs_z(by)))
    from_x, from_y, diag_a, diag_b = {}, {}, {}, {}
    kept, summed = {}, {}

    def gather_first(k):
        earlier = {1: (from_x.get(0), from_y.get(0)), 2: (first_x,), 3: (first_y,)}.get(k, ())
        from_x[k] = stages.swap_x(shards[k], *earlier)
        from_y[k] = stages.swap_y(shards[k], *earlier)

    def gather_second(k):
        diag_a[k] = stages.swap_x(from_y[k][:half])
        diag_b[k] = stages.swap_y(from_x[k][half:])

    def weight_part(k):
        place = jnp.stack(at.places(far[k])).astype(jnp.int32)
        kept[k] = run_weight(place, grad_full, stages.hold(gated), rows)

    def reduce_first(k):
        send_a, keep_a, send_b, keep_b = kept[k]
        kept[k] = (keep_a, stages.swap_x(send_a), keep_b, stages.swap_y(send_b))

    def reduce_second(k):
        keep_a, got_a, keep_b, got_b = kept[k]
        next_a = (keep_a[1].astype(F32) + got_a[1].astype(F32)).astype(BF16)
        next_b = (keep_b[1].astype(F32) + got_b[1].astype(F32)).astype(BF16)
        kept[k] = (keep_a, got_a, stages.swap_y(next_a), keep_b, got_b, stages.swap_x(next_b))

    def reduce_third(k):
        keep_a, got_a, last_a, keep_b, got_b, last_b = kept.pop(k)
        sum_a = keep_a[0].astype(F32) + got_a[0].astype(F32) + last_a.astype(F32)
        sum_b = keep_b[0].astype(F32) + got_b[0].astype(F32) + last_b.astype(F32)
        joint = jnp.concatenate([sum_a, sum_b], axis=1)
        by = far[k]
        summed[k] = joint if by == 0 else lax.ppermute(joint.astype(BF16), "ctx", at.pairs_z(by))

    mixed = gated = place = products = None

    def mix():
        nonlocal mixed, gated
        mixed, gated = run_mix(all_filters, stages.hold(kv_product), prior, gate_values, forward, backward)

    def product(part):
        nonlocal products
        diag = diag_a if 2 * part < PARTS else diag_b
        pieces = [p for k in range(at.depth) for p in (shards[k], from_x[k], from_y[k], diag[k])]
        places = jnp.stack([c for by in near for c in at.places(-by)]).astype(jnp.int32)
        products = run_product(
            part, places, grad_full, pieces, stages.hold(mixed), gate_values, kv_product, prior,
            all_filters, forward, backward, products or (),
        )
        stages.finished(products[3])

    depth = at.depth
    plan = {}
    for k in range(depth):
        plan.setdefault(k, []).append((gather_first, k))
        plan.setdefault(k + 2, []).append((gather_second, k))
        plan.setdefault(k + depth, []).append((reduce_first, k))
        plan.setdefault(k + depth + 2, []).append((reduce_second, k))
    for stage in range(max(2 * depth + 4, depth + 3 + PARTS)):
        if stage == 2:
            mix()
        for k in range(depth):
            if stage == max(3, k + depth - 1 + 0):
                weight_part(k)
            if stage == k + depth + 4:
                reduce_third(k)
        for part in range(PARTS):
            if stage == depth + 3 + part:
                product(part)
        for action, k in plan.get(stage, []):
            action(k)
        stages.advance()

    total = summed[depth - 1]
    for k in range(depth - 1):
        total = total + summed[k].astype(F32)
    w_grad = total * norm_scale

    gate_grad, kv_grad, last, head, filt_part = products
    tail = lax.ppermute(head, "ctx", to_left)
    kv_grad = lax.dynamic_update_slice(
        kv_grad, (last + tail.astype(F32)).astype(BF16), (0, seq_len - taps)
    )
    filter_grad = reduce_filters(at, filt_part, chan_count) * norm_scale
    return (gate_grad, kv_grad, filter_grad.reshape(filters.shape), w_grad)


def solution(mesh):
    in_specs = (
        P("fsdp", "ctx"),
        P("fsdp", "ctx"),
        P("fsdp", "ctx"),
        P("ctx", "fsdp"),
        P("fsdp", "ctx", None, None),
    )
    out_specs = (P("fsdp", "ctx"), P("fsdp", "ctx"), P("fsdp", "ctx", None, None), P("ctx", "fsdp"))
    return jax.shard_map(
        on_device, mesh=mesh, in_specs=in_specs, out_specs=out_specs, check_vma=False
    )
```

```python
import math

import jax
import jax.numpy as jnp
import ml_dtypes
import numpy as np
from jax import lax
from jax.experimental import pallas as pl
from jax.experimental.pallas import tpu as pltpu
from jax.sharding import PartitionSpec as P

F32 = jnp.float32
BF16 = jnp.bfloat16
VMEM = 58 * 1024 * 1024
PARTS = 2


def split_pair(matrix):
    high = matrix.astype(ml_dtypes.bfloat16)
    low = (matrix - high.astype(np.float64)).astype(ml_dtypes.bfloat16)
    return high, low


def dft_matrices(taps):
    points = 2 * taps
    place = np.arange(taps)
    angle = 2.0 * np.pi * ((place[:, None] * place[None, :]) % points) / points
    turn = (-1.0) ** place
    forward = np.concatenate([np.cos(angle), -np.sin(angle)], axis=1)
    forward[:, taps] = turn
    weight = np.full((taps, 1), 2.0 / points)
    weight[0] = 1.0 / points
    backward = np.concatenate([weight * np.cos(angle), -weight * np.sin(angle)], axis=0)
    backward[taps, :] = turn / points
    forward = np.concatenate(split_pair(forward), axis=0)
    backward = np.concatenate(split_pair(backward), axis=1)
    return forward, backward


def spectrum(block, forward):
    taps = block.shape[1]
    both = jnp.dot(jnp.concatenate([block, block], axis=1), forward, preferred_element_type=F32)
    return both[:, :taps], both[:, taps:]


def inverse(real, imag, backward):
    taps = real.shape[1]
    whole = jnp.concatenate([real, imag], axis=1)
    high = whole.astype(BF16)
    low = (whole - high.astype(F32)).astype(BF16)
    both = jnp.dot(high, backward, preferred_element_type=F32)
    rest = jnp.dot(low, backward[:, :taps], preferred_element_type=F32)
    return both[:, :taps] + both[:, taps:] + rest


def lane_facts(taps):
    lane = lax.broadcasted_iota(jnp.int32, (1, taps), 1)
    sign = jnp.where(lane % 2 == 0, 1.0, -1.0)
    return lane == 0, sign


def filter_spectrum(filt, forward, first):
    real, imag = spectrum(filt, forward)
    return real, jnp.where(first, imag, real), jnp.where(first, 0.0, imag)


def mix_kernel(filt_ref, kv_ref, prior_ref, gate_ref, forward_ref, backward_ref, mixed_ref, gated_ref):
    taps = filt_ref.shape[1]
    blocks = kv_ref.shape[1] // taps
    forward, backward = forward_ref[...], backward_ref[...]
    first, sign = lane_facts(taps)
    sign_imag = jnp.where(first, 1.0, sign)
    h_real, h_last, h_imag = filter_spectrum(filt_ref[...], forward, first)
    prev_real, prev_imag = spectrum(prior_ref[...], forward)
    for b in range(blocks):
        span = slice(b * taps, (b + 1) * taps)
        real, imag = spectrum(kv_ref[:, span], forward)
        win_real = real + sign * prev_real
        win_imag = imag + sign_imag * prev_imag
        mixed = inverse(
            h_real * win_real - h_imag * win_imag, h_last * win_imag + h_imag * win_real, backward
        ).astype(BF16)
        mixed_ref[:, span] = mixed
        gated_ref[:, span] = (gate_ref[:, span].astype(F32) * mixed.astype(F32)).astype(BF16)
        prev_real, prev_imag = real, imag


def run_mix(filters, kv, prior, gate, forward, backward):
    chan, seq_len = kv.shape
    taps = filters.shape[1]
    group = min(256, chan)
    rows = lambda width: pl.BlockSpec((group, width), lambda g: (g, 0))
    whole = lambda array: pl.BlockSpec(array.shape, lambda g: (0, 0))
    return pl.pallas_call(
        mix_kernel,
        grid=(chan // group,),
        in_specs=[rows(taps), rows(seq_len), rows(taps), rows(seq_len), whole(forward), whole(backward)],
        out_specs=[rows(seq_len), rows(seq_len)],
        out_shape=[jax.ShapeDtypeStruct((chan, seq_len), BF16)] * 2,
        compiler_params=pltpu.CompilerParams(vmem_limit_bytes=VMEM),
        cost_estimate=pl.CostEstimate(
            flops=14 * chan * seq_len * 2 * taps, bytes_accessed=8 * chan * seq_len, transcendentals=0
        ),
        name="mix_kernel",
    )(filters, kv, prior, gate, forward, backward)


def weight_kernel(place_ref, g00, g01, g10, g11, left_ref, right_ref, send_a, keep_a, send_b, keep_b):
    rows = g00.shape[0]
    stack = jnp.concatenate([g01[...], g11[...], g00[...], g10[...]], axis=0)
    contract = (((1,), (1,)), ((), ()))
    left = lax.dot_general(stack, left_ref[...], contract, preferred_element_type=F32).astype(BF16)
    send_a[0] = left[:rows]
    send_a[1] = left[rows : 2 * rows]
    keep_a[0] = left[2 * rows : 3 * rows]
    keep_a[1] = left[3 * rows :]
    right = lax.dot_general(stack, right_ref[...], contract, preferred_element_type=F32).astype(BF16)
    send_b[0] = right[3 * rows :]
    send_b[1] = right[rows : 2 * rows]
    keep_b[0] = right[2 * rows : 3 * rows]
    keep_b[1] = right[:rows]


def run_weight(place, grad_full, gated, rows):
    chan, seq_len = gated.shape
    width = chan // 4
    grad_spec = lambda k: pl.BlockSpec((rows, seq_len), lambda n, place: (place[k], 0))
    gated_spec = lambda first: pl.BlockSpec((width, seq_len), lambda n, place: (n + first, 0))
    out_spec = pl.BlockSpec((2, rows, width), lambda n, place: (0, 0, n))
    return pl.pallas_call(
        weight_kernel,
        grid_spec=pltpu.PrefetchScalarGridSpec(
            num_scalar_prefetch=1,
            grid=(2,),
            in_specs=[grad_spec(k) for k in range(4)] + [gated_spec(0), gated_spec(2)],
            out_specs=[out_spec] * 4,
        ),
        out_shape=[jax.ShapeDtypeStruct((2, rows, chan // 2), BF16)] * 4,
        compiler_params=pltpu.CompilerParams(vmem_limit_bytes=VMEM),
        cost_estimate=pl.CostEstimate(
            flops=8 * rows * chan * seq_len,
            bytes_accessed=2 * (4 * rows * (seq_len + chan) + chan * seq_len),
            transcendentals=0,
        ),
        name="weight_kernel",
    )(place, grad_full, grad_full, grad_full, grad_full, gated, gated)


def product_kernel(count, place_ref, grad_hbm, *refs):
    pieces = refs[:count]
    mixed_ref, gate_ref, kv_ref, prior_ref, filt_ref, forward_ref, backward_ref = refs[count : count + 7]
    gate_grad_ref, kv_grad_ref, last_ref, head_ref, filt_grad_ref, conv, grad, sems = refs[-8:]
    step = pl.program_id(0)
    rows = pieces[0].shape[1]

    @pl.when(step == 0)
    def _():
        copies = [
            pltpu.make_async_copy(
                grad_hbm.at[pl.ds(pl.multiple_of(place_ref[k] * rows, rows), rows)],
                grad.at[pl.ds(k * rows, rows)],
                sems.at[k],
            )
            for k in range(count)
        ]
        for copy in copies:
            copy.start()
        for copy in copies:
            copy.wait()

    wide = [piece[...] for piece in pieces]
    total = jnp.dot(jnp.concatenate(wide, axis=1), grad[...], preferred_element_type=F32)
    gate_grad_ref[...] = total * mixed_ref[...].astype(F32)
    conv[...] = (total * gate_ref[...].astype(F32)).astype(BF16)

    group, taps = filt_ref.shape
    blocks = kv_ref.shape[1] // taps
    forward, backward = forward_ref[...], backward_ref[...]
    first, sign = lane_facts(taps)
    sign_imag = jnp.where(first, 1.0, sign)
    part = min(256, group)
    for at in range(0, group, part):
        chans = slice(at, at + part)
        h_real, h_last, h_imag = filter_spectrum(filt_ref[chans, :], forward, first)

        def pull_back(win_real, win_imag):
            return inverse(
                h_real * win_real + h_imag * win_imag, h_last * win_imag - h_imag * win_real, backward
            )

        past_real, past_imag = spectrum(prior_ref[chans, :], forward)
        g_real = g_imag = sum_real = sum_imag = 0.0
        for b in range(blocks):
            span = slice(b * taps, (b + 1) * taps)
            now_real, now_imag = spectrum(conv[chans, span], forward)
            back = pull_back(g_real + sign * now_real, g_imag + sign_imag * now_imag).astype(BF16)
            if b == 0:
                head_ref[chans, :] = back
            else:
                kv_grad_ref[chans, (b - 1) * taps : b * taps] = back
            x_real, x_imag = spectrum(kv_ref[chans, span], forward)
            win_real = x_real + sign * past_real
            win_imag = x_imag + sign_imag * past_imag
            win_last, win_skew = jnp.where(first, win_imag, win_real), jnp.where(first, 0.0, win_imag)
            sum_real = sum_real + now_real * win_real + now_imag * win_skew
            sum_imag = sum_imag + now_imag * win_last - now_real * win_skew
            g_real, g_imag = now_real, now_imag
            past_real, past_imag = x_real, x_imag
        last = pull_back(g_real, g_imag)
        last_ref[chans, :] = last
        kv_grad_ref[chans, (blocks - 1) * taps :] = last.astype(BF16)
        filt_grad_ref[chans, :] = inverse(sum_real, sum_imag, backward)


def run_product(part, place, grad_full, pieces, mixed, gate, kv, prior, filters, forward, backward, written):
    chan, seq_len = mixed.shape
    taps = filters.shape[1]
    depth = grad_full.shape[0]
    rows = pieces[0].shape[1]
    count = len(pieces)
    group = min(512, chan // PARTS)
    steps = chan // PARTS // group
    offset = part * steps
    local_offset = offset % (chan // 2 // group)
    full = lambda width: pl.BlockSpec((group, width), lambda m, place: (m + offset, 0))
    local = pl.BlockSpec((group, rows), lambda m, place: (m + local_offset, 0))
    whole = lambda array: pl.BlockSpec(array.shape, lambda m, place: (0, 0))
    anywhere = pl.BlockSpec(memory_space=pl.ANY)
    return pl.pallas_call(
        lambda *refs: product_kernel(count, *refs),
        grid_spec=pltpu.PrefetchScalarGridSpec(
            num_scalar_prefetch=1,
            grid=(steps,),
            in_specs=[anywhere]
            + [local if piece.shape[0] < chan else full(rows) for piece in pieces]
            + [full(seq_len), full(seq_len), full(seq_len), full(taps), full(taps)]
            + [whole(forward), whole(backward)]
            + [anywhere] * len(written),
            out_specs=[full(seq_len), full(seq_len), full(taps), full(taps), full(taps)],
            scratch_shapes=[
                pltpu.VMEM((group, seq_len), BF16),
                pltpu.VMEM((depth, seq_len), BF16),
                pltpu.SemaphoreType.DMA((count,)),
            ],
        ),
        out_shape=[
            jax.ShapeDtypeStruct((chan, seq_len), F32),
            jax.ShapeDtypeStruct((chan, seq_len), BF16),
            jax.ShapeDtypeStruct((chan, taps), F32),
            jax.ShapeDtypeStruct((chan, taps), BF16),
            jax.ShapeDtypeStruct((chan, taps), F32),
        ],
        input_output_aliases={9 + count + k: k for k in range(len(written))},
        compiler_params=pltpu.CompilerParams(vmem_limit_bytes=VMEM),
        cost_estimate=pl.CostEstimate(
            flops=2 * group * steps * seq_len * (depth + 16 * taps),
            bytes_accessed=2 * depth * (seq_len + group * steps) + 12 * group * steps * seq_len,
            transcendentals=0,
        ),
        name="product_kernel",
    )(place, grad_full, *pieces, mixed, gate, kv, prior, filters, forward, backward, *written)


def after(array, *earlier):
    return lax.optimization_barrier((array,) + earlier)[0] if earlier else array


class Layout:
    def __init__(self):
        self.count = lax.axis_size("ctx")
        self.depth = self.count // 4
        index = lax.axis_index("ctx")
        self.z, self.y, self.x = index // 4, (index // 2) % 2, index % 2
        self.pairs_x = [(i, i ^ 1) for i in range(self.count)]
        self.pairs_y = [(i, i ^ 2) for i in range(self.count)]

    def pairs_z(self, by):
        return [(i, (i + 4 * by) % self.count) for i in range(self.count)]

    def places(self, by):
        base = 4 * ((self.z + by) % self.depth)
        return [base + 2 * (self.y ^ dy) + (self.x ^ dx) for dy in range(2) for dx in range(2)]


class Stages:
    def __init__(self, at):
        self.at = at
        self.arrived = [()] * 3
        self.now = []
        self.ready = self.next_ready = ()
        self.back = 2

    def advance(self):
        self.arrived.append(tuple(self.now))
        self.now, self.ready, self.next_ready = [], self.next_ready, ()

    def hold(self, array):
        return after(array, *self.arrived[-2])

    def finished(self, *arrays):
        self.next_ready += arrays

    def send(self, array, pairs, *earlier):
        got = lax.ppermute(after(array, *self.arrived[-self.back], *self.ready, *earlier), "ctx", pairs)
        self.now.append(got)
        return got

    def swap_x(self, array, *earlier):
        return self.send(array, self.at.pairs_x, *earlier)

    def swap_y(self, array, *earlier):
        return self.send(array, self.at.pairs_y, *earlier)


def pick(bit, array, axis):
    halves = [lax.index_in_dim(array, k, axis, keepdims=False) for k in range(2)]
    return jnp.where(bit == 0, halves[0], halves[1])


def ordered(bit, mine, other):
    return jnp.stack([jnp.where(bit == 0, mine, other), jnp.where(bit == 0, other, mine)])


def reduce_filters(at, part, chan_count):
    taps = part.shape[1]
    part = part.reshape(at.depth, 2, 2, chan_count, taps)
    part = pick(at.x, part, 2) + lax.ppermute(pick(1 - at.x, part, 2), "ctx", at.pairs_x)
    part = pick(at.y, part, 1) + lax.ppermute(pick(1 - at.y, part, 1), "ctx", at.pairs_y)
    at_z = lambda by: lax.dynamic_index_in_dim(part, (at.z + by) % at.depth, 0, keepdims=False)
    total = at_z(0)
    for by in range(1, at.depth):
        total = total + lax.ppermute(at_z(by), "ctx", at.pairs_z(by))
    return total


def on_device(out_grad, gate_values, kv_product, w_out, filters):
    at = Layout()
    stages = Stages(at)
    chan_count = filters.shape[2]
    taps = filters.shape[3]
    seq_len = out_grad.shape[1]
    rows, chan = w_out.shape
    half = chan // 2
    norm_scale = 1.0 / math.sqrt(at.count * seq_len)
    to_right = [(i, i + 1) for i in range(at.count - 1)]
    to_left = [(i + 1, i) for i in range(at.count - 1)]
    forward, backward = (jnp.asarray(m) for m in dft_matrices(taps))

    grad_full = lax.all_gather(out_grad, "fsdp", axis=0, tiled=True)

    near = sorted(range(at.depth), key=lambda d: min(d, at.depth - d))
    far = near[::-1]
    own, own_filters = w_out.T, filters.reshape(chan_count, taps)
    filters_x = lax.ppermute(own_filters, "ctx", at.pairs_x)
    pair = ordered(at.x, own_filters, filters_x)
    filters_y = lax.ppermute(pair, "ctx", at.pairs_y)
    plane = ordered(at.y, pair, filters_y)
    shards = [own]
    for by in near[1:2]:
        shards.append(lax.ppermute(after(own, filters_y), "ctx", at.pairs_z(by)))
    ring = [
        lax.ppermute(after(plane, *shards[1:]), "ctx", at.pairs_z(by)) for by in range(at.depth - 1, 0, -1)
    ]
    for by in near[2:]:
        shards.append(lax.ppermute(after(own, *(ring if len(shards) == 2 else shards[-1:])), "ctx", at.pairs_z(by)))
    ring = jnp.stack((ring + [plane]) * 2)
    ring = lax.dynamic_slice_in_dim(ring, at.depth - 1 - at.z, at.depth, axis=0)
    all_filters = ring.reshape(chan, taps)
    prior = lax.ppermute(after(kv_product[:, seq_len - taps :], shards[1]), "ctx", to_right)

    from_x, from_y, diag_a, diag_b = {}, {}, {}, {}
    kept, summed = {}, {}

    def gather_first(k):
        both = (from_x[0], from_y[0]) if k == 1 else ()
        from_x[k] = stages.swap_x(shards[k], *(both if k else (filters_x,)))
        from_y[k] = stages.swap_y(shards[k], *(both if k else (filters_y,)))

    def gather_second(k):
        diag_a[k] = stages.swap_x(from_y[k][:half])
        diag_b[k] = stages.swap_y(from_x[k][half:])

    def weight_part(k):
        place = jnp.stack(at.places(far[k])).astype(jnp.int32)
        kept[k] = run_weight(place, grad_full, stages.hold(gated), rows)
        stages.finished(kept[k][0])

    def reduce_first(k):
        send_a, keep_a, send_b, keep_b = kept[k]
        kept[k] = (keep_a, stages.swap_x(send_a), keep_b, stages.swap_y(send_b))

    def reduce_second(k):
        keep_a, got_a, keep_b, got_b = kept[k]
        next_a = (keep_a[1].astype(F32) + got_a[1].astype(F32)).astype(BF16)
        next_b = (keep_b[1].astype(F32) + got_b[1].astype(F32)).astype(BF16)
        kept[k] = (keep_a, got_a, stages.swap_y(next_a), keep_b, got_b, stages.swap_x(next_b))

    def reduce_third(k):
        keep_a, got_a, last_a, keep_b, got_b, last_b = kept.pop(k)
        sum_a = keep_a[0].astype(F32) + got_a[0].astype(F32) + last_a.astype(F32)
        sum_b = keep_b[0].astype(F32) + got_b[0].astype(F32) + last_b.astype(F32)
        joint = jnp.concatenate([sum_a, sum_b], axis=1)
        by = far[k]
        summed[k] = joint if by == 0 else lax.ppermute(joint.astype(BF16), "ctx", at.pairs_z(by))
        if k + 2 < depth:
            stages.finished(summed[k])

    mixed = gated = place = products = None

    def mix():
        nonlocal mixed, gated
        mixed, gated = run_mix(all_filters, stages.hold(kv_product), prior, gate_values, forward, backward)
        stages.finished(mixed)

    def product(part):
        nonlocal products
        diag = diag_a if 2 * part < PARTS else diag_b
        pieces = [p for k in range(at.depth) for p in (shards[k], from_x[k], from_y[k], diag[k])]
        places = jnp.stack([c for by in near for c in at.places(-by)]).astype(jnp.int32)
        products = run_product(
            part, places, grad_full, pieces, stages.hold(mixed), gate_values, kv_product, prior,
            all_filters, forward, backward, products or (),
        )
        stages.finished(*products[3:4])

    depth = at.depth
    plan = {}
    for k in range(depth):
        plan.setdefault(k, []).append((gather_first, k))
        plan.setdefault(k + 2, []).append((gather_second, k))
        plan.setdefault(depth + [0, 1, 2, 2][min(k, 3)] + max(0, k - 3), []).append((reduce_first, k))
        plan.setdefault(depth + [2, 3, 4, 5][min(k, 3)] + max(0, k - 3), []).append((reduce_second, k))
    for stage in range(2 * depth + 4 + 0):
        if stage >= 2 * depth:
            stages.back = 1
        if stage == 2:
            mix()
        for k in range(depth):
            if stage == (2, 3, 4, 5)[min(k, 3)] + max(0, k - 3):
                weight_part(k)
            if stage == k + depth + 3:
                reduce_third(k)
        for part in range(PARTS):
            if stage == depth + [2, 3][part]:
                product(part)
        for action, k in plan.get(stage, []):
            action(k)
        stages.advance()

    total = summed[depth - 1]
    for k in range(depth - 1):
        total = total + summed[k].astype(F32)
    w_grad = total * norm_scale

    gate_grad, kv_grad, last, head, filt_part = products
    tail = lax.ppermute(head, "ctx", to_left)
    kv_grad = lax.dynamic_update_slice(
        kv_grad, (last + tail.astype(F32)).astype(BF16), (0, seq_len - taps)
    )
    filter_grad = reduce_filters(at, filt_part, chan_count) * norm_scale
    return (gate_grad, kv_grad, filter_grad.reshape(filters.shape), w_grad)


def solution(mesh):
    in_specs = (
        P("fsdp", "ctx"),
        P("fsdp", "ctx"),
        P("fsdp", "ctx"),
        P("ctx", "fsdp"),
        P("fsdp", "ctx", None, None),
    )
    out_specs = (P("fsdp", "ctx"), P("fsdp", "ctx"), P("fsdp", "ctx", None, None), P("ctx", "fsdp"))
    return jax.shard_map(
        on_device, mesh=mesh, in_specs=in_specs, out_specs=out_specs, check_vma=False
    )
```

```python
import math

import jax
import jax.numpy as jnp
import ml_dtypes
import numpy as np
from jax import lax
from jax.experimental import pallas as pl
from jax.experimental.pallas import tpu as pltpu
from jax.sharding import PartitionSpec as P

F32 = jnp.float32
BF16 = jnp.bfloat16
VMEM = 58 * 1024 * 1024
PARTS = 2


def split_pair(matrix):
    high = matrix.astype(ml_dtypes.bfloat16)
    low = (matrix - high.astype(np.float64)).astype(ml_dtypes.bfloat16)
    return high, low


def dft_matrices(taps):
    points = 2 * taps
    place = np.arange(taps)
    angle = 2.0 * np.pi * ((place[:, None] * place[None, :]) % points) / points
    turn = (-1.0) ** place
    forward = np.concatenate([np.cos(angle), -np.sin(angle)], axis=1)
    forward[:, taps] = turn
    weight = np.full((taps, 1), 2.0 / points)
    weight[0] = 1.0 / points
    backward = np.concatenate([weight * np.cos(angle), -weight * np.sin(angle)], axis=0)
    backward[taps, :] = turn / points
    forward = np.concatenate(split_pair(forward), axis=0)
    backward = np.concatenate(split_pair(backward), axis=1)
    return forward, backward


def spectrum(block, forward):
    taps = block.shape[1]
    both = jnp.dot(jnp.concatenate([block, block], axis=1), forward, preferred_element_type=F32)
    return both[:, :taps], both[:, taps:]


def inverse(real, imag, backward):
    taps = real.shape[1]
    whole = jnp.concatenate([real, imag], axis=1)
    high = whole.astype(BF16)
    low = (whole - high.astype(F32)).astype(BF16)
    both = jnp.dot(high, backward, preferred_element_type=F32)
    rest = jnp.dot(low, backward[:, :taps], preferred_element_type=F32)
    return both[:, :taps] + both[:, taps:] + rest


def lane_facts(taps):
    lane = lax.broadcasted_iota(jnp.int32, (1, taps), 1)
    sign = jnp.where(lane % 2 == 0, 1.0, -1.0)
    return lane == 0, sign


def filter_spectrum(filt, forward, first):
    real, imag = spectrum(filt, forward)
    return real, jnp.where(first, imag, real), jnp.where(first, 0.0, imag)


def mix_kernel(filt_ref, kv_ref, prior_ref, gate_ref, forward_ref, backward_ref, mixed_ref, gated_ref):
    taps = filt_ref.shape[1]
    blocks = kv_ref.shape[1] // taps
    forward, backward = forward_ref[...], backward_ref[...]
    first, sign = lane_facts(taps)
    sign_imag = jnp.where(first, 1.0, sign)
    h_real, h_last, h_imag = filter_spectrum(filt_ref[...], forward, first)
    prev_real, prev_imag = spectrum(prior_ref[...], forward)
    for b in range(blocks):
        span = slice(b * taps, (b + 1) * taps)
        real, imag = spectrum(kv_ref[:, span], forward)
        win_real = real + sign * prev_real
        win_imag = imag + sign_imag * prev_imag
        mixed = inverse(
            h_real * win_real - h_imag * win_imag, h_last * win_imag + h_imag * win_real, backward
        ).astype(BF16)
        mixed_ref[:, span] = mixed
        gated_ref[:, span] = (gate_ref[:, span].astype(F32) * mixed.astype(F32)).astype(BF16)
        prev_real, prev_imag = real, imag


def run_mix(filters, kv, prior, gate, forward, backward):
    chan, seq_len = kv.shape
    taps = filters.shape[1]
    group = min(256, chan)
    rows = lambda width: pl.BlockSpec((group, width), lambda g: (g, 0))
    whole = lambda array: pl.BlockSpec(array.shape, lambda g: (0, 0))
    return pl.pallas_call(
        mix_kernel,
        grid=(chan // group,),
        in_specs=[rows(taps), rows(seq_len), rows(taps), rows(seq_len), whole(forward), whole(backward)],
        out_specs=[rows(seq_len), rows(seq_len)],
        out_shape=[jax.ShapeDtypeStruct((chan, seq_len), BF16)] * 2,
        compiler_params=pltpu.CompilerParams(vmem_limit_bytes=VMEM),
        cost_estimate=pl.CostEstimate(
            flops=14 * chan * seq_len * 2 * taps, bytes_accessed=8 * chan * seq_len, transcendentals=0
        ),
        name="mix_kernel",
    )(filters, kv, prior, gate, forward, backward)


def weight_kernel(place_ref, g00, g01, g10, g11, left_ref, right_ref, send_a, keep_a, send_b, keep_b):
    rows = g00.shape[0]
    stack = jnp.concatenate([g01[...], g11[...], g00[...], g10[...]], axis=0)
    contract = (((1,), (1,)), ((), ()))
    left = lax.dot_general(stack, left_ref[...], contract, preferred_element_type=F32).astype(BF16)
    send_a[0] = left[:rows]
    send_a[1] = left[rows : 2 * rows]
    keep_a[0] = left[2 * rows : 3 * rows]
    keep_a[1] = left[3 * rows :]
    right = lax.dot_general(stack, right_ref[...], contract, preferred_element_type=F32).astype(BF16)
    send_b[0] = right[3 * rows :]
    send_b[1] = right[rows : 2 * rows]
    keep_b[0] = right[2 * rows : 3 * rows]
    keep_b[1] = right[:rows]


def run_weight(place, grad_full, gated, rows):
    chan, seq_len = gated.shape
    width = chan // 4
    grad_spec = lambda k: pl.BlockSpec((rows, seq_len), lambda n, place: (place[k], 0))
    gated_spec = lambda first: pl.BlockSpec((width, seq_len), lambda n, place: (n + first, 0))
    out_spec = pl.BlockSpec((2, rows, width), lambda n, place: (0, 0, n))
    return pl.pallas_call(
        weight_kernel,
        grid_spec=pltpu.PrefetchScalarGridSpec(
            num_scalar_prefetch=1,
            grid=(2,),
            in_specs=[grad_spec(k) for k in range(4)] + [gated_spec(0), gated_spec(2)],
            out_specs=[out_spec] * 4,
        ),
        out_shape=[jax.ShapeDtypeStruct((2, rows, chan // 2), BF16)] * 4,
        compiler_params=pltpu.CompilerParams(vmem_limit_bytes=VMEM),
        cost_estimate=pl.CostEstimate(
            flops=8 * rows * chan * seq_len,
            bytes_accessed=2 * (4 * rows * (seq_len + chan) + chan * seq_len),
            transcendentals=0,
        ),
        name="weight_kernel",
    )(place, grad_full, grad_full, grad_full, grad_full, gated, gated)


def product_kernel(count, place_ref, grad_hbm, *refs):
    pieces = refs[:count]
    mixed_ref, gate_ref, kv_ref, prior_ref, filt_ref, forward_ref, backward_ref = refs[count : count + 7]
    gate_grad_ref, kv_grad_ref, last_ref, head_ref, filt_grad_ref, conv, grad, sems = refs[-8:]
    step = pl.program_id(0)
    rows = pieces[0].shape[1]

    @pl.when(step == 0)
    def _():
        copies = [
            pltpu.make_async_copy(
                grad_hbm.at[pl.ds(pl.multiple_of(place_ref[k] * rows, rows), rows)],
                grad.at[pl.ds(k * rows, rows)],
                sems.at[k],
            )
            for k in range(count)
        ]
        for copy in copies:
            copy.start()
        for copy in copies:
            copy.wait()

    wide = [piece[...] for piece in pieces]
    total = jnp.dot(jnp.concatenate(wide, axis=1), grad[...], preferred_element_type=F32)
    gate_grad_ref[...] = total * mixed_ref[...].astype(F32)
    conv[...] = (total * gate_ref[...].astype(F32)).astype(BF16)

    group, taps = filt_ref.shape
    blocks = kv_ref.shape[1] // taps
    forward, backward = forward_ref[...], backward_ref[...]
    first, sign = lane_facts(taps)
    sign_imag = jnp.where(first, 1.0, sign)
    part = min(256, group)
    for at in range(0, group, part):
        chans = slice(at, at + part)
        h_real, h_last, h_imag = filter_spectrum(filt_ref[chans, :], forward, first)

        def pull_back(win_real, win_imag):
            return inverse(
                h_real * win_real + h_imag * win_imag, h_last * win_imag - h_imag * win_real, backward
            )

        past_real, past_imag = spectrum(prior_ref[chans, :], forward)
        g_real = g_imag = sum_real = sum_imag = 0.0
        for b in range(blocks):
            span = slice(b * taps, (b + 1) * taps)
            now_real, now_imag = spectrum(conv[chans, span], forward)
            back = pull_back(g_real + sign * now_real, g_imag + sign_imag * now_imag).astype(BF16)
            if b == 0:
                head_ref[chans, :] = back
            else:
                kv_grad_ref[chans, (b - 1) * taps : b * taps] = back
            x_real, x_imag = spectrum(kv_ref[chans, span], forward)
            win_real = x_real + sign * past_real
            win_imag = x_imag + sign_imag * past_imag
            win_last, win_skew = jnp.where(first, win_imag, win_real), jnp.where(first, 0.0, win_imag)
            sum_real = sum_real + now_real * win_real + now_imag * win_skew
            sum_imag = sum_imag + now_imag * win_last - now_real * win_skew
            g_real, g_imag = now_real, now_imag
            past_real, past_imag = x_real, x_imag
        last = pull_back(g_real, g_imag)
        last_ref[chans, :] = last
        kv_grad_ref[chans, (blocks - 1) * taps :] = last.astype(BF16)
        filt_grad_ref[chans, :] = inverse(sum_real, sum_imag, backward)


def run_product(part, place, grad_full, pieces, mixed, gate, kv, prior, filters, forward, backward, written):
    chan, seq_len = mixed.shape
    taps = filters.shape[1]
    depth = grad_full.shape[0]
    rows = pieces[0].shape[1]
    count = len(pieces)
    group = min(512, chan // PARTS)
    steps = chan // PARTS // group
    offset = part * steps
    local_offset = offset % (chan // 2 // group)
    full = lambda width: pl.BlockSpec((group, width), lambda m, place: (m + offset, 0))
    local = pl.BlockSpec((group, rows), lambda m, place: (m + local_offset, 0))
    whole = lambda array: pl.BlockSpec(array.shape, lambda m, place: (0, 0))
    anywhere = pl.BlockSpec(memory_space=pl.ANY)
    return pl.pallas_call(
        lambda *refs: product_kernel(count, *refs),
        grid_spec=pltpu.PrefetchScalarGridSpec(
            num_scalar_prefetch=1,
            grid=(steps,),
            in_specs=[anywhere]
            + [local if piece.shape[0] < chan else full(rows) for piece in pieces]
            + [full(seq_len), full(seq_len), full(seq_len), full(taps), full(taps)]
            + [whole(forward), whole(backward)]
            + [anywhere] * len(written),
            out_specs=[full(seq_len), full(seq_len), full(taps), full(taps), full(taps)],
            scratch_shapes=[
                pltpu.VMEM((group, seq_len), BF16),
                pltpu.VMEM((depth, seq_len), BF16),
                pltpu.SemaphoreType.DMA((count,)),
            ],
        ),
        out_shape=[
            jax.ShapeDtypeStruct((chan, seq_len), F32),
            jax.ShapeDtypeStruct((chan, seq_len), BF16),
            jax.ShapeDtypeStruct((chan, taps), F32),
            jax.ShapeDtypeStruct((chan, taps), BF16),
            jax.ShapeDtypeStruct((chan, taps), F32),
        ],
        input_output_aliases={9 + count + k: k for k in range(len(written))},
        compiler_params=pltpu.CompilerParams(vmem_limit_bytes=VMEM),
        cost_estimate=pl.CostEstimate(
            flops=2 * group * steps * seq_len * (depth + 16 * taps),
            bytes_accessed=2 * depth * (seq_len + group * steps) + 12 * group * steps * seq_len,
            transcendentals=0,
        ),
        name="product_kernel",
    )(place, grad_full, *pieces, mixed, gate, kv, prior, filters, forward, backward, *written)


def after(array, *earlier):
    return lax.optimization_barrier((array,) + earlier)[0] if earlier else array


class Layout:
    def __init__(self):
        self.count = lax.axis_size("ctx")
        self.depth = self.count // 4
        index = lax.axis_index("ctx")
        self.z, self.y, self.x = index // 4, (index // 2) % 2, index % 2
        self.pairs_x = [(i, i ^ 1) for i in range(self.count)]
        self.pairs_y = [(i, i ^ 2) for i in range(self.count)]

    def pairs_z(self, by):
        return [(i, (i + 4 * by) % self.count) for i in range(self.count)]

    def places(self, by):
        base = 4 * ((self.z + by) % self.depth)
        return [base + 2 * (self.y ^ dy) + (self.x ^ dx) for dy in range(2) for dx in range(2)]


class Stages:
    def __init__(self, at):
        self.at = at
        self.arrived = [()] * 3
        self.now = []
        self.ready = self.next_ready = ()
        self.back = 2

    def advance(self):
        self.arrived.append(tuple(self.now))
        self.now, self.ready, self.next_ready = [], self.next_ready, ()

    def hold(self, array):
        return after(array, *self.arrived[-2])

    def finished(self, *arrays):
        self.next_ready += arrays

    def send(self, array, pairs, *earlier):
        got = lax.ppermute(after(array, *self.arrived[-self.back], *self.ready, *earlier), "ctx", pairs)
        self.now.append(got)
        return got

    def swap_x(self, array, *earlier):
        return self.send(array, self.at.pairs_x, *earlier)

    def swap_y(self, array, *earlier):
        return self.send(array, self.at.pairs_y, *earlier)


def pick(bit, array, axis):
    halves = [lax.index_in_dim(array, k, axis, keepdims=False) for k in range(2)]
    return jnp.where(bit == 0, halves[0], halves[1])


def ordered(bit, mine, other):
    return jnp.stack([jnp.where(bit == 0, mine, other), jnp.where(bit == 0, other, mine)])


def reduce_filters(at, part, chan_count):
    taps = part.shape[1]
    part = part.reshape(at.depth, 2, 2, chan_count, taps)
    for bit, pairs, axis in ((at.x, at.pairs_x, 2), (at.y, at.pairs_y, 1)):
        got = lax.ppermute(pick(1 - bit, part, axis).astype(BF16), "ctx", pairs)
        part = pick(bit, part, axis) + got.astype(F32)
    at_z = lambda by: lax.dynamic_index_in_dim(part, (at.z + by) % at.depth, 0, keepdims=False)
    total = at_z(0)
    for by in range(1, at.depth):
        total = total + lax.ppermute(at_z(by), "ctx", at.pairs_z(by))
    return total


def on_device(out_grad, gate_values, kv_product, w_out, filters):
    at = Layout()
    stages = Stages(at)
    chan_count = filters.shape[2]
    taps = filters.shape[3]
    seq_len = out_grad.shape[1]
    rows, chan = w_out.shape
    half = chan // 2
    norm_scale = 1.0 / math.sqrt(at.count * seq_len)
    to_right = [(i, i + 1) for i in range(at.count - 1)]
    to_left = [(i + 1, i) for i in range(at.count - 1)]
    forward, backward = (jnp.asarray(m) for m in dft_matrices(taps))

    grad_full = lax.all_gather(out_grad, "fsdp", axis=0, tiled=True)

    near = sorted(range(at.depth), key=lambda d: min(d, at.depth - d))
    far = near[::-1]
    own, own_filters = w_out.T, filters.reshape(chan_count, taps)
    filters_x = lax.ppermute(own_filters, "ctx", at.pairs_x)
    pair = ordered(at.x, own_filters, filters_x)
    filters_y = lax.ppermute(pair, "ctx", at.pairs_y)
    plane = ordered(at.y, pair, filters_y)
    shards = {0: own}
    ring = {0: plane}

    def step_z(held, by, *earlier):
        way = 1 if by <= at.depth // 2 else -1
        return lax.ppermute(after(held[(by - way) % at.depth], *earlier), "ctx", at.pairs_z(way))

    before = filters_y
    for by in near[1:]:
        shards[by] = step_z(shards, by, before)
        if by == near[1]:
            for way in near[1:]:
                ring[way] = step_z(ring, way, shards[by])
        before = (shards[by], ring[near[-1]])[by == near[1]]
    ring = [ring[by] for by in range(at.depth - 1, 0, -1)]
    shards = [shards[by] for by in near]
    ring = jnp.stack((ring + [plane]) * 2)
    ring = lax.dynamic_slice_in_dim(ring, at.depth - 1 - at.z, at.depth, axis=0)
    all_filters = ring.reshape(chan, taps)
    prior = lax.ppermute(after(kv_product[:, seq_len - taps :], shards[1]), "ctx", to_right)

    from_x, from_y, diag_a, diag_b = {}, {}, {}, {}
    kept, summed, carried = {}, {}, {}
    depth = at.depth

    def gather_first(k):
        both = (from_x[0], from_y[0]) if k == 1 else ()
        from_x[k] = stages.swap_x(shards[k], *(both if k else (filters_x,)))
        from_y[k] = stages.swap_y(shards[k], *(both if k else (filters_y,)))

    def gather_second(k):
        diag_a[k] = stages.swap_x(from_y[k][:half])
        diag_b[k] = stages.swap_y(from_x[k][half:])

    def weight_part(k):
        place = jnp.stack(at.places(far[k])).astype(jnp.int32)
        kept[k] = run_weight(place, grad_full, stages.hold(gated), rows)
        stages.finished(kept[k][0])

    def reduce_first(k):
        send_a, keep_a, send_b, keep_b = kept[k]
        kept[k] = (keep_a, stages.swap_x(send_a), keep_b, stages.swap_y(send_b))

    def reduce_second(k):
        keep_a, got_a, keep_b, got_b = kept[k]
        next_a = (keep_a[1].astype(F32) + got_a[1].astype(F32)).astype(BF16)
        next_b = (keep_b[1].astype(F32) + got_b[1].astype(F32)).astype(BF16)
        kept[k] = (keep_a, got_a, stages.swap_y(next_a), keep_b, got_b, stages.swap_x(next_b))

    def reduce_third(k):
        keep_a, got_a, last_a, keep_b, got_b, last_b = kept.pop(k)
        sum_a = keep_a[0].astype(F32) + got_a[0].astype(F32) + last_a.astype(F32)
        sum_b = keep_b[0].astype(F32) + got_b[0].astype(F32) + last_b.astype(F32)
        joint = jnp.concatenate([sum_a, sum_b], axis=1)
        by = far[k]
        for piece in carried.pop(by, ()):
            joint = joint + piece.astype(F32)
        if by == 0:
            summed[0] = joint
            return
        way = 1 if by <= depth // 2 else -1
        got = lax.ppermute(joint.astype(BF16), "ctx", at.pairs_z(way))
        carried.setdefault((by - way) % depth, []).append(got)
        if k < 2:
            stages.finished(got)

    mixed = gated = place = products = None

    def mix():
        nonlocal mixed, gated
        mixed, gated = run_mix(all_filters, stages.hold(kv_product), prior, gate_values, forward, backward)
        stages.finished(mixed)

    def product(part):
        nonlocal products
        diag = diag_a if 2 * part < PARTS else diag_b
        pieces = [p for k in range(at.depth) for p in (shards[k], from_x[k], from_y[k], diag[k])]
        places = jnp.stack([c for by in near for c in at.places(-by)]).astype(jnp.int32)
        products = run_product(
            part, places, grad_full, pieces, stages.hold(mixed), gate_values, kv_product, prior,
            all_filters, forward, backward, products or (),
        )
        stages.finished(*products[3:4])

    depth = at.depth
    plan = {}
    for k in range(depth):
        plan.setdefault(k, []).append((gather_first, k))
        plan.setdefault(k + 2, []).append((gather_second, k))
        plan.setdefault(depth + [0, 1, 2, 2][min(k, 3)] + max(0, k - 3), []).append((reduce_first, k))
        plan.setdefault(depth + [2, 3, 4, 5][min(k, 3)] + max(0, k - 3), []).append((reduce_second, k))
    for stage in range(2 * depth + 4 + 0):
        if stage >= 2 * depth:
            stages.back = 1
        if stage == 2:
            mix()
        for k in range(depth):
            if stage == (2, 3, 4, 5)[min(k, 3)] + max(0, k - 3):
                weight_part(k)
            if stage == depth + [3, 4, 5, 6][min(k, 3)] + max(0, k - 3):
                reduce_third(k)
        for part in range(PARTS):
            if stage == depth + [2, 3][part]:
                product(part)
        for action, k in plan.get(stage, []):
            action(k)
        stages.advance()

    w_grad = summed[0] * norm_scale

    gate_grad, kv_grad, last, head, filt_part = products
    tail = lax.ppermute(head, "ctx", to_left)
    kv_grad = lax.dynamic_update_slice(
        kv_grad, (last + tail.astype(F32)).astype(BF16), (0, seq_len - taps)
    )
    filter_grad = reduce_filters(at, filt_part, chan_count) * norm_scale
    return (gate_grad, kv_grad, filter_grad.reshape(filters.shape), w_grad)


def solution(mesh):
    in_specs = (
        P("fsdp", "ctx"),
        P("fsdp", "ctx"),
        P("fsdp", "ctx"),
        P("ctx", "fsdp"),
        P("fsdp", "ctx", None, None),
    )
    out_specs = (P("fsdp", "ctx"), P("fsdp", "ctx"), P("fsdp", "ctx", None, None), P("ctx", "fsdp"))
    return jax.shard_map(
        on_device, mesh=mesh, in_specs=in_specs, out_specs=out_specs, check_vma=False
    )
```

```python
import math

import jax
import jax.numpy as jnp
import ml_dtypes
import numpy as np
from jax import lax
from jax.experimental import pallas as pl
from jax.experimental.pallas import tpu as pltpu
from jax.sharding import PartitionSpec as P

F32 = jnp.float32
BF16 = jnp.bfloat16
VMEM = 58 * 1024 * 1024
PARTS = 2
MIX_STAGE = 2
WEIGHT_STAGE = (2, 3, 4, 6)
THIRD_STAGE = (7, 7, 8, 9)
PRODUCT_STAGE = (6, 7)
GATHER_SECOND = (2, 4, 4, 5)
REDUCE_FIRST = (4, 4, 5, 7)
REDUCE_SECOND = (6, 6, 6, 8)
CLOSE_STAGE = 8
Z_PINNED = 2


def split_pair(matrix):
    high = matrix.astype(ml_dtypes.bfloat16)
    low = (matrix - high.astype(np.float64)).astype(ml_dtypes.bfloat16)
    return high, low


def dft_matrices(taps):
    points = 2 * taps
    place = np.arange(taps)
    angle = 2.0 * np.pi * ((place[:, None] * place[None, :]) % points) / points
    turn = (-1.0) ** place
    forward = np.concatenate([np.cos(angle), -np.sin(angle)], axis=1)
    forward[:, taps] = turn
    weight = np.full((taps, 1), 2.0 / points)
    weight[0] = 1.0 / points
    backward = np.concatenate([weight * np.cos(angle), -weight * np.sin(angle)], axis=0)
    backward[taps, :] = turn / points
    forward = np.concatenate(split_pair(forward), axis=0)
    backward = np.concatenate(split_pair(backward), axis=1)
    return forward, backward


def spectrum(block, forward):
    taps = block.shape[1]
    both = jnp.dot(jnp.concatenate([block, block], axis=1), forward, preferred_element_type=F32)
    return both[:, :taps], both[:, taps:]


def inverse(real, imag, backward):
    taps = real.shape[1]
    whole = jnp.concatenate([real, imag], axis=1)
    high = whole.astype(BF16)
    low = (whole - high.astype(F32)).astype(BF16)
    both = jnp.dot(high, backward, preferred_element_type=F32)
    rest = jnp.dot(low, backward[:, :taps], preferred_element_type=F32)
    return both[:, :taps] + both[:, taps:] + rest


def lane_facts(taps):
    lane = lax.broadcasted_iota(jnp.int32, (1, taps), 1)
    sign = jnp.where(lane % 2 == 0, 1.0, -1.0)
    return lane == 0, sign


def filter_spectrum(filt, forward, first):
    real, imag = spectrum(filt, forward)
    return real, jnp.where(first, imag, real), jnp.where(first, 0.0, imag)


def mix_kernel(filt_ref, kv_ref, prior_ref, gate_ref, forward_ref, backward_ref, mixed_ref, gated_ref):
    taps = filt_ref.shape[1]
    blocks = kv_ref.shape[1] // taps
    forward, backward = forward_ref[...], backward_ref[...]
    first, sign = lane_facts(taps)
    sign_imag = jnp.where(first, 1.0, sign)
    h_real, h_last, h_imag = filter_spectrum(filt_ref[...], forward, first)
    prev_real, prev_imag = spectrum(prior_ref[...], forward)
    for b in range(blocks):
        span = slice(b * taps, (b + 1) * taps)
        real, imag = spectrum(kv_ref[:, span], forward)
        win_real = real + sign * prev_real
        win_imag = imag + sign_imag * prev_imag
        mixed = inverse(
            h_real * win_real - h_imag * win_imag, h_last * win_imag + h_imag * win_real, backward
        ).astype(BF16)
        mixed_ref[:, span] = mixed
        gated_ref[:, span] = (gate_ref[:, span].astype(F32) * mixed.astype(F32)).astype(BF16)
        prev_real, prev_imag = real, imag


def run_mix(filters, kv, prior, gate, forward, backward):
    chan, seq_len = kv.shape
    taps = filters.shape[1]
    group = min(256, chan)
    rows = lambda width: pl.BlockSpec((group, width), lambda g: (g, 0))
    whole = lambda array: pl.BlockSpec(array.shape, lambda g: (0, 0))
    return pl.pallas_call(
        mix_kernel,
        grid=(chan // group,),
        in_specs=[rows(taps), rows(seq_len), rows(taps), rows(seq_len), whole(forward), whole(backward)],
        out_specs=[rows(seq_len), rows(seq_len)],
        out_shape=[jax.ShapeDtypeStruct((chan, seq_len), BF16)] * 2,
        compiler_params=pltpu.CompilerParams(vmem_limit_bytes=VMEM),
        cost_estimate=pl.CostEstimate(
            flops=14 * chan * seq_len * 2 * taps, bytes_accessed=8 * chan * seq_len, transcendentals=0
        ),
        name="mix_kernel",
    )(filters, kv, prior, gate, forward, backward)


def weight_kernel(place_ref, g00, g01, g10, g11, left_ref, right_ref, *refs):
    added, (send_a, keep_a, send_b, keep_b) = refs[:-4], refs[-4:]
    rows = g00.shape[0]
    stack = jnp.concatenate([g01[...], g11[...], g00[...], g10[...]], axis=0)
    contract = (((1,), (1,)), ((), ()))
    left = lax.dot_general(stack, left_ref[...], contract, preferred_element_type=F32)
    diag = left[rows : 2 * rows]
    for piece in added[0::2]:
        diag = diag + piece[...].astype(F32)
    send_a[0] = left[:rows].astype(BF16)
    send_a[1] = diag.astype(BF16)
    keep_a[0] = left[2 * rows : 3 * rows].astype(BF16)
    keep_a[1] = left[3 * rows :].astype(BF16)
    right = lax.dot_general(stack, right_ref[...], contract, preferred_element_type=F32)
    diag = right[rows : 2 * rows]
    for piece in added[1::2]:
        diag = diag + piece[...].astype(F32)
    send_b[0] = right[3 * rows :].astype(BF16)
    send_b[1] = diag.astype(BF16)
    keep_b[0] = right[2 * rows : 3 * rows].astype(BF16)
    keep_b[1] = right[:rows].astype(BF16)


def direct_kernel(place_ref, g00, g01, g10, g11, gated_ref, keep, send_x, send_y, send_z):
    rows = g00.shape[0]
    stack = jnp.concatenate([g00[...], g01[...], g10[...], g11[...]], axis=0)
    both = lax.dot_general(stack, gated_ref[...], (((1,), (1,)), ((), ())), preferred_element_type=F32)
    for k, ref in enumerate((keep, send_x, send_y, send_z)):
        ref[...] = both[k * rows : (k + 1) * rows].astype(BF16)


def run_weight(place, grad_full, gated, rows, direct, added=()):
    chan, seq_len = gated.shape
    width = chan // 4
    grad_spec = lambda k: pl.BlockSpec((rows, seq_len), lambda n, place: (place[k], 0))
    gated_spec = lambda first: pl.BlockSpec((width, seq_len), lambda n, place: (n + first, 0))
    added_spec = lambda first: pl.BlockSpec((rows, width), lambda n, place: (0, n + first))
    grads = [grad_spec(k) for k in range(4)]
    if direct:
        kernel, steps, in_specs, operands = direct_kernel, 4, grads + [gated_spec(0)], [gated]
        out_spec = pl.BlockSpec((rows, width), lambda n, place: (0, n))
        out_shape = jax.ShapeDtypeStruct((rows, chan), BF16)
    else:
        kernel, steps, in_specs, operands = weight_kernel, 2, grads + [gated_spec(0), gated_spec(2)], [gated, gated]
        for piece in added:
            in_specs += [added_spec(0), added_spec(2)]
            operands += [piece, piece]
        out_spec = pl.BlockSpec((2, rows, width), lambda n, place: (0, 0, n))
        out_shape = jax.ShapeDtypeStruct((2, rows, chan // 2), BF16)
    return pl.pallas_call(
        kernel,
        grid_spec=pltpu.PrefetchScalarGridSpec(
            num_scalar_prefetch=1, grid=(steps,), in_specs=in_specs, out_specs=[out_spec] * 4
        ),
        out_shape=[out_shape] * 4,
        compiler_params=pltpu.CompilerParams(vmem_limit_bytes=VMEM),
        cost_estimate=pl.CostEstimate(
            flops=8 * rows * chan * seq_len,
            bytes_accessed=2 * (4 * rows * (seq_len + chan) + chan * seq_len),
            transcendentals=0,
        ),
        name="weight_kernel",
    )(place, grad_full, grad_full, grad_full, grad_full, *operands)


def product_kernel(count, place_ref, grad_hbm, *refs):
    pieces = refs[:count]
    mixed_ref, gate_ref, kv_ref, prior_ref, filt_ref, forward_ref, backward_ref = refs[count : count + 7]
    gate_grad_ref, kv_grad_ref, last_ref, head_ref, filt_grad_ref, conv, grad, sems = refs[-8:]
    step = pl.program_id(0)
    rows = pieces[0].shape[1]

    @pl.when(step == 0)
    def _():
        copies = [
            pltpu.make_async_copy(
                grad_hbm.at[pl.ds(pl.multiple_of(place_ref[k] * rows, rows), rows)],
                grad.at[pl.ds(k * rows, rows)],
                sems.at[k],
            )
            for k in range(count)
        ]
        for copy in copies:
            copy.start()
        for copy in copies:
            copy.wait()

    wide = [piece[...] for piece in pieces]
    total = jnp.dot(jnp.concatenate(wide, axis=1), grad[...], preferred_element_type=F32)
    gate_grad_ref[...] = total * mixed_ref[...].astype(F32)
    conv[...] = (total * gate_ref[...].astype(F32)).astype(BF16)

    group, taps = filt_ref.shape
    blocks = kv_ref.shape[1] // taps
    forward, backward = forward_ref[...], backward_ref[...]
    first, sign = lane_facts(taps)
    sign_imag = jnp.where(first, 1.0, sign)
    part = min(256, group)
    for at in range(0, group, part):
        chans = slice(at, at + part)
        h_real, h_last, h_imag = filter_spectrum(filt_ref[chans, :], forward, first)

        def pull_back(win_real, win_imag):
            return inverse(
                h_real * win_real + h_imag * win_imag, h_last * win_imag - h_imag * win_real, backward
            )

        past_real, past_imag = spectrum(prior_ref[chans, :], forward)
        g_real = g_imag = sum_real = sum_imag = 0.0
        for b in range(blocks):
            span = slice(b * taps, (b + 1) * taps)
            now_real, now_imag = spectrum(conv[chans, span], forward)
            back = pull_back(g_real + sign * now_real, g_imag + sign_imag * now_imag).astype(BF16)
            if b == 0:
                head_ref[chans, :] = back
            else:
                kv_grad_ref[chans, (b - 1) * taps : b * taps] = back
            x_real, x_imag = spectrum(kv_ref[chans, span], forward)
            win_real = x_real + sign * past_real
            win_imag = x_imag + sign_imag * past_imag
            win_last, win_skew = jnp.where(first, win_imag, win_real), jnp.where(first, 0.0, win_imag)
            sum_real = sum_real + now_real * win_real + now_imag * win_skew
            sum_imag = sum_imag + now_imag * win_last - now_real * win_skew
            g_real, g_imag = now_real, now_imag
            past_real, past_imag = x_real, x_imag
        last = pull_back(g_real, g_imag)
        last_ref[chans, :] = last
        kv_grad_ref[chans, (blocks - 1) * taps :] = last.astype(BF16)
        filt_grad_ref[chans, :] = inverse(sum_real, sum_imag, backward)


def run_product(part, place, grad_full, pieces, mixed, gate, kv, prior, filters, forward, backward, written):
    chan, seq_len = mixed.shape
    taps = filters.shape[1]
    depth = grad_full.shape[0]
    rows = pieces[0].shape[1]
    count = len(pieces)
    group = min(512, chan // PARTS)
    steps = chan // PARTS // group
    offset = part * steps
    local_offset = offset % (chan // 2 // group)
    full = lambda width: pl.BlockSpec((group, width), lambda m, place: (m + offset, 0))
    local = pl.BlockSpec((group, rows), lambda m, place: (m + local_offset, 0))
    whole = lambda array: pl.BlockSpec(array.shape, lambda m, place: (0, 0))
    anywhere = pl.BlockSpec(memory_space=pl.ANY)
    return pl.pallas_call(
        lambda *refs: product_kernel(count, *refs),
        grid_spec=pltpu.PrefetchScalarGridSpec(
            num_scalar_prefetch=1,
            grid=(steps,),
            in_specs=[anywhere]
            + [local if piece.shape[0] < chan else full(rows) for piece in pieces]
            + [full(seq_len), full(seq_len), full(seq_len), full(taps), full(taps)]
            + [whole(forward), whole(backward)]
            + [anywhere] * len(written),
            out_specs=[full(seq_len), full(seq_len), full(taps), full(taps), full(taps)],
            scratch_shapes=[
                pltpu.VMEM((group, seq_len), BF16),
                pltpu.VMEM((depth, seq_len), BF16),
                pltpu.SemaphoreType.DMA((count,)),
            ],
        ),
        out_shape=[
            jax.ShapeDtypeStruct((chan, seq_len), F32),
            jax.ShapeDtypeStruct((chan, seq_len), BF16),
            jax.ShapeDtypeStruct((chan, taps), F32),
            jax.ShapeDtypeStruct((chan, taps), BF16),
            jax.ShapeDtypeStruct((chan, taps), F32),
        ],
        input_output_aliases={9 + count + k: k for k in range(len(written))},
        compiler_params=pltpu.CompilerParams(vmem_limit_bytes=VMEM),
        cost_estimate=pl.CostEstimate(
            flops=2 * group * steps * seq_len * (depth + 16 * taps),
            bytes_accessed=2 * depth * (seq_len + group * steps) + 12 * group * steps * seq_len,
            transcendentals=0,
        ),
        name="product_kernel",
    )(place, grad_full, *pieces, mixed, gate, kv, prior, filters, forward, backward, *written)


def after(array, *earlier):
    return lax.optimization_barrier((array,) + earlier)[0] if earlier else array


class Layout:
    def __init__(self):
        self.count = lax.axis_size("ctx")
        self.depth = self.count // 4
        index = lax.axis_index("ctx")
        self.z, self.y, self.x = index // 4, (index // 2) % 2, index % 2
        self.pairs_x = [(i, i ^ 1) for i in range(self.count)]
        self.pairs_y = [(i, i ^ 2) for i in range(self.count)]

    def pairs_z(self, by):
        return [(i, (i + 4 * by) % self.count) for i in range(self.count)]

    def places(self, by):
        base = 4 * ((self.z + by) % self.depth)
        return [base + 2 * (self.y ^ dy) + (self.x ^ dx) for dy in range(2) for dx in range(2)]


class Stages:
    def __init__(self, at):
        self.at = at
        self.arrived = [()] * 3
        self.now = []
        self.ready = self.next_ready = ()
        self.back = 2

    def advance(self):
        self.arrived.append(tuple(self.now))
        self.now, self.ready, self.next_ready = [], self.next_ready, ()

    def hold(self, array):
        return after(array, *self.arrived[-2])

    def finished(self, *arrays):
        self.next_ready += arrays

    def send(self, array, pairs, *earlier):
        got = lax.ppermute(after(array, *self.arrived[-self.back], *self.ready, *earlier), "ctx", pairs)
        self.now.append(got)
        return got

    def swap_x(self, array, *earlier):
        return self.send(array, self.at.pairs_x, *earlier)

    def swap_y(self, array, *earlier):
        return self.send(array, self.at.pairs_y, *earlier)


def pick(bit, array, axis):
    halves = [lax.index_in_dim(array, k, axis, keepdims=False) for k in range(2)]
    return jnp.where(bit == 0, halves[0], halves[1])


def ordered(bit, mine, other):
    return jnp.stack([jnp.where(bit == 0, mine, other), jnp.where(bit == 0, other, mine)])


def reduce_filters(at, part, chan_count):
    taps = part.shape[1]
    part = part.reshape(at.depth, 2, 2, chan_count, taps)
    for bit, pairs, axis in ((at.x, at.pairs_x, 2), (at.y, at.pairs_y, 1)):
        got = lax.ppermute(pick(1 - bit, part, axis).astype(BF16), "ctx", pairs)
        part = pick(bit, part, axis) + got.astype(F32)
    at_z = lambda by: lax.dynamic_index_in_dim(part, (at.z + by) % at.depth, 0, keepdims=False)
    total = at_z(0)
    for by in range(1, at.depth):
        total = total + lax.ppermute(at_z(by), "ctx", at.pairs_z(by))
    return total


def on_device(out_grad, gate_values, kv_product, w_out, filters):
    at = Layout()
    stages = Stages(at)
    chan_count = filters.shape[2]
    taps = filters.shape[3]
    seq_len = out_grad.shape[1]
    rows, chan = w_out.shape
    half = chan // 2
    norm_scale = 1.0 / math.sqrt(at.count * seq_len)
    to_right = [(i, i + 1) for i in range(at.count - 1)]
    to_left = [(i + 1, i) for i in range(at.count - 1)]
    forward, backward = (jnp.asarray(m) for m in dft_matrices(taps))

    grad_full = lax.all_gather(out_grad, "fsdp", axis=0, tiled=True)

    near = sorted(range(at.depth), key=lambda d: min(d, at.depth - d))
    far = near[::-1]
    own, own_filters = w_out.T, filters.reshape(chan_count, taps)
    filters_x = lax.ppermute(own_filters, "ctx", at.pairs_x)
    pair = ordered(at.x, own_filters, filters_x)
    filters_y = lax.ppermute(pair, "ctx", at.pairs_y)
    plane = ordered(at.y, pair, filters_y)
    depth = at.depth
    shards = {0: own}
    ring = {0: plane}
    beside = {1, depth - 1} if depth > 2 else set()

    def step_z(held, by, *earlier):
        way = 1 if by <= depth // 2 else -1
        return lax.ppermute(after(held[(by - way) % depth], *earlier), "ctx", at.pairs_z(way))

    before = filters_y
    for by in near[1:]:
        shards[by] = before = step_z(shards, by, before)
        if by == near[1]:
            for way in near[1:]:
                ring[way] = step_z(ring, way, shards[by])
    ring = [ring[by] for by in range(depth - 1, 0, -1)]
    shards = [shards[by] for by in near]
    ring = jnp.stack((ring + [plane]) * 2)
    ring = lax.dynamic_slice_in_dim(ring, depth - 1 - at.z, depth, axis=0)
    all_filters = ring.reshape(chan, taps)
    prior = lax.ppermute(after(kv_product[:, seq_len - taps :], shards[1]), "ctx", to_right)

    from_x, from_y, diag_a, diag_b = {}, {}, {}, {}
    kept, carried, crossed, last_sent = {}, {}, [], []
    mixed = gated = products = w_grad = None

    def gather_first(k):
        both = (from_x[0], from_y[0]) if k == 1 else ()
        from_x[k] = stages.swap_x(shards[k], *both)
        from_y[k] = stages.swap_y(shards[k], *both)

    def gather_second(k):
        if near[k] in beside:
            pairs = at.pairs_z(1 if near[k] == 1 else -1)
            diag_a[k] = lax.ppermute(diag_a[0], "ctx", pairs)
            diag_b[k] = lax.ppermute(diag_b[0], "ctx", pairs)
            stages.finished(diag_a[k], diag_b[k])
        else:
            diag_a[k] = stages.swap_x(from_y[k][:half])
            diag_b[k] = stages.swap_y(from_x[k][half:])

    def mix():
        nonlocal mixed, gated
        mixed, gated = run_mix(all_filters, stages.hold(kv_product), prior, gate_values, forward, backward)
        stages.finished(mixed)

    def weight_part(k):
        place = jnp.stack(at.places(far[k])).astype(jnp.int32)
        added = crossed if far[k] == 0 else ()
        kept[k] = run_weight(place, grad_full, stages.hold(gated), rows, far[k] in beside, added)
        stages.finished(kept[k][0])

    def reduce_first(k):
        by = far[k]
        if by in beside:
            keep, send_x, send_y, send_z = kept[k]
            kept[k] = (keep, stages.swap_x(send_x), stages.swap_y(send_y))
            crossed.append(lax.ppermute(send_z, "ctx", at.pairs_z(1 if by == 1 else -1)))
        else:
            send_a, keep_a, send_b, keep_b = kept[k]
            kept[k] = (keep_a, stages.swap_x(send_a), keep_b, stages.swap_y(send_b))
            if by == 0:
                last_sent.extend((kept[k][1], kept[k][3]))

    def reduce_second(k):
        if far[k] in beside:
            return
        keep_a, got_a, keep_b, got_b = kept[k]
        next_a = (keep_a[1].astype(F32) + got_a[1].astype(F32)).astype(BF16)
        next_b = (keep_b[1].astype(F32) + got_b[1].astype(F32)).astype(BF16)
        kept[k] = (keep_a, got_a, stages.swap_y(next_a), keep_b, got_b, stages.swap_x(next_b))

    def reduce_third(k):
        nonlocal w_grad
        by = far[k]
        if by in beside:
            joint = sum(piece.astype(F32) for piece in kept.pop(k))
        else:
            keep_a, got_a, last_a, keep_b, got_b, last_b = kept.pop(k)
            sum_a = keep_a[0].astype(F32) + got_a[0].astype(F32) + last_a.astype(F32)
            sum_b = keep_b[0].astype(F32) + got_b[0].astype(F32) + last_b.astype(F32)
            joint = jnp.concatenate([sum_a, sum_b], axis=1)
        for piece in carried.pop(by, ()):
            joint = joint + piece.astype(F32)
        if by == 0:
            w_grad = joint * norm_scale
            return
        way = 1 if by <= depth // 2 else -1
        got = lax.ppermute(joint.astype(BF16), "ctx", at.pairs_z(way))
        carried.setdefault((by - way) % depth, []).append(got)
        if k < Z_PINNED:
            stages.finished(got)

    def product(part):
        nonlocal products
        diag = diag_a if 2 * part < PARTS else diag_b
        pieces = [p for k in range(depth) for p in (shards[k], from_x[k], from_y[k], diag[k])]
        places = jnp.stack([c for by in near for c in at.places(-by)]).astype(jnp.int32)
        products = run_product(
            part, places, grad_full, pieces, stages.hold(mixed), gate_values, kv_product, prior,
            all_filters, forward, backward, products or (),
        )
        stages.finished(products[3])

    late = depth - 4
    plan = {}

    def at_stage(stage, action, k):
        plan.setdefault(stage, []).append((action, k))

    at_stage(MIX_STAGE, lambda _: mix(), 0)
    for k in range(depth):
        more = max(0, k - 3)
        at_stage(WEIGHT_STAGE[min(k, 3)] + more + late, weight_part, k)
    for k in range(depth):
        at_stage(THIRD_STAGE[min(k, 3)] + max(0, k - 3) + late, reduce_third, k)
    for part in range(PARTS):
        at_stage(PRODUCT_STAGE[part] + 2 * late, lambda p: product(p), part)
    for k in range(depth):
        more = max(0, k - 3)
        at_stage(k, gather_first, k)
        at_stage(GATHER_SECOND[min(k, 3)] + more, gather_second, k)
        at_stage(REDUCE_FIRST[min(k, 3)] + more + late, reduce_first, k)
        at_stage(REDUCE_SECOND[min(k, 3)] + more + late, reduce_second, k)
    for stage in range(max(plan) + 1):
        if stage >= CLOSE_STAGE + 2 * late:
            stages.back = 1
        for action, k in plan.get(stage, []):
            action(k)
        stages.advance()

    gate_grad, kv_grad, last, head, filt_part = products
    tail = lax.ppermute(head, "ctx", to_left)
    kv_grad = lax.dynamic_update_slice(
        kv_grad, (last + tail.astype(F32)).astype(BF16), (0, seq_len - taps)
    )
    filter_grad = reduce_filters(at, after(filt_part, *last_sent), chan_count) * norm_scale
    return (gate_grad, kv_grad, filter_grad.reshape(filters.shape), w_grad)


def solution(mesh):
    in_specs = (
        P("fsdp", "ctx"),
        P("fsdp", "ctx"),
        P("fsdp", "ctx"),
        P("ctx", "fsdp"),
        P("fsdp", "ctx", None, None),
    )
    out_specs = (P("fsdp", "ctx"), P("fsdp", "ctx"), P("fsdp", "ctx", None, None), P("ctx", "fsdp"))
    return jax.shard_map(
        on_device, mesh=mesh, in_specs=in_specs, out_specs=out_specs, check_vma=False
    )
```

```python
import math

import jax
import jax.numpy as jnp
import ml_dtypes
import numpy as np
from jax import lax
from jax.experimental import pallas as pl
from jax.experimental.pallas import tpu as pltpu
from jax.sharding import PartitionSpec as P

F32 = jnp.float32
BF16 = jnp.bfloat16
VMEM = 58 * 1024 * 1024
MIX_STAGE = 2
WEIGHT_STAGE = (2, 3, 4, 6)
THIRD_STAGE = (7, 7, 8, 9)
PRODUCT_STAGE = (6, 7)
GATHER_SECOND = (2, 3, 4, 5)
REDUCE_FIRST = (4, 4, 5, 7)
REDUCE_SECOND = (6, 6, 6, 8)
CLOSE_STAGE = 8
Z_PINNED = 2
PARTS = 2


def split_pair(matrix):
    high = matrix.astype(ml_dtypes.bfloat16)
    low = (matrix - high.astype(np.float64)).astype(ml_dtypes.bfloat16)
    return high, low


def dft_matrices(taps):
    points = 2 * taps
    place = np.arange(taps)
    angle = 2.0 * np.pi * ((place[:, None] * place[None, :]) % points) / points
    turn = (-1.0) ** place
    forward = np.concatenate([np.cos(angle), -np.sin(angle)], axis=1)
    forward[:, taps] = turn
    weight = np.full((taps, 1), 2.0 / points)
    weight[0] = 1.0 / points
    backward = np.concatenate([weight * np.cos(angle), -weight * np.sin(angle)], axis=0)
    backward[taps, :] = turn / points
    forward = np.concatenate(split_pair(forward), axis=0)
    backward = np.concatenate(split_pair(backward), axis=1)
    return forward, backward


def spectrum(block, forward):
    taps = block.shape[1]
    both = jnp.dot(jnp.concatenate([block, block], axis=1), forward, preferred_element_type=F32)
    return both[:, :taps], both[:, taps:]


def inverse(real, imag, backward):
    taps = real.shape[1]
    whole = jnp.concatenate([real, imag], axis=1)
    high = whole.astype(BF16)
    low = (whole - high.astype(F32)).astype(BF16)
    both = jnp.dot(high, backward, preferred_element_type=F32)
    rest = jnp.dot(low, backward[:, :taps], preferred_element_type=F32)
    return both[:, :taps] + both[:, taps:] + rest


def lane_facts(taps):
    lane = lax.broadcasted_iota(jnp.int32, (1, taps), 1)
    sign = jnp.where(lane % 2 == 0, 1.0, -1.0)
    return lane == 0, sign


def filter_spectrum(filt, forward, first):
    real, imag = spectrum(filt, forward)
    return real, jnp.where(first, imag, real), jnp.where(first, 0.0, imag)


def mix_kernel(filt_ref, kv_ref, prior_ref, gate_ref, forward_ref, backward_ref, mixed_ref, gated_ref):
    taps = filt_ref.shape[1]
    blocks = kv_ref.shape[1] // taps
    forward, backward = forward_ref[...], backward_ref[...]
    first, sign = lane_facts(taps)
    sign_imag = jnp.where(first, 1.0, sign)
    h_real, h_last, h_imag = filter_spectrum(filt_ref[...], forward, first)
    prev_real, prev_imag = spectrum(prior_ref[...], forward)
    for b in range(blocks):
        span = slice(b * taps, (b + 1) * taps)
        real, imag = spectrum(kv_ref[:, span], forward)
        win_real = real + sign * prev_real
        win_imag = imag + sign_imag * prev_imag
        mixed = inverse(
            h_real * win_real - h_imag * win_imag, h_last * win_imag + h_imag * win_real, backward
        ).astype(BF16)
        mixed_ref[:, span] = mixed
        gated_ref[:, span] = (gate_ref[:, span].astype(F32) * mixed.astype(F32)).astype(BF16)
        prev_real, prev_imag = real, imag


def run_mix(filters, kv, prior, gate, forward, backward):
    chan, seq_len = kv.shape
    taps = filters.shape[1]
    group = min(256, chan)
    rows = lambda width: pl.BlockSpec((group, width), lambda g: (g, 0))
    whole = lambda array: pl.BlockSpec(array.shape, lambda g: (0, 0))
    return pl.pallas_call(
        mix_kernel,
        grid=(chan // group,),
        in_specs=[rows(taps), rows(seq_len), rows(taps), rows(seq_len), whole(forward), whole(backward)],
        out_specs=[rows(seq_len), rows(seq_len)],
        out_shape=[jax.ShapeDtypeStruct((chan, seq_len), BF16)] * 2,
        compiler_params=pltpu.CompilerParams(vmem_limit_bytes=VMEM),
        cost_estimate=pl.CostEstimate(
            flops=14 * chan * seq_len * 2 * taps, bytes_accessed=8 * chan * seq_len, transcendentals=0
        ),
        name="mix_kernel",
    )(filters, kv, prior, gate, forward, backward)


def weight_kernel(place_ref, g00, g01, g10, g11, left_ref, right_ref, *refs):
    added, (send_a, keep_a, send_b, keep_b) = refs[:-4], refs[-4:]
    rows = g00.shape[0]
    stack = jnp.concatenate([g01[...], g11[...], g00[...], g10[...]], axis=0)
    contract = (((1,), (1,)), ((), ()))
    left = lax.dot_general(stack, left_ref[...], contract, preferred_element_type=F32)
    diag = left[rows : 2 * rows]
    for piece in added[0::2]:
        diag = diag + piece[...].astype(F32)
    send_a[0] = left[:rows].astype(BF16)
    send_a[1] = diag.astype(BF16)
    keep_a[0] = left[2 * rows : 3 * rows].astype(BF16)
    keep_a[1] = left[3 * rows :].astype(BF16)
    right = lax.dot_general(stack, right_ref[...], contract, preferred_element_type=F32)
    diag = right[rows : 2 * rows]
    for piece in added[1::2]:
        diag = diag + piece[...].astype(F32)
    send_b[0] = right[3 * rows :].astype(BF16)
    send_b[1] = diag.astype(BF16)
    keep_b[0] = right[2 * rows : 3 * rows].astype(BF16)
    keep_b[1] = right[:rows].astype(BF16)


def direct_kernel(place_ref, g00, g01, g10, g11, gated_ref, keep, send_x, send_y, send_z):
    rows = g00.shape[0]
    stack = jnp.concatenate([g00[...], g01[...], g10[...], g11[...]], axis=0)
    both = lax.dot_general(stack, gated_ref[...], (((1,), (1,)), ((), ())), preferred_element_type=F32)
    for k, ref in enumerate((keep, send_x, send_y, send_z)):
        ref[...] = both[k * rows : (k + 1) * rows].astype(BF16)


def run_weight(place, grad_full, gated, rows, direct, added=()):
    chan, seq_len = gated.shape
    width = chan // 4
    grad_spec = lambda k: pl.BlockSpec((rows, seq_len), lambda n, place: (place[k], 0))
    gated_spec = lambda first: pl.BlockSpec((width, seq_len), lambda n, place: (n + first, 0))
    added_spec = lambda first: pl.BlockSpec((rows, width), lambda n, place: (0, n + first))
    grads = [grad_spec(k) for k in range(4)]
    if direct:
        kernel, steps, in_specs, operands = direct_kernel, 4, grads + [gated_spec(0)], [gated]
        out_spec = pl.BlockSpec((rows, width), lambda n, place: (0, n))
        out_shape = jax.ShapeDtypeStruct((rows, chan), BF16)
    else:
        kernel, steps, in_specs, operands = weight_kernel, 2, grads + [gated_spec(0), gated_spec(2)], [gated, gated]
        for piece in added:
            in_specs += [added_spec(0), added_spec(2)]
            operands += [piece, piece]
        out_spec = pl.BlockSpec((2, rows, width), lambda n, place: (0, 0, n))
        out_shape = jax.ShapeDtypeStruct((2, rows, chan // 2), BF16)
    return pl.pallas_call(
        kernel,
        grid_spec=pltpu.PrefetchScalarGridSpec(
            num_scalar_prefetch=1, grid=(steps,), in_specs=in_specs, out_specs=[out_spec] * 4
        ),
        out_shape=[out_shape] * 4,
        compiler_params=pltpu.CompilerParams(vmem_limit_bytes=VMEM),
        cost_estimate=pl.CostEstimate(
            flops=8 * rows * chan * seq_len,
            bytes_accessed=2 * (4 * rows * (seq_len + chan) + chan * seq_len),
            transcendentals=0,
        ),
        name="weight_kernel",
    )(place, grad_full, grad_full, grad_full, grad_full, *operands)


def product_kernel(count, place_ref, grad_hbm, *refs):
    pieces = refs[:count]
    mixed_ref, gate_ref, kv_ref, prior_ref, filt_ref, forward_ref, backward_ref = refs[count : count + 7]
    gate_grad_ref, kv_grad_ref, last_ref, head_ref, filt_grad_ref, conv, grad, sems = refs[-8:]
    step = pl.program_id(0)
    rows = pieces[0].shape[1]

    @pl.when(step == 0)
    def _():
        copies = [
            pltpu.make_async_copy(
                grad_hbm.at[pl.ds(pl.multiple_of(place_ref[k] * rows, rows), rows)],
                grad.at[pl.ds(k * rows, rows)],
                sems.at[k],
            )
            for k in range(count)
        ]
        for copy in copies:
            copy.start()
        for copy in copies:
            copy.wait()

    wide = [piece[...] for piece in pieces]
    total = jnp.dot(jnp.concatenate(wide, axis=1), grad[...], preferred_element_type=F32)
    gate_grad_ref[...] = total * mixed_ref[...].astype(F32)
    conv[...] = (total * gate_ref[...].astype(F32)).astype(BF16)

    group, taps = filt_ref.shape
    blocks = kv_ref.shape[1] // taps
    forward, backward = forward_ref[...], backward_ref[...]
    first, sign = lane_facts(taps)
    sign_imag = jnp.where(first, 1.0, sign)
    part = min(256, group)
    for at in range(0, group, part):
        chans = slice(at, at + part)
        h_real, h_last, h_imag = filter_spectrum(filt_ref[chans, :], forward, first)

        def pull_back(win_real, win_imag):
            return inverse(
                h_real * win_real + h_imag * win_imag, h_last * win_imag - h_imag * win_real, backward
            )

        past_real, past_imag = spectrum(prior_ref[chans, :], forward)
        g_real = g_imag = sum_real = sum_imag = 0.0
        for b in range(blocks):
            span = slice(b * taps, (b + 1) * taps)
            now_real, now_imag = spectrum(conv[chans, span], forward)
            back = pull_back(g_real + sign * now_real, g_imag + sign_imag * now_imag).astype(BF16)
            if b == 0:
                head_ref[chans, :] = back
            else:
                kv_grad_ref[chans, (b - 1) * taps : b * taps] = back
            x_real, x_imag = spectrum(kv_ref[chans, span], forward)
            win_real = x_real + sign * past_real
            win_imag = x_imag + sign_imag * past_imag
            win_last, win_skew = jnp.where(first, win_imag, win_real), jnp.where(first, 0.0, win_imag)
            sum_real = sum_real + now_real * win_real + now_imag * win_skew
            sum_imag = sum_imag + now_imag * win_last - now_real * win_skew
            g_real, g_imag = now_real, now_imag
            past_real, past_imag = x_real, x_imag
        last = pull_back(g_real, g_imag)
        last_ref[chans, :] = last
        kv_grad_ref[chans, (blocks - 1) * taps :] = last.astype(BF16)
        filt_grad_ref[chans, :] = inverse(sum_real, sum_imag, backward)


def run_product(part, place, grad_full, pieces, mixed, gate, kv, prior, filters, forward, backward, written):
    chan, seq_len = mixed.shape
    taps = filters.shape[1]
    depth = grad_full.shape[0]
    rows = pieces[0].shape[1]
    count = len(pieces)
    group = min(512, chan // PARTS)
    steps = chan // PARTS // group
    offset = part * steps
    local_offset = offset % (chan // 2 // group)
    full = lambda width: pl.BlockSpec((group, width), lambda m, place: (m + offset, 0))
    local = pl.BlockSpec((group, rows), lambda m, place: (m + local_offset, 0))
    whole = lambda array: pl.BlockSpec(array.shape, lambda m, place: (0, 0))
    anywhere = pl.BlockSpec(memory_space=pl.ANY)
    return pl.pallas_call(
        lambda *refs: product_kernel(count, *refs),
        grid_spec=pltpu.PrefetchScalarGridSpec(
            num_scalar_prefetch=1,
            grid=(steps,),
            in_specs=[anywhere]
            + [local if piece.shape[0] < chan else full(rows) for piece in pieces]
            + [full(seq_len), full(seq_len), full(seq_len), full(taps), full(taps)]
            + [whole(forward), whole(backward)]
            + [anywhere] * len(written),
            out_specs=[full(seq_len), full(seq_len), full(taps), full(taps), full(taps)],
            scratch_shapes=[
                pltpu.VMEM((group, seq_len), BF16),
                pltpu.VMEM((depth, seq_len), BF16),
                pltpu.SemaphoreType.DMA((count,)),
            ],
        ),
        out_shape=[
            jax.ShapeDtypeStruct((chan, seq_len), F32),
            jax.ShapeDtypeStruct((chan, seq_len), BF16),
            jax.ShapeDtypeStruct((chan, taps), F32),
            jax.ShapeDtypeStruct((chan, taps), BF16),
            jax.ShapeDtypeStruct((chan, taps), F32),
        ],
        input_output_aliases={9 + count + k: k for k in range(len(written))},
        compiler_params=pltpu.CompilerParams(vmem_limit_bytes=VMEM),
        cost_estimate=pl.CostEstimate(
            flops=2 * group * steps * seq_len * (depth + 16 * taps),
            bytes_accessed=2 * depth * (seq_len + group * steps) + 12 * group * steps * seq_len,
            transcendentals=0,
        ),
        name="product_kernel",
    )(place, grad_full, *pieces, mixed, gate, kv, prior, filters, forward, backward, *written)


def after(array, *earlier):
    return lax.optimization_barrier((array,) + earlier)[0] if earlier else array


class Layout:
    def __init__(self):
        self.count = lax.axis_size("ctx")
        self.depth = self.count // 4
        index = lax.axis_index("ctx")
        self.z, self.y, self.x = index // 4, (index // 2) % 2, index % 2
        self.pairs_x = [(i, i ^ 1) for i in range(self.count)]
        self.pairs_y = [(i, i ^ 2) for i in range(self.count)]

    def pairs_z(self, by):
        return [(i, (i + 4 * by) % self.count) for i in range(self.count)]

    def places(self, by):
        base = 4 * ((self.z + by) % self.depth)
        return [base + 2 * (self.y ^ dy) + (self.x ^ dx) for dy in range(2) for dx in range(2)]


class Stages:
    def __init__(self, at):
        self.at = at
        self.arrived = [()] * 3
        self.now = []
        self.ready = self.next_ready = ()
        self.back = 2

    def advance(self):
        self.arrived.append(tuple(self.now))
        self.now, self.ready, self.next_ready = [], self.next_ready, ()

    def hold(self, array):
        return after(array, *self.arrived[-2])

    def finished(self, *arrays):
        self.next_ready += arrays

    def send(self, array, pairs, *earlier):
        got = lax.ppermute(after(array, *self.arrived[-self.back], *self.ready, *earlier), "ctx", pairs)
        self.now.append(got)
        return got

    def swap_x(self, array, *earlier):
        return self.send(array, self.at.pairs_x, *earlier)

    def swap_y(self, array, *earlier):
        return self.send(array, self.at.pairs_y, *earlier)


def pick(bit, array, axis):
    halves = [lax.index_in_dim(array, k, axis, keepdims=False) for k in range(2)]
    return jnp.where(bit == 0, halves[0], halves[1])


def ordered(bit, mine, other):
    return jnp.stack([jnp.where(bit == 0, mine, other), jnp.where(bit == 0, other, mine)])


def reduce_filters(at, part, chan_count):
    taps = part.shape[1]
    part = part.reshape(at.depth, 2, 2, chan_count, taps)
    first = None
    for bit, pairs, axis in ((at.x, at.pairs_x, 2), (at.y, at.pairs_y, 1)):
        got = lax.ppermute(pick(1 - bit, part, axis).astype(BF16), "ctx", pairs)
        first = got if first is None else first
        part = pick(bit, part, axis) + got.astype(F32)
    at_z = lambda by: lax.dynamic_index_in_dim(part, (at.z + by) % at.depth, 0, keepdims=False)
    total = at_z(0)
    for by in range(1, at.depth):
        total = total + lax.ppermute(at_z(by), "ctx", at.pairs_z(by))
    return total, first


def on_device(out_grad, gate_values, kv_product, w_out, filters):
    at = Layout()
    stages = Stages(at)
    chan_count = filters.shape[2]
    taps = filters.shape[3]
    seq_len = out_grad.shape[1]
    rows, chan = w_out.shape
    half = chan // 2
    norm_scale = 1.0 / math.sqrt(at.count * seq_len)
    to_right = [(i, i + 1) for i in range(at.count - 1)]
    to_left = [(i + 1, i) for i in range(at.count - 1)]
    forward, backward = (jnp.asarray(m) for m in dft_matrices(taps))

    grad_full = lax.all_gather(out_grad, "fsdp", axis=0, tiled=True)

    near = sorted(range(at.depth), key=lambda d: min(d, at.depth - d))
    far = near[::-1]
    own, own_filters = w_out.T, filters.reshape(chan_count, taps)
    filters_x = lax.ppermute(own_filters, "ctx", at.pairs_x)
    pair = ordered(at.x, own_filters, filters_x)
    filters_y = lax.ppermute(pair, "ctx", at.pairs_y)
    plane = ordered(at.y, pair, filters_y)
    depth = at.depth
    shards = {0: own}
    ring = {0: plane}
    beside = {1, depth - 1} if depth > 2 else set()

    def step_z(held, by, *earlier):
        way = 1 if by <= depth // 2 else -1
        return lax.ppermute(after(held[(by - way) % depth], *earlier), "ctx", at.pairs_z(way))

    before = filters_y
    for by in near[1:]:
        shards[by] = before = step_z(shards, by, before)
    for way in near[1:]:
        ring[way] = step_z(ring, way, shards[near[min(2, depth - 1)] if way not in beside and depth > 2 else near[1]])
    ring = [ring[by] for by in range(depth - 1, 0, -1)]
    shards = [shards[by] for by in near]
    ring = jnp.stack((ring + [plane]) * 2)
    ring = lax.dynamic_slice_in_dim(ring, depth - 1 - at.z, depth, axis=0)
    all_filters = ring.reshape(chan, taps)
    prior = lax.ppermute(after(kv_product[:, seq_len - taps :], filters_y), "ctx", to_right)

    from_x, from_y, diag_a, diag_b = {}, {}, {}, {}
    kept, carried, crossed, last_sent = {}, {}, [], []
    mixed = gated = products = w_grad = None

    def gather_first(k):
        both = (from_x[0], from_y[0], prior) if k == 1 else ()
        from_x[k] = stages.swap_x(shards[k], *both)
        from_y[k] = stages.swap_y(shards[k], *both)

    def gather_second(k):
        if near[k] in beside:
            pairs = at.pairs_z(1 if near[k] == 1 else -1)
            diag_a[k] = lax.ppermute(diag_a[0], "ctx", pairs)
            diag_b[k] = lax.ppermute(diag_b[0], "ctx", pairs)
            stages.finished(diag_a[k], diag_b[k])
        else:
            diag_a[k] = stages.swap_x(from_y[k][:half])
            diag_b[k] = stages.swap_y(from_x[k][half:])

    def mix():
        nonlocal mixed, gated
        mixed, gated = run_mix(all_filters, stages.hold(kv_product), prior, gate_values, forward, backward)
        stages.finished(mixed)

    def weight_part(k):
        place = jnp.stack(at.places(far[k])).astype(jnp.int32)
        added = crossed if far[k] == 0 else ()
        kept[k] = run_weight(place, grad_full, stages.hold(gated), rows, far[k] in beside, added)
        stages.finished(kept[k][0])

    def reduce_first(k):
        by = far[k]
        if by in beside:
            keep, send_x, send_y, send_z = kept[k]
            kept[k] = (keep, stages.swap_x(send_x), stages.swap_y(send_y))
            crossed.append(lax.ppermute(send_z, "ctx", at.pairs_z(1 if by == 1 else -1)))
        else:
            send_a, keep_a, send_b, keep_b = kept[k]
            kept[k] = (keep_a, stages.swap_x(send_a), keep_b, stages.swap_y(send_b))
            if by == 0:
                last_sent.extend((kept[k][1], kept[k][3]))

    def reduce_second(k):
        if far[k] in beside:
            return
        keep_a, got_a, keep_b, got_b = kept[k]
        next_a = (keep_a[1].astype(F32) + got_a[1].astype(F32)).astype(BF16)
        next_b = (keep_b[1].astype(F32) + got_b[1].astype(F32)).astype(BF16)
        kept[k] = (keep_a, got_a, stages.swap_y(next_a), keep_b, got_b, stages.swap_x(next_b))

    def reduce_third(k):
        nonlocal w_grad
        by = far[k]
        if by in beside:
            joint = sum(piece.astype(F32) for piece in kept.pop(k))
        else:
            keep_a, got_a, last_a, keep_b, got_b, last_b = kept.pop(k)
            sum_a = keep_a[0].astype(F32) + got_a[0].astype(F32) + last_a.astype(F32)
            sum_b = keep_b[0].astype(F32) + got_b[0].astype(F32) + last_b.astype(F32)
            joint = jnp.concatenate([sum_a, sum_b], axis=1)
        for piece in carried.pop(by, ()):
            joint = joint + piece.astype(F32)
        if by == 0:
            w_grad = joint * norm_scale
            return
        way = 1 if by <= depth // 2 else -1
        got = lax.ppermute(joint.astype(BF16), "ctx", at.pairs_z(way))
        carried.setdefault((by - way) % depth, []).append(got)
        if k < Z_PINNED:
            stages.finished(got)

    def product(part):
        nonlocal products
        diag = diag_a if 2 * part < PARTS else diag_b
        pieces = [p for k in range(depth) for p in (shards[k], from_x[k], from_y[k], diag[k])]
        places = jnp.stack([c for by in near for c in at.places(-by)]).astype(jnp.int32)
        products = run_product(
            part, places, grad_full, pieces, stages.hold(mixed), gate_values, kv_product, prior,
            all_filters, forward, backward, products or (),
        )
        stages.finished(products[3])

    late = depth - 4
    plan = {}

    def at_stage(stage, action, k):
        plan.setdefault(stage, []).append((action, k))

    at_stage(MIX_STAGE, lambda _: mix(), 0)
    for k in range(depth):
        more = max(0, k - 3)
        at_stage(WEIGHT_STAGE[min(k, 3)] + more + late, weight_part, k)
    for k in range(depth):
        at_stage(THIRD_STAGE[min(k, 3)] + max(0, k - 3) + late, reduce_third, k)
    for part in range(PARTS):
        at_stage(PRODUCT_STAGE[part] + 2 * late, lambda p: product(p), part)
    for k in range(depth):
        more = max(0, k - 3)
        at_stage(k, gather_first, k)
        at_stage(GATHER_SECOND[min(k, 3)] + more, gather_second, k)
        at_stage(REDUCE_FIRST[min(k, 3)] + more + late, reduce_first, k)
        at_stage(REDUCE_SECOND[min(k, 3)] + more + late, reduce_second, k)
    for stage in range(max(plan) + 1):
        if stage >= CLOSE_STAGE + 2 * late:
            stages.back = 1
        for action, k in plan.get(stage, []):
            action(k)
        stages.advance()

    gate_grad, kv_grad, last, head, filt_part = products
    filter_grad, crossed_x = reduce_filters(at, after(filt_part, *last_sent), chan_count)
    filter_grad = filter_grad * norm_scale
    tail = lax.ppermute(after(head, crossed_x), "ctx", to_left)
    kv_grad = lax.dynamic_update_slice(
        kv_grad, (last + tail.astype(F32)).astype(BF16), (0, seq_len - taps)
    )
    return (gate_grad, kv_grad, filter_grad.reshape(filters.shape), w_grad)


def solution(mesh):
    in_specs = (
        P("fsdp", "ctx"),
        P("fsdp", "ctx"),
        P("fsdp", "ctx"),
        P("ctx", "fsdp"),
        P("fsdp", "ctx", None, None),
    )
    out_specs = (P("fsdp", "ctx"), P("fsdp", "ctx"), P("fsdp", "ctx", None, None), P("ctx", "fsdp"))
    return jax.shard_map(
        on_device, mesh=mesh, in_specs=in_specs, out_specs=out_specs, check_vma=False
    )
```

```python
import math

import jax
import jax.numpy as jnp
import ml_dtypes
import numpy as np
from jax import lax
from jax.experimental import pallas as pl
from jax.experimental.pallas import tpu as pltpu
from jax.sharding import PartitionSpec as P

F32 = jnp.float32
BF16 = jnp.bfloat16
VMEM = 58 * 1024 * 1024
MIX_STAGE = 2
WEIGHT_STAGE = (2, 3, 4, 6)
THIRD_STAGE = (7, 7, 8, 9)
PRODUCT_STAGE = (6, 7)
GATHER_SECOND = (2, 3, 4, 5)
REDUCE_FIRST = (4, 5, 5, 7)
REDUCE_SECOND = (6, 6, 6, 8)
CLOSE_STAGE = 8
Z_PINNED = 2
PARTS = 2


def split_pair(matrix):
    high = matrix.astype(ml_dtypes.bfloat16)
    low = (matrix - high.astype(np.float64)).astype(ml_dtypes.bfloat16)
    return high, low


def dft_matrices(taps):
    points = 2 * taps
    place = np.arange(taps)
    angle = 2.0 * np.pi * ((place[:, None] * place[None, :]) % points) / points
    turn = (-1.0) ** place
    forward = np.concatenate([np.cos(angle), -np.sin(angle)], axis=1)
    forward[:, taps] = turn
    weight = np.full((taps, 1), 2.0 / points)
    weight[0] = 1.0 / points
    backward = np.concatenate([weight * np.cos(angle), -weight * np.sin(angle)], axis=0)
    backward[taps, :] = turn / points
    forward = np.concatenate(split_pair(forward), axis=0)
    backward = np.concatenate(split_pair(backward), axis=1)
    return forward, backward


def spectrum(block, forward):
    taps = block.shape[1]
    both = jnp.dot(jnp.concatenate([block, block], axis=1), forward, preferred_element_type=F32)
    return both[:, :taps], both[:, taps:]


def inverse(real, imag, backward):
    taps = real.shape[1]
    whole = jnp.concatenate([real, imag], axis=1)
    high = whole.astype(BF16)
    low = (whole - high.astype(F32)).astype(BF16)
    both = jnp.dot(high, backward, preferred_element_type=F32)
    rest = jnp.dot(low, backward[:, :taps], preferred_element_type=F32)
    return both[:, :taps] + both[:, taps:] + rest


def lane_facts(taps):
    lane = lax.broadcasted_iota(jnp.int32, (1, taps), 1)
    sign = jnp.where(lane % 2 == 0, 1.0, -1.0)
    return lane == 0, sign


def filter_spectrum(filt, forward, first):
    real, imag = spectrum(filt, forward)
    return real, jnp.where(first, imag, real), jnp.where(first, 0.0, imag)


def mix_kernel(filt_ref, kv_ref, prior_ref, gate_ref, forward_ref, backward_ref, mixed_ref, gated_ref):
    taps = filt_ref.shape[1]
    blocks = kv_ref.shape[1] // taps
    forward, backward = forward_ref[...], backward_ref[...]
    first, sign = lane_facts(taps)
    sign_imag = jnp.where(first, 1.0, sign)
    h_real, h_last, h_imag = filter_spectrum(filt_ref[...], forward, first)
    prev_real, prev_imag = spectrum(prior_ref[...], forward)
    for b in range(blocks):
        span = slice(b * taps, (b + 1) * taps)
        real, imag = spectrum(kv_ref[:, span], forward)
        win_real = real + sign * prev_real
        win_imag = imag + sign_imag * prev_imag
        mixed = inverse(
            h_real * win_real - h_imag * win_imag, h_last * win_imag + h_imag * win_real, backward
        ).astype(BF16)
        mixed_ref[:, span] = mixed
        gated_ref[:, span] = (gate_ref[:, span].astype(F32) * mixed.astype(F32)).astype(BF16)
        prev_real, prev_imag = real, imag


def run_mix(filters, kv, prior, gate, forward, backward):
    chan, seq_len = kv.shape
    taps = filters.shape[1]
    group = min(256, chan)
    rows = lambda width: pl.BlockSpec((group, width), lambda g: (g, 0))
    whole = lambda array: pl.BlockSpec(array.shape, lambda g: (0, 0))
    return pl.pallas_call(
        mix_kernel,
        grid=(chan // group,),
        in_specs=[rows(taps), rows(seq_len), rows(taps), rows(seq_len), whole(forward), whole(backward)],
        out_specs=[rows(seq_len), rows(seq_len)],
        out_shape=[jax.ShapeDtypeStruct((chan, seq_len), BF16)] * 2,
        compiler_params=pltpu.CompilerParams(vmem_limit_bytes=VMEM),
        cost_estimate=pl.CostEstimate(
            flops=14 * chan * seq_len * 2 * taps, bytes_accessed=8 * chan * seq_len, transcendentals=0
        ),
        name="mix_kernel",
    )(filters, kv, prior, gate, forward, backward)


def weight_kernel(place_ref, g00, g01, g10, g11, left_ref, right_ref, *refs):
    added, (send_a, keep_a, send_b, keep_b) = refs[:-4], refs[-4:]
    rows = g00.shape[0]
    stack = jnp.concatenate([g01[...], g11[...], g00[...], g10[...]], axis=0)
    contract = (((1,), (1,)), ((), ()))
    left = lax.dot_general(stack, left_ref[...], contract, preferred_element_type=F32)
    diag = left[rows : 2 * rows]
    for piece in added[0::2]:
        diag = diag + piece[...].astype(F32)
    send_a[0] = left[:rows].astype(BF16)
    send_a[1] = diag.astype(BF16)
    keep_a[0] = left[2 * rows : 3 * rows].astype(BF16)
    keep_a[1] = left[3 * rows :].astype(BF16)
    right = lax.dot_general(stack, right_ref[...], contract, preferred_element_type=F32)
    diag = right[rows : 2 * rows]
    for piece in added[1::2]:
        diag = diag + piece[...].astype(F32)
    send_b[0] = right[3 * rows :].astype(BF16)
    send_b[1] = diag.astype(BF16)
    keep_b[0] = right[2 * rows : 3 * rows].astype(BF16)
    keep_b[1] = right[:rows].astype(BF16)


def direct_kernel(place_ref, g00, g01, g10, g11, gated_ref, keep, send_x, send_y, send_z):
    rows = g00.shape[0]
    stack = jnp.concatenate([g00[...], g01[...], g10[...], g11[...]], axis=0)
    both = lax.dot_general(stack, gated_ref[...], (((1,), (1,)), ((), ())), preferred_element_type=F32)
    for k, ref in enumerate((keep, send_x, send_y, send_z)):
        ref[...] = both[k * rows : (k + 1) * rows].astype(BF16)


def run_weight(place, grad_full, gated, rows, direct, added=()):
    chan, seq_len = gated.shape
    width = chan // 4
    grad_spec = lambda k: pl.BlockSpec((rows, seq_len), lambda n, place: (place[k], 0))
    gated_spec = lambda first: pl.BlockSpec((width, seq_len), lambda n, place: (n + first, 0))
    added_spec = lambda first: pl.BlockSpec((rows, width), lambda n, place: (0, n + first))
    grads = [grad_spec(k) for k in range(4)]
    if direct:
        kernel, steps, in_specs, operands = direct_kernel, 4, grads + [gated_spec(0)], [gated]
        out_spec = pl.BlockSpec((rows, width), lambda n, place: (0, n))
        out_shape = jax.ShapeDtypeStruct((rows, chan), BF16)
    else:
        kernel, steps, in_specs, operands = weight_kernel, 2, grads + [gated_spec(0), gated_spec(2)], [gated, gated]
        for piece in added:
            in_specs += [added_spec(0), added_spec(2)]
            operands += [piece, piece]
        out_spec = pl.BlockSpec((2, rows, width), lambda n, place: (0, 0, n))
        out_shape = jax.ShapeDtypeStruct((2, rows, chan // 2), BF16)
    return pl.pallas_call(
        kernel,
        grid_spec=pltpu.PrefetchScalarGridSpec(
            num_scalar_prefetch=1, grid=(steps,), in_specs=in_specs, out_specs=[out_spec] * 4
        ),
        out_shape=[out_shape] * 4,
        compiler_params=pltpu.CompilerParams(vmem_limit_bytes=VMEM),
        cost_estimate=pl.CostEstimate(
            flops=8 * rows * chan * seq_len,
            bytes_accessed=2 * (4 * rows * (seq_len + chan) + chan * seq_len),
            transcendentals=0,
        ),
        name="weight_kernel",
    )(place, grad_full, grad_full, grad_full, grad_full, *operands)


def product_kernel(count, place_ref, grad_hbm, *refs):
    pieces = refs[:count]
    mixed_ref, gate_ref, kv_ref, prior_ref, filt_ref, forward_ref, backward_ref = refs[count : count + 7]
    gate_grad_ref, kv_grad_ref, last_ref, head_ref, filt_grad_ref, conv, grad, sems = refs[-8:]
    step = pl.program_id(0)
    rows = pieces[0].shape[1]

    @pl.when(step == 0)
    def _():
        copies = [
            pltpu.make_async_copy(
                grad_hbm.at[pl.ds(pl.multiple_of(place_ref[k] * rows, rows), rows)],
                grad.at[pl.ds(k * rows, rows)],
                sems.at[k],
            )
            for k in range(count)
        ]
        for copy in copies:
            copy.start()
        for copy in copies:
            copy.wait()

    wide = [piece[...] for piece in pieces]
    total = jnp.dot(jnp.concatenate(wide, axis=1), grad[...], preferred_element_type=F32)
    gate_grad_ref[...] = total * mixed_ref[...].astype(F32)
    conv[...] = (total * gate_ref[...].astype(F32)).astype(BF16)

    group, taps = filt_ref.shape
    blocks = kv_ref.shape[1] // taps
    forward, backward = forward_ref[...], backward_ref[...]
    first, sign = lane_facts(taps)
    sign_imag = jnp.where(first, 1.0, sign)
    part = min(256, group)
    for at in range(0, group, part):
        chans = slice(at, at + part)
        h_real, h_last, h_imag = filter_spectrum(filt_ref[chans, :], forward, first)

        def pull_back(win_real, win_imag):
            return inverse(
                h_real * win_real + h_imag * win_imag, h_last * win_imag - h_imag * win_real, backward
            )

        past_real, past_imag = spectrum(prior_ref[chans, :], forward)
        g_real = g_imag = sum_real = sum_imag = 0.0
        for b in range(blocks):
            span = slice(b * taps, (b + 1) * taps)
            now_real, now_imag = spectrum(conv[chans, span], forward)
            back = pull_back(g_real + sign * now_real, g_imag + sign_imag * now_imag).astype(BF16)
            if b == 0:
                head_ref[chans, :] = back
            else:
                kv_grad_ref[chans, (b - 1) * taps : b * taps] = back
            x_real, x_imag = spectrum(kv_ref[chans, span], forward)
            win_real = x_real + sign * past_real
            win_imag = x_imag + sign_imag * past_imag
            win_last, win_skew = jnp.where(first, win_imag, win_real), jnp.where(first, 0.0, win_imag)
            sum_real = sum_real + now_real * win_real + now_imag * win_skew
            sum_imag = sum_imag + now_imag * win_last - now_real * win_skew
            g_real, g_imag = now_real, now_imag
            past_real, past_imag = x_real, x_imag
        last = pull_back(g_real, g_imag)
        last_ref[chans, :] = last
        kv_grad_ref[chans, (blocks - 1) * taps :] = last.astype(BF16)
        filt_grad_ref[chans, :] = inverse(sum_real, sum_imag, backward)


def run_product(part, place, grad_full, pieces, mixed, gate, kv, prior, filters, forward, backward, written):
    chan, seq_len = mixed.shape
    taps = filters.shape[1]
    depth = grad_full.shape[0]
    rows = pieces[0].shape[1]
    count = len(pieces)
    group = min(512, chan // PARTS)
    steps = chan // PARTS // group
    offset = part * steps
    local_offset = offset % (chan // 2 // group)
    full = lambda width: pl.BlockSpec((group, width), lambda m, place: (m + offset, 0))
    local = pl.BlockSpec((group, rows), lambda m, place: (m + local_offset, 0))
    whole = lambda array: pl.BlockSpec(array.shape, lambda m, place: (0, 0))
    anywhere = pl.BlockSpec(memory_space=pl.ANY)
    return pl.pallas_call(
        lambda *refs: product_kernel(count, *refs),
        grid_spec=pltpu.PrefetchScalarGridSpec(
            num_scalar_prefetch=1,
            grid=(steps,),
            in_specs=[anywhere]
            + [local if piece.shape[0] < chan else full(rows) for piece in pieces]
            + [full(seq_len), full(seq_len), full(seq_len), full(taps), full(taps)]
            + [whole(forward), whole(backward)]
            + [anywhere] * len(written),
            out_specs=[full(seq_len), full(seq_len), full(taps), full(taps), full(taps)],
            scratch_shapes=[
                pltpu.VMEM((group, seq_len), BF16),
                pltpu.VMEM((depth, seq_len), BF16),
                pltpu.SemaphoreType.DMA((count,)),
            ],
        ),
        out_shape=[
            jax.ShapeDtypeStruct((chan, seq_len), F32),
            jax.ShapeDtypeStruct((chan, seq_len), BF16),
            jax.ShapeDtypeStruct((chan, taps), F32),
            jax.ShapeDtypeStruct((chan, taps), BF16),
            jax.ShapeDtypeStruct((chan, taps), F32),
        ],
        input_output_aliases={9 + count + k: k for k in range(len(written))},
        compiler_params=pltpu.CompilerParams(vmem_limit_bytes=VMEM),
        cost_estimate=pl.CostEstimate(
            flops=2 * group * steps * seq_len * (depth + 16 * taps),
            bytes_accessed=2 * depth * (seq_len + group * steps) + 12 * group * steps * seq_len,
            transcendentals=0,
        ),
        name="product_kernel",
    )(place, grad_full, *pieces, mixed, gate, kv, prior, filters, forward, backward, *written)


def after(array, *earlier):
    return lax.optimization_barrier((array,) + earlier)[0] if earlier else array


class Layout:
    def __init__(self):
        self.count = lax.axis_size("ctx")
        self.depth = self.count // 4
        index = lax.axis_index("ctx")
        self.z, self.y, self.x = index // 4, (index // 2) % 2, index % 2
        self.pairs_x = [(i, i ^ 1) for i in range(self.count)]
        self.pairs_y = [(i, i ^ 2) for i in range(self.count)]

    def pairs_z(self, by):
        return [(i, (i + 4 * by) % self.count) for i in range(self.count)]

    def places(self, by):
        base = 4 * ((self.z + by) % self.depth)
        return [base + 2 * (self.y ^ dy) + (self.x ^ dx) for dy in range(2) for dx in range(2)]


class Stages:
    def __init__(self, at):
        self.at = at
        self.arrived = [()] * 3
        self.now = []
        self.ready = self.next_ready = ()
        self.back = 2

    def advance(self):
        self.arrived.append(tuple(self.now))
        self.now, self.ready, self.next_ready = [], self.next_ready, ()

    def hold(self, array):
        return after(array, *self.arrived[-2])

    def finished(self, *arrays):
        self.next_ready += arrays

    def send(self, array, pairs, *earlier):
        got = lax.ppermute(after(array, *self.arrived[-self.back], *self.ready, *earlier), "ctx", pairs)
        self.now.append(got)
        return got

    def swap_x(self, array, *earlier):
        return self.send(array, self.at.pairs_x, *earlier)

    def swap_y(self, array, *earlier):
        return self.send(array, self.at.pairs_y, *earlier)


def pick(bit, array, axis):
    halves = [lax.index_in_dim(array, k, axis, keepdims=False) for k in range(2)]
    return jnp.where(bit == 0, halves[0], halves[1])


def ordered(bit, mine, other):
    return jnp.stack([jnp.where(bit == 0, mine, other), jnp.where(bit == 0, other, mine)])


def reduce_filters(at, part, chan_count):
    taps = part.shape[1]
    part = part.reshape(at.depth, 2, 2, chan_count, taps)
    first = None
    for bit, pairs, axis in ((at.x, at.pairs_x, 2), (at.y, at.pairs_y, 1)):
        got = lax.ppermute(pick(1 - bit, part, axis).astype(BF16), "ctx", pairs)
        first = got if first is None else first
        part = pick(bit, part, axis) + got.astype(F32)
    at_z = lambda by: lax.dynamic_index_in_dim(part, (at.z + by) % at.depth, 0, keepdims=False)
    total = at_z(0)
    for by in range(1, at.depth):
        total = total + lax.ppermute(at_z(by), "ctx", at.pairs_z(by))
    return total, first


def on_device(out_grad, gate_values, kv_product, w_out, filters):
    at = Layout()
    stages = Stages(at)
    chan_count = filters.shape[2]
    taps = filters.shape[3]
    seq_len = out_grad.shape[1]
    rows, chan = w_out.shape
    half = chan // 2
    norm_scale = 1.0 / math.sqrt(at.count * seq_len)
    to_right = [(i, i + 1) for i in range(at.count - 1)]
    to_left = [(i + 1, i) for i in range(at.count - 1)]
    forward, backward = (jnp.asarray(m) for m in dft_matrices(taps))

    grad_full = lax.all_gather(out_grad, "fsdp", axis=0, tiled=True)

    near = sorted(range(at.depth), key=lambda d: min(d, at.depth - d))
    far = near[::-1]
    own, own_filters = w_out.T, filters.reshape(chan_count, taps)
    filters_x = lax.ppermute(own_filters, "ctx", at.pairs_x)
    pair = ordered(at.x, own_filters, filters_x)
    filters_y = lax.ppermute(pair, "ctx", at.pairs_y)
    plane = ordered(at.y, pair, filters_y)
    depth = at.depth
    shards = {0: own}
    ring = {0: plane}
    beside = {1, depth - 1} if depth > 2 else set()

    def step_z(held, by, *earlier):
        way = 1 if by <= depth // 2 else -1
        return lax.ppermute(after(held[(by - way) % depth], *earlier), "ctx", at.pairs_z(way))

    before = filters_y
    for by in near[1:]:
        shards[by] = before = step_z(shards, by, before)
    for way in near[1:]:
        ring[way] = step_z(ring, way, shards[near[min(1, depth - 1)] if way not in beside and depth > 2 else near[1]])
    ring = [ring[by] for by in range(depth - 1, 0, -1)]
    shards = [shards[by] for by in near]
    ring = jnp.stack((ring + [plane]) * 2)
    ring = lax.dynamic_slice_in_dim(ring, depth - 1 - at.z, depth, axis=0)
    all_filters = ring.reshape(chan, taps)
    prior = lax.ppermute(after(kv_product[:, seq_len - taps :], shards[1]), "ctx", to_right)

    from_x, from_y, diag_a, diag_b = {}, {}, {}, {}
    kept, carried, crossed, last_sent = {}, {}, [], []
    mixed = gated = products = w_grad = None

    def gather_first(k):
        both = (from_x[0], from_y[0]) if k == 1 else ()
        from_x[k] = stages.swap_x(shards[k], *both)
        from_y[k] = stages.swap_y(shards[k], *both)

    def gather_second(k):
        if near[k] in beside:
            pairs = at.pairs_z(1 if near[k] == 1 else -1)
            diag_a[k] = lax.ppermute(diag_a[0], "ctx", pairs)
            diag_b[k] = lax.ppermute(diag_b[0], "ctx", pairs)
            stages.finished(diag_a[k], diag_b[k])
        else:
            diag_a[k] = stages.swap_x(from_y[k][:half])
            diag_b[k] = stages.swap_y(from_x[k][half:])

    def mix():
        nonlocal mixed, gated
        mixed, gated = run_mix(all_filters, stages.hold(kv_product), prior, gate_values, forward, backward)
        stages.finished(mixed)

    def weight_part(k):
        place = jnp.stack(at.places(far[k])).astype(jnp.int32)
        added = crossed if far[k] == 0 else ()
        kept[k] = run_weight(place, grad_full, stages.hold(gated), rows, far[k] in beside, added)
        stages.finished(kept[k][0])

    def reduce_first(k):
        by = far[k]
        if by in beside:
            keep, send_x, send_y, send_z = kept[k]
            behind = (diag_a[depth - 1], diag_b[depth - 1])
            kept[k] = (keep, stages.swap_x(send_x, *behind), stages.swap_y(send_y, *behind))
            crossed.append(lax.ppermute(send_z, "ctx", at.pairs_z(1 if by == 1 else -1)))
        else:
            send_a, keep_a, send_b, keep_b = kept[k]
            kept[k] = (keep_a, stages.swap_x(send_a), keep_b, stages.swap_y(send_b))
            if by == 0:
                last_sent.extend((kept[k][1], kept[k][3]))

    def reduce_second(k):
        if far[k] in beside:
            return
        keep_a, got_a, keep_b, got_b = kept[k]
        next_a = (keep_a[1].astype(F32) + got_a[1].astype(F32)).astype(BF16)
        next_b = (keep_b[1].astype(F32) + got_b[1].astype(F32)).astype(BF16)
        kept[k] = (keep_a, got_a, stages.swap_y(next_a), keep_b, got_b, stages.swap_x(next_b))

    def reduce_third(k):
        nonlocal w_grad
        by = far[k]
        if by in beside:
            joint = sum(piece.astype(F32) for piece in kept.pop(k))
        else:
            keep_a, got_a, last_a, keep_b, got_b, last_b = kept.pop(k)
            sum_a = keep_a[0].astype(F32) + got_a[0].astype(F32) + last_a.astype(F32)
            sum_b = keep_b[0].astype(F32) + got_b[0].astype(F32) + last_b.astype(F32)
            joint = jnp.concatenate([sum_a, sum_b], axis=1)
        for piece in carried.pop(by, ()):
            joint = joint + piece.astype(F32)
        if by == 0:
            w_grad = joint * norm_scale
            return
        way = 1 if by <= depth // 2 else -1
        got = lax.ppermute(joint.astype(BF16), "ctx", at.pairs_z(way))
        carried.setdefault((by - way) % depth, []).append(got)
        if k < Z_PINNED:
            stages.finished(got)

    def product(part):
        nonlocal products
        diag = diag_a if 2 * part < PARTS else diag_b
        pieces = [p for k in range(depth) for p in (shards[k], from_x[k], from_y[k], diag[k])]
        places = jnp.stack([c for by in near for c in at.places(-by)]).astype(jnp.int32)
        products = run_product(
            part, places, grad_full, pieces, stages.hold(mixed), gate_values, kv_product, prior,
            all_filters, forward, backward, products or (),
        )
        stages.finished(products[3])

    late = depth - 4
    plan = {}

    def at_stage(stage, action, k):
        plan.setdefault(stage, []).append((action, k))

    at_stage(MIX_STAGE, lambda _: mix(), 0)
    for k in range(depth):
        more = max(0, k - 3)
        at_stage(WEIGHT_STAGE[min(k, 3)] + more + late, weight_part, k)
    for k in range(depth):
        at_stage(THIRD_STAGE[min(k, 3)] + max(0, k - 3) + late, reduce_third, k)
    for part in range(PARTS):
        at_stage(PRODUCT_STAGE[part] + 2 * late, lambda p: product(p), part)
    for k in range(depth):
        more = max(0, k - 3)
        at_stage(k, gather_first, k)
        at_stage(GATHER_SECOND[min(k, 3)] + more, gather_second, k)
    for k in range(depth):
        more = max(0, k - 3)
        at_stage(REDUCE_FIRST[min(k, 3)] + more + late, reduce_first, k)
        at_stage(REDUCE_SECOND[min(k, 3)] + more + late, reduce_second, k)
    for stage in range(max(plan) + 1):
        if stage >= CLOSE_STAGE + 2 * late:
            stages.back = 1
        for action, k in plan.get(stage, []):
            action(k)
        stages.advance()

    gate_grad, kv_grad, last, head, filt_part = products
    filter_grad, crossed_x = reduce_filters(at, after(filt_part, *last_sent), chan_count)
    filter_grad = filter_grad * norm_scale
    tail = lax.ppermute(head, "ctx", to_left)
    kv_grad = lax.dynamic_update_slice(
        kv_grad, (last + tail.astype(F32)).astype(BF16), (0, seq_len - taps)
    )
    return (gate_grad, kv_grad, filter_grad.reshape(filters.shape), w_grad)


def solution(mesh):
    in_specs = (
        P("fsdp", "ctx"),
        P("fsdp", "ctx"),
        P("fsdp", "ctx"),
        P("ctx", "fsdp"),
        P("fsdp", "ctx", None, None),
    )
    out_specs = (P("fsdp", "ctx"), P("fsdp", "ctx"), P("fsdp", "ctx", None, None), P("ctx", "fsdp"))
    return jax.shard_map(
        on_device, mesh=mesh, in_specs=in_specs, out_specs=out_specs, check_vma=False
    )
```

```python
import math

import jax
import jax.numpy as jnp
import ml_dtypes
import numpy as np
from jax import lax
from jax.experimental import pallas as pl
from jax.experimental.pallas import tpu as pltpu
from jax.sharding import PartitionSpec as P

F32 = jnp.float32
BF16 = jnp.bfloat16
VMEM = 58 * 1024 * 1024
MIX_STAGE = 2
WEIGHT_STAGE = (2, 3, 4, 6)
THIRD_STAGE = (7, 7, 8, 9)
PRODUCT_STAGE = (6, 7)
GATHER_SECOND = (2, 4, 4, 5)
REDUCE_FIRST = (4, 5, 5, 7)
REDUCE_SECOND = (6, 6, 6, 8)
CLOSE_STAGE = 8
Z_PINNED = 2
PARTS = 2


def split_pair(matrix):
    high = matrix.astype(ml_dtypes.bfloat16)
    low = (matrix - high.astype(np.float64)).astype(ml_dtypes.bfloat16)
    return high, low


def dft_matrices(taps):
    points = 2 * taps
    place = np.arange(taps)
    angle = 2.0 * np.pi * ((place[:, None] * place[None, :]) % points) / points
    turn = (-1.0) ** place
    forward = np.concatenate([np.cos(angle), -np.sin(angle)], axis=1)
    forward[:, taps] = turn
    weight = np.full((taps, 1), 2.0 / points)
    weight[0] = 1.0 / points
    backward = np.concatenate([weight * np.cos(angle), -weight * np.sin(angle)], axis=0)
    backward[taps, :] = turn / points
    forward = np.concatenate(split_pair(forward), axis=0)
    backward = np.concatenate(split_pair(backward), axis=1)
    return forward, backward


def spectrum(block, forward):
    taps = block.shape[1]
    both = jnp.dot(jnp.concatenate([block, block], axis=1), forward, preferred_element_type=F32)
    return both[:, :taps], both[:, taps:]


def inverse(real, imag, backward):
    taps = real.shape[1]
    whole = jnp.concatenate([real, imag], axis=1)
    high = whole.astype(BF16)
    low = (whole - high.astype(F32)).astype(BF16)
    both = jnp.dot(high, backward, preferred_element_type=F32)
    rest = jnp.dot(low, backward[:, :taps], preferred_element_type=F32)
    return both[:, :taps] + both[:, taps:] + rest


def lane_facts(taps):
    lane = lax.broadcasted_iota(jnp.int32, (1, taps), 1)
    sign = jnp.where(lane % 2 == 0, 1.0, -1.0)
    return lane == 0, sign


def filter_spectrum(filt, forward, first):
    real, imag = spectrum(filt, forward)
    return real, jnp.where(first, imag, real), jnp.where(first, 0.0, imag)


def mix_kernel(filt_ref, kv_ref, prior_ref, gate_ref, forward_ref, backward_ref, mixed_ref, gated_ref):
    taps = filt_ref.shape[1]
    blocks = kv_ref.shape[1] // taps
    forward, backward = forward_ref[...], backward_ref[...]
    first, sign = lane_facts(taps)
    sign_imag = jnp.where(first, 1.0, sign)
    h_real, h_last, h_imag = filter_spectrum(filt_ref[...], forward, first)
    prev_real, prev_imag = spectrum(prior_ref[...], forward)
    for b in range(blocks):
        span = slice(b * taps, (b + 1) * taps)
        real, imag = spectrum(kv_ref[:, span], forward)
        win_real = real + sign * prev_real
        win_imag = imag + sign_imag * prev_imag
        mixed = inverse(
            h_real * win_real - h_imag * win_imag, h_last * win_imag + h_imag * win_real, backward
        ).astype(BF16)
        mixed_ref[:, span] = mixed
        gated_ref[:, span] = (gate_ref[:, span].astype(F32) * mixed.astype(F32)).astype(BF16)
        prev_real, prev_imag = real, imag


def run_mix(filters, kv, prior, gate, forward, backward):
    chan, seq_len = kv.shape
    taps = filters.shape[1]
    group = min(256, chan)
    rows = lambda width: pl.BlockSpec((group, width), lambda g: (g, 0))
    whole = lambda array: pl.BlockSpec(array.shape, lambda g: (0, 0))
    return pl.pallas_call(
        mix_kernel,
        grid=(chan // group,),
        in_specs=[rows(taps), rows(seq_len), rows(taps), rows(seq_len), whole(forward), whole(backward)],
        out_specs=[rows(seq_len), rows(seq_len)],
        out_shape=[jax.ShapeDtypeStruct((chan, seq_len), BF16)] * 2,
        compiler_params=pltpu.CompilerParams(vmem_limit_bytes=VMEM),
        cost_estimate=pl.CostEstimate(
            flops=14 * chan * seq_len * 2 * taps, bytes_accessed=8 * chan * seq_len, transcendentals=0
        ),
        name="mix_kernel",
    )(filters, kv, prior, gate, forward, backward)


def weight_kernel(place_ref, g00, g01, g10, g11, left_ref, right_ref, *refs):
    added, (send_a, keep_a, send_b, keep_b) = refs[:-4], refs[-4:]
    rows = g00.shape[0]
    stack = jnp.concatenate([g01[...], g11[...], g00[...], g10[...]], axis=0)
    contract = (((1,), (1,)), ((), ()))
    left = lax.dot_general(stack, left_ref[...], contract, preferred_element_type=F32)
    diag = left[rows : 2 * rows]
    for piece in added[0::2]:
        diag = diag + piece[...].astype(F32)
    send_a[0] = left[:rows].astype(BF16)
    send_a[1] = diag.astype(BF16)
    keep_a[0] = left[2 * rows : 3 * rows].astype(BF16)
    keep_a[1] = left[3 * rows :].astype(BF16)
    right = lax.dot_general(stack, right_ref[...], contract, preferred_element_type=F32)
    diag = right[rows : 2 * rows]
    for piece in added[1::2]:
        diag = diag + piece[...].astype(F32)
    send_b[0] = right[3 * rows :].astype(BF16)
    send_b[1] = diag.astype(BF16)
    keep_b[0] = right[2 * rows : 3 * rows].astype(BF16)
    keep_b[1] = right[:rows].astype(BF16)


def direct_kernel(place_ref, g00, g01, g10, g11, gated_ref, keep, send_x, send_y, send_z):
    rows = g00.shape[0]
    stack = jnp.concatenate([g00[...], g01[...], g10[...], g11[...]], axis=0)
    both = lax.dot_general(stack, gated_ref[...], (((1,), (1,)), ((), ())), preferred_element_type=F32)
    for k, ref in enumerate((keep, send_x, send_y, send_z)):
        ref[...] = both[k * rows : (k + 1) * rows].astype(BF16)


def run_weight(place, grad_full, gated, rows, direct, added=()):
    chan, seq_len = gated.shape
    width = chan // 4
    grad_spec = lambda k: pl.BlockSpec((rows, seq_len), lambda n, place: (place[k], 0))
    gated_spec = lambda first: pl.BlockSpec((width, seq_len), lambda n, place: (n + first, 0))
    added_spec = lambda first: pl.BlockSpec((rows, width), lambda n, place: (0, n + first))
    grads = [grad_spec(k) for k in range(4)]
    if direct:
        kernel, steps, in_specs, operands = direct_kernel, 4, grads + [gated_spec(0)], [gated]
        out_spec = pl.BlockSpec((rows, width), lambda n, place: (0, n))
        out_shape = jax.ShapeDtypeStruct((rows, chan), BF16)
    else:
        kernel, steps, in_specs, operands = weight_kernel, 2, grads + [gated_spec(0), gated_spec(2)], [gated, gated]
        for piece in added:
            in_specs += [added_spec(0), added_spec(2)]
            operands += [piece, piece]
        out_spec = pl.BlockSpec((2, rows, width), lambda n, place: (0, 0, n))
        out_shape = jax.ShapeDtypeStruct((2, rows, chan // 2), BF16)
    return pl.pallas_call(
        kernel,
        grid_spec=pltpu.PrefetchScalarGridSpec(
            num_scalar_prefetch=1, grid=(steps,), in_specs=in_specs, out_specs=[out_spec] * 4
        ),
        out_shape=[out_shape] * 4,
        compiler_params=pltpu.CompilerParams(vmem_limit_bytes=VMEM),
        cost_estimate=pl.CostEstimate(
            flops=8 * rows * chan * seq_len,
            bytes_accessed=2 * (4 * rows * (seq_len + chan) + chan * seq_len),
            transcendentals=0,
        ),
        name="weight_kernel",
    )(place, grad_full, grad_full, grad_full, grad_full, *operands)


def product_kernel(count, place_ref, grad_hbm, *refs):
    pieces = refs[:count]
    mixed_ref, gate_ref, kv_ref, prior_ref, filt_ref, forward_ref, backward_ref = refs[count : count + 7]
    gate_grad_ref, kv_grad_ref, last_ref, head_ref, filt_grad_ref, conv, grad, sems = refs[-8:]
    step = pl.program_id(0)
    rows = pieces[0].shape[1]

    @pl.when(step == 0)
    def _():
        copies = [
            pltpu.make_async_copy(
                grad_hbm.at[pl.ds(pl.multiple_of(place_ref[k] * rows, rows), rows)],
                grad.at[pl.ds(k * rows, rows)],
                sems.at[k],
            )
            for k in range(count)
        ]
        for copy in copies:
            copy.start()
        for copy in copies:
            copy.wait()

    wide = [piece[...] for piece in pieces]
    total = jnp.dot(jnp.concatenate(wide, axis=1), grad[...], preferred_element_type=F32)
    gate_grad_ref[...] = total * mixed_ref[...].astype(F32)
    conv[...] = (total * gate_ref[...].astype(F32)).astype(BF16)

    group, taps = filt_ref.shape
    blocks = kv_ref.shape[1] // taps
    forward, backward = forward_ref[...], backward_ref[...]
    first, sign = lane_facts(taps)
    sign_imag = jnp.where(first, 1.0, sign)
    part = min(256, group)
    for at in range(0, group, part):
        chans = slice(at, at + part)
        h_real, h_last, h_imag = filter_spectrum(filt_ref[chans, :], forward, first)

        def pull_back(win_real, win_imag):
            return inverse(
                h_real * win_real + h_imag * win_imag, h_last * win_imag - h_imag * win_real, backward
            )

        past_real, past_imag = spectrum(prior_ref[chans, :], forward)
        g_real = g_imag = sum_real = sum_imag = 0.0
        for b in range(blocks):
            span = slice(b * taps, (b + 1) * taps)
            now_real, now_imag = spectrum(conv[chans, span], forward)
            back = pull_back(g_real + sign * now_real, g_imag + sign_imag * now_imag).astype(BF16)
            if b == 0:
                head_ref[chans, :] = back
            else:
                kv_grad_ref[chans, (b - 1) * taps : b * taps] = back
            x_real, x_imag = spectrum(kv_ref[chans, span], forward)
            win_real = x_real + sign * past_real
            win_imag = x_imag + sign_imag * past_imag
            win_last, win_skew = jnp.where(first, win_imag, win_real), jnp.where(first, 0.0, win_imag)
            sum_real = sum_real + now_real * win_real + now_imag * win_skew
            sum_imag = sum_imag + now_imag * win_last - now_real * win_skew
            g_real, g_imag = now_real, now_imag
            past_real, past_imag = x_real, x_imag
        last = pull_back(g_real, g_imag)
        last_ref[chans, :] = last
        kv_grad_ref[chans, (blocks - 1) * taps :] = last.astype(BF16)
        filt_grad_ref[chans, :] = inverse(sum_real, sum_imag, backward)


def run_product(part, place, grad_full, pieces, mixed, gate, kv, prior, filters, forward, backward, written):
    chan, seq_len = mixed.shape
    taps = filters.shape[1]
    depth = grad_full.shape[0]
    rows = pieces[0].shape[1]
    count = len(pieces)
    group = min(512, chan // PARTS)
    steps = chan // PARTS // group
    offset = part * steps
    local_offset = offset % (chan // 2 // group)
    full = lambda width: pl.BlockSpec((group, width), lambda m, place: (m + offset, 0))
    local = pl.BlockSpec((group, rows), lambda m, place: (m + local_offset, 0))
    whole = lambda array: pl.BlockSpec(array.shape, lambda m, place: (0, 0))
    anywhere = pl.BlockSpec(memory_space=pl.ANY)
    return pl.pallas_call(
        lambda *refs: product_kernel(count, *refs),
        grid_spec=pltpu.PrefetchScalarGridSpec(
            num_scalar_prefetch=1,
            grid=(steps,),
            in_specs=[anywhere]
            + [local if piece.shape[0] < chan else full(rows) for piece in pieces]
            + [full(seq_len), full(seq_len), full(seq_len), full(taps), full(taps)]
            + [whole(forward), whole(backward)]
            + [anywhere] * len(written),
            out_specs=[full(seq_len), full(seq_len), full(taps), full(taps), full(taps)],
            scratch_shapes=[
                pltpu.VMEM((group, seq_len), BF16),
                pltpu.VMEM((depth, seq_len), BF16),
                pltpu.SemaphoreType.DMA((count,)),
            ],
        ),
        out_shape=[
            jax.ShapeDtypeStruct((chan, seq_len), F32),
            jax.ShapeDtypeStruct((chan, seq_len), BF16),
            jax.ShapeDtypeStruct((chan, taps), F32),
            jax.ShapeDtypeStruct((chan, taps), BF16),
            jax.ShapeDtypeStruct((chan, taps), F32),
        ],
        input_output_aliases={9 + count + k: k for k in range(len(written))},
        compiler_params=pltpu.CompilerParams(vmem_limit_bytes=VMEM),
        cost_estimate=pl.CostEstimate(
            flops=2 * group * steps * seq_len * (depth + 16 * taps),
            bytes_accessed=2 * depth * (seq_len + group * steps) + 12 * group * steps * seq_len,
            transcendentals=0,
        ),
        name="product_kernel",
    )(place, grad_full, *pieces, mixed, gate, kv, prior, filters, forward, backward, *written)


def after(array, *earlier):
    return lax.optimization_barrier((array,) + earlier)[0] if earlier else array


class Layout:
    def __init__(self):
        self.count = lax.axis_size("ctx")
        self.depth = self.count // 4
        index = lax.axis_index("ctx")
        self.z, self.y, self.x = index // 4, (index // 2) % 2, index % 2
        self.pairs_x = [(i, i ^ 1) for i in range(self.count)]
        self.pairs_y = [(i, i ^ 2) for i in range(self.count)]

    def pairs_z(self, by):
        return [(i, (i + 4 * by) % self.count) for i in range(self.count)]

    def places(self, by):
        base = 4 * ((self.z + by) % self.depth)
        return [base + 2 * (self.y ^ dy) + (self.x ^ dx) for dy in range(2) for dx in range(2)]


class Stages:
    def __init__(self, at):
        self.at = at
        self.arrived = [()] * 3
        self.now = []
        self.ready = self.next_ready = ()
        self.back = 2

    def advance(self):
        self.arrived.append(tuple(self.now))
        self.now, self.ready, self.next_ready = [], self.next_ready, ()

    def hold(self, array):
        return after(array, *self.arrived[-2])

    def finished(self, *arrays):
        self.next_ready += arrays

    def send(self, array, pairs, *earlier):
        got = lax.ppermute(after(array, *self.arrived[-self.back], *self.ready, *earlier), "ctx", pairs)
        self.now.append(got)
        return got

    def swap_x(self, array, *earlier):
        return self.send(array, self.at.pairs_x, *earlier)

    def swap_y(self, array, *earlier):
        return self.send(array, self.at.pairs_y, *earlier)


def pick(bit, array, axis):
    halves = [lax.index_in_dim(array, k, axis, keepdims=False) for k in range(2)]
    return jnp.where(bit == 0, halves[0], halves[1])


def ordered(bit, mine, other):
    return jnp.stack([jnp.where(bit == 0, mine, other), jnp.where(bit == 0, other, mine)])


def reduce_filters(at, part, chan_count):
    taps = part.shape[1]
    part = part.reshape(at.depth, 2, 2, chan_count, taps)
    first = None
    for bit, pairs, axis in ((at.x, at.pairs_x, 2), (at.y, at.pairs_y, 1)):
        got = lax.ppermute(pick(1 - bit, part, axis).astype(BF16), "ctx", pairs)
        first = got if first is None else first
        part = pick(bit, part, axis) + got.astype(F32)
    at_z = lambda by: lax.dynamic_index_in_dim(part, (at.z + by) % at.depth, 0, keepdims=False)
    total = at_z(0)
    for by in range(1, at.depth):
        total = total + lax.ppermute(at_z(by), "ctx", at.pairs_z(by))
    return total, first


def on_device(out_grad, gate_values, kv_product, w_out, filters):
    at = Layout()
    stages = Stages(at)
    chan_count = filters.shape[2]
    taps = filters.shape[3]
    seq_len = out_grad.shape[1]
    rows, chan = w_out.shape
    half = chan // 2
    norm_scale = 1.0 / math.sqrt(at.count * seq_len)
    to_right = [(i, i + 1) for i in range(at.count - 1)]
    to_left = [(i + 1, i) for i in range(at.count - 1)]
    forward, backward = (jnp.asarray(m) for m in dft_matrices(taps))

    grad_full = lax.all_gather(out_grad, "fsdp", axis=0, tiled=True)

    near = sorted(range(at.depth), key=lambda d: min(d, at.depth - d))
    far = near[::-1]
    own, own_filters = w_out.T, filters.reshape(chan_count, taps)
    filters_x = lax.ppermute(own_filters, "ctx", at.pairs_x)
    pair = ordered(at.x, own_filters, filters_x)
    filters_y = lax.ppermute(pair, "ctx", at.pairs_y)
    plane = ordered(at.y, pair, filters_y)
    depth = at.depth
    shards = {0: own}
    ring = {0: plane}
    beside = {1, depth - 1} if depth > 2 else set()

    def step_z(held, by, *earlier):
        way = 1 if by <= depth // 2 else -1
        return lax.ppermute(after(held[(by - way) % depth], *earlier), "ctx", at.pairs_z(way))

    before = filters_y
    for by in near[1:]:
        shards[by] = before = step_z(shards, by, before)
    for way in near[1:]:
        ring[way] = step_z(ring, way, shards[near[min(1, depth - 1)] if way not in beside and depth > 2 else near[1]])
    ring = [ring[by] for by in range(depth - 1, 0, -1)]
    shards = [shards[by] for by in near]
    ring = jnp.stack((ring + [plane]) * 2)
    ring = lax.dynamic_slice_in_dim(ring, depth - 1 - at.z, depth, axis=0)
    all_filters = ring.reshape(chan, taps)
    prior = lax.ppermute(after(kv_product[:, seq_len - taps :], shards[1]), "ctx", to_right)

    from_x, from_y, diag_a, diag_b = {}, {}, {}, {}
    kept, carried, crossed, last_sent = {}, {}, [], []
    mixed = gated = products = w_grad = None

    def gather_first(k):
        both = (from_x[0], from_y[0]) if k == 1 else ()
        from_x[k] = stages.swap_x(shards[k], *both)
        from_y[k] = stages.swap_y(shards[k], *both)

    def gather_second(k):
        if near[k] in beside:
            pairs = at.pairs_z(1 if near[k] == 1 else -1)
            diag_a[k] = lax.ppermute(diag_a[0], "ctx", pairs)
            diag_b[k] = lax.ppermute(diag_b[0], "ctx", pairs)
            stages.finished(diag_a[k], diag_b[k])
        else:
            diag_a[k] = stages.swap_x(from_y[k][:half])
            diag_b[k] = stages.swap_y(from_x[k][half:])

    def mix():
        nonlocal mixed, gated
        mixed, gated = run_mix(all_filters, stages.hold(kv_product), prior, gate_values, forward, backward)
        stages.finished(mixed)

    def weight_part(k):
        place = jnp.stack(at.places(far[k])).astype(jnp.int32)
        added = crossed if far[k] == 0 else ()
        kept[k] = run_weight(place, grad_full, stages.hold(gated), rows, far[k] in beside, added)
        stages.finished(kept[k][0])

    def reduce_first(k):
        by = far[k]
        if by in beside:
            keep, send_x, send_y, send_z = kept[k]
            behind = (diag_a[depth - 1], diag_b[depth - 1]) if by == 1 else ()
            kept[k] = (keep, stages.swap_x(send_x, *behind), stages.swap_y(send_y, *behind))
            crossed.append(lax.ppermute(send_z, "ctx", at.pairs_z(1 if by == 1 else -1)))
        else:
            send_a, keep_a, send_b, keep_b = kept[k]
            kept[k] = (keep_a, stages.swap_x(send_a), keep_b, stages.swap_y(send_b))
            if by == 0:
                last_sent.extend((kept[k][1], kept[k][3]))

    def reduce_second(k):
        if far[k] in beside:
            return
        keep_a, got_a, keep_b, got_b = kept[k]
        next_a = (keep_a[1].astype(F32) + got_a[1].astype(F32)).astype(BF16)
        next_b = (keep_b[1].astype(F32) + got_b[1].astype(F32)).astype(BF16)
        kept[k] = (keep_a, got_a, stages.swap_y(next_a), keep_b, got_b, stages.swap_x(next_b))

    def reduce_third(k):
        nonlocal w_grad
        by = far[k]
        if by in beside:
            joint = sum(piece.astype(F32) for piece in kept.pop(k))
        else:
            keep_a, got_a, last_a, keep_b, got_b, last_b = kept.pop(k)
            sum_a = keep_a[0].astype(F32) + got_a[0].astype(F32) + last_a.astype(F32)
            sum_b = keep_b[0].astype(F32) + got_b[0].astype(F32) + last_b.astype(F32)
            joint = jnp.concatenate([sum_a, sum_b], axis=1)
        for piece in carried.pop(by, ()):
            joint = joint + piece.astype(F32)
        if by == 0:
            w_grad = joint * norm_scale
            return
        way = 1 if by <= depth // 2 else -1
        got = lax.ppermute(joint.astype(BF16), "ctx", at.pairs_z(way))
        carried.setdefault((by - way) % depth, []).append(got)
        if k < Z_PINNED:
            stages.finished(got)

    def product(part):
        nonlocal products
        diag = diag_a if 2 * part < PARTS else diag_b
        pieces = [p for k in range(depth) for p in (shards[k], from_x[k], from_y[k], diag[k])]
        places = jnp.stack([c for by in near for c in at.places(-by)]).astype(jnp.int32)
        products = run_product(
            part, places, grad_full, pieces, stages.hold(mixed), gate_values, kv_product, prior,
            all_filters, forward, backward, products or (),
        )
        stages.finished(products[3])

    late = depth - 4
    plan = {}

    def at_stage(stage, action, k):
        plan.setdefault(stage, []).append((action, k))

    at_stage(MIX_STAGE, lambda _: mix(), 0)
    for k in range(depth):
        more = max(0, k - 3)
        at_stage(WEIGHT_STAGE[min(k, 3)] + more + late, weight_part, k)
    for k in range(depth):
        at_stage(THIRD_STAGE[min(k, 3)] + max(0, k - 3) + late, reduce_third, k)
    for part in range(PARTS):
        at_stage(PRODUCT_STAGE[part] + 2 * late, lambda p: product(p), part)
    for k in range(depth):
        more = max(0, k - 3)
        at_stage(k, gather_first, k)
        at_stage(GATHER_SECOND[min(k, 3)] + more, gather_second, k)
    for k in range(depth):
        more = max(0, k - 3)
        at_stage(REDUCE_FIRST[min(k, 3)] + more + late, reduce_first, k)
        at_stage(REDUCE_SECOND[min(k, 3)] + more + late, reduce_second, k)
    for stage in range(max(plan) + 1):
        if stage >= CLOSE_STAGE + 2 * late:
            stages.back = 1
        for action, k in plan.get(stage, []):
            action(k)
        stages.advance()

    gate_grad, kv_grad, last, head, filt_part = products
    filter_grad, crossed_x = reduce_filters(at, after(filt_part, *last_sent), chan_count)
    filter_grad = filter_grad * norm_scale
    tail = lax.ppermute(head, "ctx", to_left)
    kv_grad = lax.dynamic_update_slice(
        kv_grad, (last + tail.astype(F32)).astype(BF16), (0, seq_len - taps)
    )
    return (gate_grad, kv_grad, filter_grad.reshape(filters.shape), w_grad)


def solution(mesh):
    in_specs = (
        P("fsdp", "ctx"),
        P("fsdp", "ctx"),
        P("fsdp", "ctx"),
        P("ctx", "fsdp"),
        P("fsdp", "ctx", None, None),
    )
    out_specs = (P("fsdp", "ctx"), P("fsdp", "ctx"), P("fsdp", "ctx", None, None), P("ctx", "fsdp"))
    return jax.shard_map(
        on_device, mesh=mesh, in_specs=in_specs, out_specs=out_specs, check_vma=False
    )
```
